512 devices in a mesh: herd: 128 (over y, z, core), snp: 4 (over x).
Axes of the slice: x: 4, y: 4, z: 16, core: 2. Of those that a mesh axis runs over, the one named last changes fastest.
Arguments:
- sol_u: float32 [16, 524288], P('snp', 'herd'), may hold values from -6 to 6
- res_u: float32 [16, 524288], P('snp', 'herd'), may hold values from -50 to 50
- dir_u: float32 [16, 524288], P('snp', 'herd'), may hold values from -50 to 50
- rec_weight: float32 [16, 524288], P('snp', 'herd'), may hold values from 0.1 to 2
- inv_diag_u: float32 [16, 524288], P('snp', 'herd'), may hold values from 0.15 to 0.5
- sol_a: float32 [16, 4, 10240], P(None, 'snp', 'herd'), may hold values from -6 to 6
- res_a: float32 [16, 4, 10240], P(None, 'snp', 'herd'), may hold values from -50 to 50
- dir_a: float32 [16, 4, 10240], P(None, 'snp', 'herd'), may hold values from -50 to 50
- inv_diag_a: float32 [16, 4, 10240], P(None, 'snp', 'herd'), may hold values from 0.3 to 1
- genotypes: bfloat16 [4096, 40960], P('herd', 'snp'), may hold values from 0 to 2, as said below
- allele_freq: float32 [40960], P('snp'), may hold values from 0.05 to 0.5
- geno_weight: float32 [16], P('snp'), may hold values from 0.5 to 2
- snp_ridge: float32 [16], replicated, may hold values from 0.5 to 2
- genetic_inv: float32 [16, 16], P('snp'), may hold values from -0.1 to 2, as said below
- sire: int32 [524288], P('herd'), may hold values from -1 to 524287, as said below
- dam: int32 [524288], P('herd'), may hold values from -1 to 524286, as said below
Outputs:
- next_sol_u: float32 [16, 524288], P('snp', 'herd')
- next_res_u: float32 [16, 524288], P('snp', 'herd')
- next_dir_u: float32 [16, 524288], P('snp', 'herd')
- next_sol_a: float32 [16, 4, 10240], P(None, 'snp', 'herd')
- next_res_a: float32 [16, 4, 10240], P(None, 'snp', 'herd')
- next_dir_a: float32 [16, 4, 10240], P(None, 'snp', 'herd')
The draws below stay inside these ranges and needn't reach their ends.
Inputs may be any that keep to these rules, and one draw needn't show every extreme that they name: A sire is -1 or an animal of another herd group (herd group of animal i: i // 4096); the sires of one herd group's animals lie in at most 2 distinct parent blocks (animals 128 b to 128 b + 127 within one group) of any one other group, and some group has exactly 2 such blocks taken by every other group. A dam is -1 or an earlier animal of the same herd group. `genotypes`: every entry is 0, 1 or 2. `genetic_inv`: symmetric positive definite.
All inputs are finite; a program needn't handle non-finite values.
Results may differ from the reference program's by a relative error of at most 0.0003.
Values sent between devices are 32-bit elements; how exact they have to be, the bound alone decides.
No kernel may reach another device: no remote copies, remote signals or barrier semaphores. Data moves between devices by JAX's collectives and lax.ppermute only.
A program may use at most 128 MiB of HBM per device.

```python
import math
import jax
import jax.numpy as jnp
from jax import lax

TRAITS = 16
SNP_DEV = 10240
SLOTS = 2
ANI_DEV = 4096
GEN_DEV = 32
ANIMALS = 524288
GENOTYPED = 4096
SNP_BLOCKS = 4
SNPS = 40960
N_HERD = 128


def scale_grid(key, columns, rise):
    key_row, key_col = jax.random.split(key)
    spread = jnp.log(10.0 / rise)
    row_steps = jnp.arange(TRAITS, dtype=jnp.float32) / (TRAITS - 1)
    col_steps = jnp.arange(columns, dtype=jnp.float32) / (columns - 1)
    row_scale = rise ** row_steps * jnp.exp(jax.random.uniform(key_row, (TRAITS,), jnp.float32, 0.0, 1.0) * spread)
    col_scale = rise ** col_steps * jnp.exp(jax.random.uniform(key_col, (columns,), jnp.float32, 0.0, 1.0) * spread)
    return row_scale[:, None] * col_scale[None, :]


def draw_res_u(key, part):
    key = jax.random.fold_in(key, 11)
    key_base, key_scale = jax.random.split(key)
    base = jnp.clip(jax.random.normal(key_base, (TRAITS, ANIMALS), jnp.float32), -5.0, 5.0)
    grid = scale_grid(key_scale, ANIMALS, 3.0)
    return 0.1 * base * grid


def draw_dir_u(key, part):
    key = jax.random.fold_in(key, 23)
    key_base, key_scale = jax.random.split(key)
    base = jnp.clip(jax.random.normal(key_base, (TRAITS, ANIMALS), jnp.float32), -5.0, 5.0)
    grid = scale_grid(key_scale, ANIMALS, 3.0)
    return 0.1 * base * grid


def draw_res_a(key, part):
    key = jax.random.fold_in(key, 31)
    key_base, key_scale = jax.random.split(key)
    columns = SNP_BLOCKS * SNP_DEV
    base = jnp.clip(jax.random.normal(key_base, (TRAITS, columns), jnp.float32), -5.0, 5.0)
    grid = scale_grid(key_scale, columns, 3.0)
    return (0.1 * base * grid).reshape(TRAITS, SNP_BLOCKS, SNP_DEV)


def draw_dir_a(key, part):
    key = jax.random.fold_in(key, 37)
    key_base, key_scale = jax.random.split(key)
    columns = SNP_BLOCKS * SNP_DEV
    base = jnp.clip(jax.random.normal(key_base, (TRAITS, columns), jnp.float32), -5.0, 5.0)
    grid = scale_grid(key_scale, columns, 3.0)
    return (0.1 * base * grid).reshape(TRAITS, SNP_BLOCKS, SNP_DEV)


def draw_genetic_inv(key, part):
    key = jax.random.fold_in(key, 41)
    key_off, key_diag = jax.random.split(key)
    raw_values = jax.random.uniform(key_off, (TRAITS, TRAITS), jnp.float32, -0.1, 0.1)
    upper = jnp.triu(raw_values, 1)
    diagonal = jax.random.uniform(key_diag, (TRAITS,), jnp.float32, 1.6, 2.0)
    return upper + upper.T + jnp.diag(diagonal)


def draw_genotypes(key, part):
    key = jax.random.fold_in(key, 53)
    codes = jax.random.randint(key, (GENOTYPED, SNPS), 0, 3)
    return codes.astype(jnp.bfloat16)


def draw_sire(key, part):
    key = jax.random.fold_in(key, 67)
    keys = jax.random.split(key, 7)
    herd_count = N_HERD
    block_count = ANI_DEV // 128
    total_slots = herd_count * SLOTS
    herd_ids = jnp.arange(herd_count)
    counts = jax.random.randint(keys[0], (herd_count, herd_count), 0, SLOTS + 1)
    busiest = jax.random.randint(keys[1], (), 0, herd_count)
    counts = jnp.where(herd_ids[None, :] == busiest, SLOTS, counts)
    counts = counts.at[0, herd_count - 1].max(1)
    counts = jnp.where(herd_ids[:, None] == herd_ids[None, :], 0, counts)
    first = jax.random.randint(keys[2], (herd_count, herd_count), 0, block_count)
    first = first.at[0, herd_count - 1].set(block_count - 1)
    spacing = 1 + jax.random.randint(keys[3], (herd_count, herd_count, 1), 0, block_count // SLOTS)
    chosen = (first[:, :, None] + jnp.arange(SLOTS)[None, None, :] * spacing) % block_count
    animal = jnp.arange(ANI_DEV)[None, :]
    shift_slot = jax.random.randint(keys[4], (herd_count, 1), 0, total_slots)
    picked = jax.random.randint(keys[5], (herd_count, ANI_DEV), 0, total_slots)
    slot_id = jnp.where(animal < total_slots, (animal + shift_slot) % total_slots, picked)
    owner_herd = slot_id // SLOTS
    which_slot = slot_id % SLOTS
    requester = herd_ids[:, None]
    live_slot = which_slot < counts[requester, owner_herd]
    block_index = chosen[requester, owner_herd, which_slot]
    offset = jax.random.randint(keys[6], (herd_count, ANI_DEV), 0, 128)
    forced = (requester == 0) & (animal < total_slots) & (slot_id == (herd_count - 1) * SLOTS)
    offset = jnp.where(forced, 127, offset)
    sire = jnp.where(live_slot, owner_herd * ANI_DEV + block_index * 128 + offset, -1)
    return sire.reshape(ANIMALS).astype(jnp.int32)


def draw_dam(key, part):
    key = jax.random.fold_in(key, 79)
    key_gap, key_known = jax.random.split(key)
    animal = jnp.arange(ANI_DEV)[None, :]
    last_one = animal == ANI_DEV - 1
    gap_size = jax.random.randint(key_gap, (N_HERD, ANI_DEV), 1, 33)
    gap_size = jnp.where(last_one, 1, gap_size)
    known = (jax.random.randint(key_known, (N_HERD, ANI_DEV), 0, 5) > 0) | last_one
    local_dam = animal - gap_size
    group_start = jnp.arange(N_HERD)[:, None] * ANI_DEV
    dam = jnp.where(known & (local_dam >= 0), group_start + local_dam, -1)
    return dam.reshape(ANIMALS).astype(jnp.int32)


def shard_levels(own_key, shape, cuts, smallest, top_value):
    loudness, own = 1.0, jax.random.fold_in(own_key, 6)
    for axis_at, shards_of in cuts:
        heights = jnp.exp(jax.random.uniform(jax.random.fold_in(own, axis_at), (shards_of,), jnp.float32, smallest / len(cuts), top_value / len(cuts)))
        loudness = loudness * jnp.repeat(heights, shape[axis_at] // shards_of).reshape([-1 if axis == axis_at else 1 for axis in range(len(shape))])
    return loudness


def gaussian(own_key, dims, width, limit, shards=(), kind=jnp.bfloat16):
    loudness = shard_levels(own_key, dims, shards, -0.22, 0.18) if shards else 1.0
    values = jax.random.normal(own_key, dims, jnp.float32) * width * loudness
    return jnp.minimum(jnp.maximum(values, -limit), limit).astype(kind)


def setup_inputs(seed: int = 0) -> dict:
    key_of = jax.random.split(jax.random.key(seed), 17)
    return {
        "sol_u": gaussian(key_of[0], (TRAITS, ANIMALS), 1.0, 6.0, ((0, 4), (1, 128)), jnp.float32),
        "res_u": draw_res_u(jax.random.fold_in(key_of[16], 71), 0),
        "dir_u": draw_dir_u(jax.random.fold_in(key_of[16], 71), 0),
        "rec_weight": jnp.clip(jnp.exp(math.log(2.0) - 2.9957323 * jax.random.uniform(key_of[3], (TRAITS, ANIMALS), jnp.float32) ** shard_levels(key_of[3], (TRAITS, ANIMALS), ((0, 4), (1, 128)), -0.2, 0.2)), 0.1, 2.0),
        "inv_diag_u": jnp.clip(jnp.exp(math.log(0.5) - 1.2039728 * jax.random.uniform(key_of[4], (TRAITS, ANIMALS), jnp.float32) ** shard_levels(key_of[4], (TRAITS, ANIMALS), ((0, 4), (1, 128)), -0.2, 0.2)), 0.15, 0.5),
        "sol_a": gaussian(key_of[5], (TRAITS, SNP_BLOCKS, SNP_DEV), 1.0, 6.0, ((1, 4), (2, 128)), jnp.float32),
        "res_a": draw_res_a(jax.random.fold_in(key_of[16], 71), 0),
        "dir_a": draw_dir_a(jax.random.fold_in(key_of[16], 71), 0),
        "inv_diag_a": jnp.clip(jnp.exp(math.log(1.0) - 1.2039728 * jax.random.uniform(key_of[8], (TRAITS, SNP_BLOCKS, SNP_DEV), jnp.float32) ** shard_levels(key_of[8], (TRAITS, SNP_BLOCKS, SNP_DEV), ((1, 4), (2, 128)), -0.2, 0.2)), 0.3, 1.0),
        "genotypes": draw_genotypes(jax.random.fold_in(key_of[16], 71), 0),
        "allele_freq": jnp.clip(0.05 + 0.45 * jax.random.uniform(key_of[10], (SNPS,), jnp.float32) ** shard_levels(key_of[10], (SNPS,), ((0, 4),), -0.2, 0.2), 0.05, 0.5),
        "geno_weight": jnp.clip(jnp.exp(math.log(2.0) - 1.3862944 * jax.random.uniform(key_of[11], (TRAITS,), jnp.float32) ** shard_levels(key_of[11], (TRAITS,), ((0, 4),), -0.2, 0.2)), 0.5, 2.0),
        "snp_ridge": jnp.clip(jnp.exp(jax.random.uniform(key_of[12], (TRAITS,), jnp.float32, math.log(0.5), math.log(2.0))), 0.5, 2.0),
        "genetic_inv": draw_genetic_inv(jax.random.fold_in(key_of[16], 71), 0),
        "sire": draw_sire(jax.random.fold_in(key_of[16], 71), 0),
        "dam": draw_dam(jax.random.fold_in(key_of[16], 71), 0),
    }


def pedigree(field, sire, dam):
    animals = field.shape[1]
    has_sire = sire >= 0
    has_dam = dam >= 0
    sire_known = has_sire.astype(field.dtype)
    dam_known = has_dam.astype(field.dtype)
    sire_source = jnp.where(has_sire, sire, 0).astype(jnp.int32)
    dam_source = jnp.where(has_dam, dam, 0).astype(jnp.int32)
    weight = 4.0 / (4.0 - sire_known - dam_known)
    scaled = weight * (field - 0.5 * sire_known * field[:, sire_source] - 0.5 * dam_known * field[:, dam_source])
    sire_target = jnp.where(has_sire, sire, animals).astype(jnp.int32)
    dam_target = jnp.where(has_dam, dam, animals).astype(jnp.int32)
    extra = jnp.zeros((field.shape[0], animals + 1), field.dtype)
    extra = extra.at[:, dam_target].add(-0.5 * dam_known * scaled)
    extra = extra.at[:, sire_target].add(-0.5 * sire_known * scaled)
    return scaled + extra[:, :animals]

def reference(sol_u, res_u, dir_u, rec_weight, inv_diag_u, sol_a, res_a, dir_a, inv_diag_a, genotypes, allele_freq, geno_weight, snp_ridge, genetic_inv, sire, dam):
    geno_scale = 2.0 / math.sqrt(SNPS)
    flat_dir = dir_a.reshape(TRAITS, SNPS)
    blocks = genotypes.reshape(N_HERD, GEN_DEV, SNPS)
    pu_gen = dir_u.reshape(TRAITS, N_HERD, ANI_DEV)[:, :, :GEN_DEV].transpose(1, 0, 2)

    def block_step(running, block_item):
        block_rows, dir_rows = block_item
        centered = (block_rows.astype(jnp.float32) - 2.0 * allele_freq) * geno_scale
        predicted = lax.dot_general(flat_dir, centered, (((1,), (1,)), ((), ())), precision=lax.Precision.HIGHEST)
        geno_resid = geno_weight[:, None] * (dir_rows - predicted)
        running = running + jnp.dot(geno_resid, centered, precision=lax.Precision.HIGHEST)
        return (running, geno_resid)
    snp_back, resid_blocks = lax.scan(block_step, jnp.zeros((TRAITS, SNPS), jnp.float32), (blocks, pu_gen))
    image_a = snp_ridge[:, None, None] * dir_a - snp_back.reshape(TRAITS, SNP_BLOCKS, SNP_DEV)
    pedigree_term = pedigree(dir_u, sire, dam)
    image_u = rec_weight * dir_u + jnp.dot(genetic_inv, pedigree_term, precision=lax.Precision.HIGHEST)
    image_grid = image_u.reshape(TRAITS, N_HERD, ANI_DEV)
    image_grid = image_grid.at[:, :, :GEN_DEV].add(resid_blocks.transpose(1, 0, 2))
    image_u = image_grid.reshape(TRAITS, ANIMALS)
    norm_now = jnp.sum(inv_diag_u * res_u * res_u) + jnp.sum(inv_diag_a * res_a * res_a)
    curvature = jnp.sum(dir_u * image_u) + jnp.sum(dir_a * image_a)
    step_size = norm_now / curvature
    next_sol_u = sol_u + step_size * dir_u
    next_sol_a = sol_a + step_size * dir_a
    next_res_u = res_u - step_size * image_u
    next_res_a = res_a - step_size * image_a
    norm_next = jnp.sum(inv_diag_u * next_res_u * next_res_u) + jnp.sum(inv_diag_a * next_res_a * next_res_a)
    step_ratio = norm_next / norm_now
    next_dir_u = inv_diag_u * next_res_u + step_ratio * dir_u
    next_dir_a = inv_diag_a * next_res_a + step_ratio * dir_a
    return (next_sol_u, next_res_u, next_dir_u, next_sol_a, next_res_a, next_dir_a)
```

```python
import functools
import math

import jax
import jax.numpy as jnp
from jax import lax
from jax.experimental import pallas as pl
from jax.experimental.pallas import tpu as pltpu
from jax.sharding import Mesh, PartitionSpec as P

SLOTS = 2
CAP = 64
CHUNK = 512
HERD = ("y", "z", "c")
F32 = jnp.float32
BF16 = jnp.bfloat16
NT = (((1,), (1,)), ((), ()))
TN = (((0,), (0,)), ((), ()))
NN = (((1,), (0,)), ((), ()))


def call(kernel, out, scratch=(), specs=None, flops=10**8, **kw):
    return pl.pallas_call(
        kernel,
        out_shape=out,
        scratch_shapes=list(scratch),
        compiler_params=pltpu.CompilerParams(vmem_limit_bytes=40 * 2**20),
        **kw,
    )


def dot(a, b, dims=NN):
    return lax.dot_general(a, b, dims, preferred_element_type=F32)


def parts(x, n=2):
    out = []
    for _ in range(n):
        p = x.astype(BF16).astype(F32)
        out.append(p)
        x = x - p
    return out


def rows_at(n, cols):
    return lax.broadcasted_iota(jnp.int32, (n, cols), 0)


def weights(sire, dam):
    known = (sire >= 0).astype(jnp.int32) + (dam >= 0).astype(jnp.int32)
    return jnp.where(known == 2, 2.0, jnp.where(known == 1, 4.0 / 3.0, 1.0)).astype(F32)


def dam_place(dam, animals):
    local = dam & (animals - 1)
    block = jnp.where(dam >= 0, local >> 7, -1)
    return block, local & 127


def lists_kernel(dir_ref, g_ref, sire_ref, dam_ref, pay_ref, c_ref, tab_ref, rank_ref, v_ref, acc_ref):
    traits, animals = v_ref.shape
    herd = pay_ref.shape[0]
    blocks = animals // 128
    n = CHUNK
    v_ref[...] = lax.dot_general(
        g_ref[...], dir_ref[...], NN, precision=lax.Precision.HIGHEST, preferred_element_type=F32
    )
    for t in range(traits):
        for b in range(blocks):
            tab_ref[t * blocks + b : t * blocks + b + 1, :] = v_ref[t : t + 1, b * 128 : (b + 1) * 128]
    table = jnp.concatenate([p.astype(BF16) for p in parts(tab_ref[...])], axis=0)
    half = traits * blocks
    before = (rows_at(n, n) < lax.broadcasted_iota(jnp.int32, (n, n), 1)).astype(F32).astype(BF16)
    acc_ref[...] = jnp.zeros(acc_ref.shape, F32)

    def step(k, carry):
        at = pl.ds(pl.multiple_of(k * n, n), n)
        sire = sire_ref[:, at]
        dam = dam_ref[:, at]
        weight = weights(sire, dam)
        block, offset = dam_place(dam, animals)
        hit = (rows_at(128, n) == offset).astype(F32).astype(BF16)
        found = dot(table, hit)
        found = found[:half] + found[half:]
        in_block = rows_at(blocks, n) == block
        own = v_ref[:, at]
        terms = []
        for t in range(traits):
            dam_value = jnp.sum(
                jnp.where(in_block, found[t * blocks : (t + 1) * blocks], 0.0), axis=0, keepdims=True
            )
            terms.append(weight * (own[t : t + 1] - 0.5 * dam_value))
            c_ref[t : t + 1, at] = terms[t]
        owner = sire >> (animals.bit_length() - 1)
        is_owner = rows_at(herd, n) == owner
        owners = is_owner.astype(F32).astype(BF16)
        earlier = dot(owners, before) + carry
        rank = jnp.sum(jnp.where(is_owner, earlier, 0.0), axis=0, keepdims=True).astype(jnp.int32)
        rank = jnp.where(sire >= 0, rank, -1)
        rank_ref[:, at] = rank
        in_slot = rows_at(CAP, n) == rank
        local = (sire & (animals - 1)) + 1
        high = [(local & ~63).astype(F32), weight * 1.5]
        low = [(local & 63).astype(F32), jnp.zeros((1, n), F32)]
        for value in terms:
            hi, lo = parts(value)
            high.append(hi)
            low.append(lo)
        fields = jnp.concatenate(
            [jnp.where(in_slot, f, 0.0).astype(BF16) for f in high + low], axis=0
        )
        acc_ref[...] += dot(owners, fields, NT)
        return carry + jnp.sum(jnp.where(is_owner, 1.0, 0.0), axis=1, keepdims=True)

    count = lax.fori_loop(0, animals // n, step, jnp.zeros((herd, 1), F32))
    width = pay_ref.shape[1]
    overflow = jnp.where(jnp.max(count, axis=0, keepdims=True) > CAP + 0.5, 16.0, 0.0)
    lane = lax.broadcasted_iota(jnp.int32, (herd, width), 1)
    flag = jnp.where((lane >= CAP) & (lane < 2 * CAP), overflow, 0.0)
    pay_ref[...] = acc_ref[:, :width] + acc_ref[:, width:] + flag


def owner_kernel(got_ref, tab_ref, out_ref, inc_ref, over_ref, turned_ref, vals_ref, acc_ref):
    herd = got_ref.shape[0]
    half = tab_ref.shape[0]
    blocks = 32
    traits = half // blocks
    for j in range(got_ref.shape[1] // 128):
        turned_ref[j * 128 : (j + 1) * 128, :] = got_ref[:, j * 128 : (j + 1) * 128].T
    weight_rows = turned_ref[CAP : 2 * CAP, :]
    over_ref[...] = jnp.broadcast_to(jnp.max(weight_rows, keepdims=True), over_ref.shape)
    table = jnp.concatenate([p.astype(BF16) for p in parts(tab_ref[...])], axis=0)
    acc_ref[...] = jnp.zeros(acc_ref.shape, F32)
    group = 8
    n = group * herd

    def flat(first):
        tile = turned_ref[pl.ds(first, group), :]
        return jnp.concatenate([tile[j : j + 1] for j in range(group)], axis=1)

    def step(k, _):
        r = pl.multiple_of(k * group, group)
        place = flat(r).astype(jnp.int32) - 1
        block = place >> 7
        hit = (rows_at(128, n) == (place & 127)).astype(F32).astype(BF16)
        in_block = rows_at(blocks, n) == block
        found = dot(table, hit)
        found = found[:half] + found[half:]
        high, low = [], []
        for t in range(traits):
            value = jnp.sum(
                jnp.where(in_block, found[t * blocks : (t + 1) * blocks], 0.0), axis=0, keepdims=True
            )
            vals_ref[pl.ds(t * CAP + r, group), :] = jnp.concatenate(
                [value[:, j * herd : (j + 1) * herd] for j in range(group)], axis=0
            )
            hi, lo = parts(flat(2 * CAP + t * CAP + r))
            high.append(hi)
            low.append(lo)
        weight = flat(CAP + r)
        weight = jnp.where(weight >= 8.0, weight - 16.0, weight)
        fields = jnp.concatenate(
            [jnp.where(in_block, f, 0.0).astype(BF16) for f in high + low + [weight]], axis=0
        )
        acc_ref[...] += dot(fields, hit, NT)
        return 0

    lax.fori_loop(0, CAP // group, step, 0)
    out_ref[...] = vals_ref[...].T
    weight_sum = acc_ref[2 * half :, :] * (0.25 / 1.5)
    for t in range(traits):
        at = slice(t * blocks, (t + 1) * blocks)
        sums = acc_ref[at, :] + acc_ref[half + t * blocks : half + (t + 1) * blocks, :]
        inc_ref[at, :] = weight_sum * tab_ref[at, :] - 0.5 * sums


def image_kernel(
    got_ref, c_ref, rank_ref, sire_ref, dam_ref, inc_ref, resid_ref,
    dir_ref, rec_ref, res_ref, inv_ref,
    back_ref, ridge_ref, dir_a_ref, res_a_ref, inv_a_ref,
    image_ref, image_a_ref, sums_ref, acc_ref, tab_ref,
):
    traits, animals = c_ref.shape
    herd = got_ref.shape[0]
    blocks = animals // 128
    n = CHUNK
    half = traits * blocks
    table = jnp.concatenate([p.astype(BF16) for p in parts(got_ref[...])], axis=1)
    wide = traits * CAP
    acc_ref[...] = jnp.zeros(acc_ref.shape, F32)

    def step(k, _):
        at = pl.ds(pl.multiple_of(k * n, n), n)
        sire = sire_ref[:, at]
        dam = dam_ref[:, at]
        weight = weights(sire, dam)
        owner = sire >> (animals.bit_length() - 1)
        owners = (rows_at(herd, n) == owner).astype(F32).astype(BF16)
        found = dot(table, owners, TN)
        found = found[:wide] + found[wide:]
        in_slot = rows_at(CAP, n) == rank_ref[:, at]
        block, offset = dam_place(dam, animals)
        in_block = rows_at(blocks, n) == block
        hit = (rows_at(128, n) == offset).astype(F32).astype(BF16)
        high, low = [], []
        for t in range(traits):
            sire_value = jnp.sum(
                jnp.where(in_slot, found[t * CAP : (t + 1) * CAP], 0.0), axis=0, keepdims=True
            )
            scaled = c_ref[t : t + 1, at] - 0.5 * weight * sire_value
            image_ref[t : t + 1, at] = scaled
            hi, lo = parts(scaled)
            high.append(hi)
            low.append(lo)
        fields = jnp.concatenate(
            [jnp.where(in_block, f, 0.0).astype(BF16) for f in high + low], axis=0
        )
        acc_ref[...] += dot(fields, hit, NT)
        return 0

    lax.fori_loop(0, animals // n, step, 0)
    tab_ref[...] = inc_ref[...] - 0.5 * (acc_ref[:half, :] + acc_ref[half:, :])
    for b in range(blocks):
        for t in range(traits):
            at = (slice(t, t + 1), slice(b * 128, (b + 1) * 128))
            image_ref[at] = image_ref[at] + tab_ref[t * blocks + b : t * blocks + b + 1, :]
    image_ref[:, :128] = image_ref[:, :128] + resid_ref[...]
    direction = dir_ref[...]
    image = image_ref[...] + rec_ref[...] * direction
    image_ref[...] = image
    res = res_ref[...]
    inv = inv_ref[...]
    columns = dir_a_ref.shape[1]
    back = jnp.sum(back_ref[...], axis=0)[:, :columns]
    dir_a = dir_a_ref[...]
    image_a = ridge_ref[...] * dir_a - back
    image_a_ref[...] = image_a
    res_a = res_a_ref[...]
    inv_a = inv_a_ref[...]
    weighted, weighted_a = inv * res, inv_a * res_a
    lane = lax.broadcasted_iota(jnp.int32, (1, 128), 1)
    pairs = (
        (weighted * res, weighted_a * res_a),
        (direction * image, dir_a * image_a),
        (weighted * image, weighted_a * image_a),
        (inv * image * image, inv_a * image_a * image_a),
    )
    total = jnp.zeros((1, 128), F32)
    for j, (one, two) in enumerate(pairs):
        value = jnp.sum(one, keepdims=True) + jnp.sum(two, keepdims=True)
        total = jnp.where(lane == j, value, total)
    sums_ref[...] = total


def join_kernel(in_ref, out_ref, *, columns):
    cores, zs, traits, _ = in_ref.shape
    lane = lax.broadcasted_iota(jnp.int32, (traits, 128), 1)
    for k in range(out_ref.shape[1] // 128):
        tile = jnp.zeros((traits, 128), F32)
        for p in range(cores * zs):
            off = p * columns - k * 128
            if off <= -columns or off >= 128:
                continue
            piece = in_ref[p % cores, p // cores]
            if off % 128:
                piece = pltpu.roll(piece, off % 128, 1)
            tile = jnp.where((lane >= off) & (lane < off + columns), piece, tile)
        out_ref[:, k * 128 : (k + 1) * 128] = tile


def part_kernel(in_ref, out_ref, *, columns):
    cores, zs, traits, _ = out_ref.shape
    total = in_ref[0]
    for y in range(1, in_ref.shape[0]):
        total = total + in_ref[y]
    lane = lax.broadcasted_iota(jnp.int32, (traits, 128), 1)
    for p in range(cores * zs):
        first = p * columns
        k, off = first // 128, first % 128
        piece = total[:, k * 128 : (k + 1) * 128]
        if off:
            piece = pltpu.roll(piece, 128 - off, 1)
        if off + columns > 128:
            nxt = pltpu.roll(total[:, (k + 1) * 128 : (k + 2) * 128], 128 - off, 1)
            piece = jnp.where(lane < 128 - off, piece, nxt)
        out_ref[p % cores, p // cores] = jnp.where(lane < columns, piece, 0.0)


def predict_kernel(dir_ref, geno_ref, freq_ref, gw_ref, out_ref, *, scale):
    ys, traits, width = dir_ref.shape
    genotyped = geno_ref.shape[0]
    total = jnp.zeros((3 * traits, genotyped), F32)
    bias = jnp.zeros((traits, 1), F32)
    for y in range(ys):
        at = slice(y * width, (y + 1) * width)
        values = dir_ref[y]
        stack = jnp.concatenate([p.astype(BF16) for p in parts(values, 3)], axis=0)
        total = total + dot(stack, geno_ref[:, at], NT)
        bias = bias + jnp.sum(values * (2.0 * freq_ref[:, at]), axis=1, keepdims=True)
    rows = total[:traits] + total[traits : 2 * traits] + total[2 * traits :]
    out_ref[...] = jnp.zeros(out_ref.shape, F32)
    out_ref[:, :genotyped] = (rows - bias) * scale
    out_ref[:, genotyped : genotyped + 1] = gw_ref[...]


def back_kernel(pred_ref, dir_ref, geno_ref, freq_ref, out_ref, resid_ref, *, scale):
    ys, traits, width = out_ref.shape
    genotyped = geno_ref.shape[0]
    total = pred_ref[0]
    for x in range(1, pred_ref.shape[0]):
        total = total + pred_ref[x]
    lane = lax.broadcasted_iota(jnp.int32, (traits, 128), 1)
    weight = jnp.sum(jnp.where(lane == genotyped, total, 0.0), axis=1, keepdims=True)
    resid = jnp.where(lane < genotyped, weight * (dir_ref[...] - total), 0.0)
    resid_ref[...] = resid
    stack = jnp.concatenate([p.astype(BF16) for p in parts(resid, 3)], axis=0)[:, :genotyped]
    summed = jnp.sum(resid, axis=1, keepdims=True)
    for y in range(ys):
        at = slice(y * width, (y + 1) * width)
        found = dot(stack, geno_ref[:, at])
        found = found[:traits] + found[traits : 2 * traits] + found[2 * traits :]
        out_ref[y] = (found - summed * (2.0 * freq_ref[:, at])) * scale


def update_kernel(
    sums_ref, sol_ref, res_ref, dir_ref, inv_ref, image_ref,
    sol_a_ref, res_a_ref, dir_a_ref, inv_a_ref, image_a_ref,
    nsol_ref, nres_ref, ndir_ref, nsol_a_ref, nres_a_ref, ndir_a_ref,
):
    total = jnp.sum(sums_ref[...], axis=0)
    norm, curve, cross, square = (total[:, j : j + 1] for j in range(4))
    size = norm / curve
    following = norm - 2.0 * size * cross + size * size * square
    ratio = following / norm
    for sol, res, dire, inv, image, nsol, nres, ndir in (
        (sol_ref, res_ref, dir_ref, inv_ref, image_ref, nsol_ref, nres_ref, ndir_ref),
        (sol_a_ref, res_a_ref, dir_a_ref, inv_a_ref, image_a_ref, nsol_a_ref, nres_a_ref, ndir_a_ref),
    ):
        d = dire[...]
        nsol[...] = sol[...] + size * d
        left = res[...] - size * image[...]
        nres[...] = left
        ndir[...] = inv[...] * left + ratio * d


def pedigree_by_blocks(field, sire, dam, herd_count, herd_index):
    traits_here, animals = field.shape
    block_count = animals // 128
    span = SLOTS * 128
    has_sire = sire >= 0
    has_dam = dam >= 0
    sire_known = has_sire.astype(F32)
    dam_known = has_dam.astype(F32)
    owner_herd = jnp.where(has_sire, sire // animals, 0)
    block_index = jnp.where(has_sire, sire % animals // 128, 0)
    offset = jnp.where(has_sire, sire % 128, 0)
    flat_block = jnp.where(
        has_sire, owner_herd * block_count + block_index, herd_count * block_count
    )
    present = jnp.zeros((herd_count * block_count + 1,), jnp.int32).at[flat_block].max(1)
    present = present[:-1].reshape(herd_count, block_count)
    slot_order = jnp.cumsum(present, axis=1) - 1
    slot_range = jnp.arange(SLOTS, dtype=jnp.int32)
    slot_match = (present[:, :, None] == 1) & (slot_order[:, :, None] == slot_range[None, None, :])
    block_ids = jnp.arange(block_count, dtype=jnp.int32)[None, :, None] + 1
    wanted = jnp.sum(jnp.where(slot_match, block_ids, 0), axis=1) - 1
    requests = lax.all_to_all(wanted, HERD, split_axis=0, concat_axis=0, tiled=True)
    live_slot = requests >= 0
    field_tiles = field.reshape(traits_here, block_count, 128)
    outgoing = field_tiles[:, jnp.where(live_slot, requests, 0), :]
    outgoing = jnp.where(live_slot[None, :, :, None], outgoing, 0.0).reshape(
        traits_here, herd_count, span
    )
    fetched = lax.all_to_all(outgoing, HERD, split_axis=1, concat_axis=1, tiled=True).reshape(
        traits_here, herd_count * span
    )
    slot_index = slot_order[owner_herd, block_index]
    buffer_place = owner_herd * span + slot_index * 128 + offset
    sire_values = fetched[:, jnp.where(has_sire, buffer_place, 0)]
    local_dam = jnp.where(has_dam, dam - herd_index * animals, 0)
    dam_values = field[:, local_dam]
    weight = 4.0 / (4.0 - sire_known - dam_known)
    scaled = weight * (field - 0.5 * sire_known * sire_values - 0.5 * dam_known * dam_values)
    dam_target = jnp.where(has_dam, local_dam, animals)
    dam_terms = (
        jnp.zeros((traits_here, animals + 1), F32).at[:, dam_target].add(-0.5 * dam_known * scaled)
    )
    result = scaled + dam_terms[:, :animals]
    sire_target = jnp.where(has_sire, buffer_place, herd_count * span)
    outbound = (
        jnp.zeros((traits_here, herd_count * span + 1), F32)
        .at[:, sire_target]
        .add(-0.5 * sire_known * scaled)
    )
    outbound = outbound[:, :-1].reshape(traits_here, herd_count, span)
    returned = lax.all_to_all(outbound, HERD, split_axis=1, concat_axis=1, tiled=True).reshape(
        traits_here, herd_count * SLOTS, 128
    )
    block_target = jnp.where(live_slot, requests, block_count).reshape(herd_count * SLOTS)
    incoming = (
        jnp.zeros((traits_here, block_count + 1, 128), F32).at[:, block_target, :].add(returned)
    )
    return result + incoming[:, :block_count, :].reshape(traits_here, animals)


def body(
    sol_u, res_u, dir_u, rec_weight, inv_diag_u, sol_a, res_a, dir_a, inv_diag_a,
    genotypes, allele_freq, geno_weight, snp_ridge, genetic_inv, sire, dam,
):
    ny, nz, nc, nx = (lax.axis_size(a) for a in ("y", "z", "c", "x"))
    herd = ny * nz * nc
    herd_index = lax.axis_index(HERD)
    x_index = lax.axis_index("x")
    traits_here, animals = dir_u.shape
    traits, _, columns = dir_a.shape
    genotyped, snps = genotypes.shape
    blocks = animals // 128
    scale = 2.0 / math.sqrt(snps * nx)
    width = snps // ny
    sds = lambda *shape: jax.ShapeDtypeStruct(shape, F32)
    d_a, r_a, s_a, i_a = (a[:, 0, :] for a in (dir_a, res_a, sol_a, inv_diag_a))
    freq = allele_freq[None, :]
    sire_row, dam_row = sire[None, :], dam[None, :]

    dir_all = lax.all_gather(dir_u, "x", axis=0, tiled=True)
    padded = jnp.pad(d_a, ((0, 0), (0, 128 - columns)))
    along_z = lax.all_to_all(
        jnp.broadcast_to(padded[None], (nz, traits, 128)), "z", 0, 0, tiled=True
    )
    both_cores = lax.all_gather(along_z, "c", axis=0)
    joined = call(functools.partial(join_kernel, columns=columns), sds(traits, width))(both_cores)
    dir_block = lax.all_gather(joined, "y", axis=0)

    lists, c_term, table, rank = call(
        lists_kernel,
        (
            sds(herd, (2 + traits_here) * CAP),
            sds(traits_here, animals),
            sds(traits_here * blocks, 128),
            jax.ShapeDtypeStruct((1, animals), jnp.int32),
        ),
        scratch=[
            pltpu.VMEM((traits_here, animals), F32),
            pltpu.VMEM((herd, 2 * (2 + traits_here) * CAP), F32),
        ],
    )(dir_all, genetic_inv, sire_row, dam_row)
    got_lists = lax.all_to_all(lists[:, None, :], HERD, 0, 0, tiled=True)[:, 0, :]

    weight_here = lax.dynamic_update_slice(
        jnp.zeros((traits, 1), F32), geno_weight[:, None], (x_index * traits_here, 0)
    )
    predicted = call(functools.partial(predict_kernel, scale=scale), sds(traits, 128))(
        dir_block, genotypes, freq, weight_here
    )
    all_predicted = lax.all_gather(predicted, "x", axis=0)
    back, resid = call(
        functools.partial(back_kernel, scale=scale), (sds(ny, traits, width), sds(traits, 128))
    )(all_predicted, dir_all[:, :128], genotypes, freq)
    back_y = lax.all_to_all(back, "y", 0, 0, tiled=True)

    values, incoming, over = call(
        owner_kernel,
        (sds(herd, traits_here * CAP), sds(traits_here * blocks, 128), sds(8, 128)),
        scratch=[
            pltpu.VMEM(((2 + traits_here) * CAP, herd), F32),
            pltpu.VMEM((traits_here * CAP, herd), F32),
            pltpu.VMEM((2 * traits_here * blocks + blocks, 128), F32),
        ],
    )(got_lists, table)
    got_values = lax.all_to_all(values[:, None, :], HERD, 0, 0, tiled=True)[:, 0, :]

    pieces = call(
        functools.partial(part_kernel, columns=columns), sds(nc, nz, traits, 128)
    )(back_y)
    back_c = jnp.sum(lax.all_to_all(pieces, "c", 0, 0, tiled=True).reshape(nc, nz, traits, 128), axis=0)
    back_z = lax.all_to_all(back_c, "z", 0, 0, tiled=True)

    own_resid = lax.dynamic_slice_in_dim(resid, x_index * traits_here, traits_here, 0)
    image_u, image_a, sums = call(
        image_kernel,
        (sds(traits_here, animals), sds(traits, columns), sds(1, 128)),
        scratch=[
            pltpu.VMEM((2 * traits_here * blocks, 128), F32),
            pltpu.VMEM((traits_here * blocks, 128), F32),
        ],
    )(
        got_values, c_term, rank, sire_row, dam_row, incoming, own_resid,
        dir_u, rec_weight, res_u, inv_diag_u,
        back_z, snp_ridge[:, None], d_a, r_a, i_a,
    )

    def by_blocks():
        mixed = jnp.dot(genetic_inv, dir_all, precision=lax.Precision.HIGHEST)
        image = rec_weight * dir_u + pedigree_by_blocks(mixed, sire, dam, herd, herd_index)
        image = image.at[:, :genotyped].add(own_resid[:, :genotyped])
        cells = [
            jnp.sum(inv_diag_u * res_u * res_u) + jnp.sum(i_a * r_a * r_a),
            jnp.sum(dir_u * image) + jnp.sum(d_a * image_a),
            jnp.sum(inv_diag_u * res_u * image) + jnp.sum(i_a * r_a * image_a),
            jnp.sum(inv_diag_u * image * image) + jnp.sum(i_a * image_a * image_a),
        ]
        return image, jnp.pad(jnp.stack(cells), (0, 124))[None, :]

    image_u, sums = lax.cond(over[0, 0] >= 8.0, by_blocks, lambda: (image_u, sums))

    near = lax.all_to_all(
        jnp.broadcast_to(sums[None], (ny * nc * nx, 1, 128)), ("y", "c", "x"), 0, 0, tiled=True
    )
    near = jnp.sum(near, axis=0, keepdims=True)
    far = lax.all_to_all(jnp.broadcast_to(near, (nz, 1, 128)), "z", 0, 0, tiled=True)

    u, a = sds(traits_here, animals), sds(traits, columns)
    outs = call(update_kernel, (u, u, u, a, a, a))(
        far, sol_u, res_u, dir_u, inv_diag_u, image_u, s_a, r_a, d_a, i_a, image_a
    )
    return tuple(outs[:3]) + tuple(o[:, None, :] for o in outs[3:])


def solution(mesh):
    herd, nx = mesh.devices.shape
    ny, nc = (4, 2) if herd == 128 else (2, 2)
    grid = Mesh(mesh.devices.reshape(ny, herd // (ny * nc), nc, nx), ("y", "z", "c", "x"))
    u = P("x", HERD)
    a = P(None, "x", HERD)
    return jax.shard_map(
        body,
        mesh=grid,
        in_specs=(
            u, u, u, u, u, a, a, a, a,
            P(HERD, "x"), P("x"), P("x"), P(), P("x", None), P(HERD), P(HERD),
        ),
        out_specs=(u, u, u, a, a, a),
        check_vma=False,
    )
```

```python
import functools
import math

import jax
import jax.numpy as jnp
from jax import lax
from jax.experimental import pallas as pl
from jax.experimental.pallas import tpu as pltpu
from jax.sharding import Mesh, PartitionSpec as P

SLOTS = 2
CAP = 64
LIST = CAP - 1
CHUNK = 512
HERD = ("y", "z", "c")
F32 = jnp.float32
BF16 = jnp.bfloat16
NT = (((1,), (1,)), ((), ()))
TN = (((0,), (0,)), ((), ()))
NN = (((1,), (0,)), ((), ()))


def call(kernel, out, scratch=(), **kw):
    return pl.pallas_call(
        kernel,
        out_shape=out,
        scratch_shapes=list(scratch),
        compiler_params=pltpu.CompilerParams(vmem_limit_bytes=40 * 2**20),
        **kw,
    )


def dot(a, b, dims=NN):
    return lax.dot_general(a, b, dims, preferred_element_type=F32)


def parts(x, n=2):
    out = []
    for _ in range(n):
        p = x.astype(BF16).astype(F32)
        out.append(p)
        x = x - p
    return out


def rows_at(n, cols):
    return lax.broadcasted_iota(jnp.int32, (n, cols), 0)


def weights(sire, dam):
    known = (sire >= 0).astype(jnp.int32) + (dam >= 0).astype(jnp.int32)
    return jnp.where(known == 2, 2.0, jnp.where(known == 1, 4.0 / 3.0, 1.0)).astype(F32)


def dam_place(dam, animals):
    local = dam & (animals - 1)
    block = jnp.where(dam >= 0, local >> 7, -1)
    return block, local & 127


def one_hot(index, rows):
    return (rows_at(rows, index.shape[1]) == index).astype(F32).astype(BF16)


def pick(found, in_group, t):
    rows = in_group.shape[0]
    return jnp.sum(jnp.where(in_group, found[t * rows : (t + 1) * rows], 0.0), axis=0, keepdims=True)


def table_of(ref):
    return jnp.concatenate([p.astype(BF16) for p in parts(ref[...])], axis=0)


def masked(in_group, fields):
    return jnp.concatenate([jnp.where(in_group, f, 0.0).astype(BF16) for f in fields], axis=0)


def moved(width, pieces, load, rows):
    lane = lax.broadcasted_iota(jnp.int32, (rows, 128), 1)
    for k in range(width // 128):
        tile = jnp.zeros((rows, 128), F32)
        for source, first, at, length in pieces:
            lo, hi = max(at, k * 128), min(at + length, (k + 1) * 128)
            while lo < hi:
                src = first + lo - at
                end = min(hi, lo + 128 - src % 128)
                turn = (lo - src) % 128
                value = load(source, src // 128)
                if turn:
                    value = pltpu.roll(value, turn, 1)
                a, b = lo - k * 128, end - k * 128
                tile = value if (a, b) == (0, 128) else jnp.where((lane >= a) & (lane < b), value, tile)
                lo = end
        yield k, tile


def lists_kernel(dir_ref, dir_a_ref, sire_ref, dam_ref, out_ref, rank_ref, tab_ref, acc_ref, *, shape):
    ny, nz, nc = shape
    traits, animals = dir_ref.shape
    herd = ny * nz * nc
    blocks = animals // 128
    n = CHUNK
    for t in range(traits):
        for b in range(blocks):
            tab_ref[t * blocks + b : t * blocks + b + 1, :] = dir_ref[t : t + 1, b * 128 : (b + 1) * 128]
    table = table_of(tab_ref)
    half = traits * blocks
    before = (rows_at(n, n) < lax.broadcasted_iota(jnp.int32, (n, n), 1)).astype(F32).astype(BF16)
    acc_ref[...] = jnp.zeros(acc_ref.shape, F32)

    def step(k, carry):
        at = pl.ds(pl.multiple_of(k * n, n), n)
        sire = sire_ref[:, at]
        dam = dam_ref[:, at]
        weight = weights(sire, dam)
        block, offset = dam_place(dam, animals)
        found = dot(table, one_hot(offset, 128))
        found = found[:half] + found[half:]
        in_block = rows_at(blocks, n) == block
        own = dir_ref[:, at]
        is_owner = rows_at(herd, n) == owner_row(sire, animals, shape)
        owners = is_owner.astype(F32).astype(BF16)
        earlier = dot(owners, before) + carry
        rank = jnp.sum(jnp.where(is_owner, earlier, 0.0), axis=0, keepdims=True).astype(jnp.int32)
        rank = jnp.where((sire >= 0) & (rank < LIST), rank, -1)
        rank_ref[:, at] = rank
        local = (sire & (animals - 1)) + 1
        high = [(local & ~63).astype(F32), weight * 1.5]
        low = [(local & 63).astype(F32), jnp.zeros((1, n), F32)]
        for t in range(traits):
            hi, lo = parts(weight * (own[t : t + 1] - 0.5 * pick(found, in_block, t)))
            high.append(hi)
            low.append(lo)
        acc_ref[...] += dot(masked(rows_at(CAP, n) == rank, high + low), owners, NT)
        return carry + jnp.sum(jnp.where(is_owner, 1.0, 0.0), axis=1, keepdims=True)

    count = lax.fori_loop(0, animals // n, step, jnp.zeros((herd, 1), F32))
    width = (2 + traits) * CAP
    overflow = jnp.where(jnp.max(count, axis=0, keepdims=True) > LIST + 0.5, 1.0, 0.0)
    lane = lax.broadcasted_iota(jnp.int32, (herd, 128), 1)
    for j in range(width // 128):
        at = slice(j * 128, (j + 1) * 128)
        block = (acc_ref[at, :] + acc_ref[width + j * 128 : width + (j + 1) * 128, :]).T
        if j == 0:
            block = jnp.where(lane == 127, overflow, block)
        out_ref[:, :, at] = block.reshape(nz, ny * nc, 128)
    rows = ny * nc
    columns = dir_a_ref.shape[1]
    for j in range(dir_a_ref.shape[0] // rows):
        piece = dir_a_ref[j * rows : (j + 1) * rows, :]
        for z in range(nz):
            out_ref[z, :, width + j * 128 : width + j * 128 + columns] = piece


def owner_row(sire, animals, shape):
    ny, nz, nc = shape
    owner = sire >> (animals.bit_length() - 1)
    low = nc.bit_length() - 1
    c = owner & (nc - 1)
    z = (owner >> low) & (nz - 1)
    y = owner >> (low + nz.bit_length() - 1)
    return jnp.where(sire >= 0, z * (ny * nc) + y * nc + c, -1)


def forward_kernel(in_ref, out_ref, *, columns, lists):
    nz, near, _ = in_ref.shape
    traits = out_ref.shape[1]
    for g in range(near):
        out_ref[g, :nz, :lists] = in_ref[:, g, :lists]
    pieces = [(z, 0, z * columns, columns) for z in range(nz)]
    for j in range(traits // near):
        first = lists + j * 128
        load = lambda z, _: in_ref[z, :, first : first + 128]
        for k, tile in moved(nz * columns, pieces, load, near):
            for g in range(near):
                out_ref[g, j * near : (j + 1) * near, lists + k * 128 : lists + (k + 1) * 128] = tile


def gather_kernel(
    in_ref, tab_ref, geno_ref, freq_ref, gw_ref, out_ref, turned_ref, weight_ref, over_ref,
    joined_ref, acc_ref, *, shape, columns, lists, scale,
):
    ny, nz, nc = shape
    herd = ny * nz * nc
    traits = in_ref.shape[1]
    half = tab_ref.shape[0]
    blocks = weight_ref.shape[0]
    here = half // blocks
    genotyped = geno_ref.shape[0]
    for j in range(lists // 128):
        at = slice(j * 128, (j + 1) * 128)
        turned_ref[at, :] = in_ref[:, :nz, at].reshape(herd, 128).T
    over_ref[...] = jnp.broadcast_to(jnp.max(turned_ref[127:128, :], keepdims=True), over_ref.shape)
    acc_ref[...] = jnp.zeros(acc_ref.shape, F32)
    group = 8

    def step(k, _):
        r = pl.multiple_of(k * group, group)
        place = flat(turned_ref, r, group).astype(jnp.int32) - 1
        in_block = rows_at(blocks, group * herd) == (place >> 7)
        high, low = [], []
        for t in range(here):
            hi, lo = parts(flat(turned_ref, (2 + t) * CAP + r, group))
            high.append(hi)
            low.append(lo)
        fields = masked(in_block, high + low + [flat(turned_ref, CAP + r, group)])
        acc_ref[...] += dot(fields, one_hot(place & 127, 128), NT)
        return 0

    lax.fori_loop(0, CAP // group, step, 0)
    weight_ref[...] = acc_ref[2 * half :, :] * (0.25 / 1.5)
    out_ref[traits : traits + half, :] = acc_ref[:half, :] + acc_ref[half : 2 * half, :]
    out_ref[traits + half :, :] = tab_ref[...]

    width = nz * nc * columns
    total = jnp.zeros((3 * traits, genotyped), F32)
    bias = jnp.zeros((traits, 1), F32)
    for y in range(ny):
        pieces = [
            (y * nc + c, z * columns, (z * nc + c) * columns, columns) for z in range(nz) for c in range(nc)
        ]
        load = lambda g, k: in_ref[g, :, lists + k * 128 : lists + (k + 1) * 128]
        for k, tile in moved(width, pieces, load, traits):
            joined_ref[:, k * 128 : (k + 1) * 128] = tile
        at = slice(y * width, (y + 1) * width)
        values = joined_ref[...]
        stack = jnp.concatenate([p.astype(BF16) for p in parts(values, 3)], axis=0)
        total = total + dot(stack, geno_ref[:, at], NT)
        bias = bias + jnp.sum(values * (2.0 * freq_ref[:, at]), axis=1, keepdims=True)
    rows = total[:traits] + total[traits : 2 * traits] + total[2 * traits :]
    out_ref[:traits, :] = jnp.zeros((traits, 128), F32)
    out_ref[:traits, :genotyped] = (rows - bias) * scale
    out_ref[:traits, genotyped : genotyped + 1] = gw_ref[...]


def flat(ref, first, group):
    tile = ref[pl.ds(first, group), :]
    return jnp.concatenate([tile[j : j + 1] for j in range(group)], axis=1)


def reply_kernel(
    mix_ref, all_ref, ids_ref, weight_ref, geno_ref, freq_ref,
    out_ref, tab_ref, inc_ref, resid_ref, vals_ref, rows_ref, summed_ref, *, shape, columns, scale,
):
    ny, nz, nc = shape
    herd = ny * nz * nc
    nx = all_ref.shape[0]
    traits = resid_ref.shape[0]
    half = tab_ref.shape[0]
    blocks = weight_ref.shape[0]
    here = half // blocks
    genotyped = geno_ref.shape[0]
    for t in range(here):
        value = jnp.zeros((blocks, 128), F32)
        added = jnp.zeros((blocks, 128), F32)
        for x in range(nx):
            for s in range(here):
                factor = mix_ref[t, x * here + s]
                at = traits + s * blocks
                added = added + factor * all_ref[x, at : at + blocks, :]
                value = value + factor * all_ref[x, half + at : half + at + blocks, :]
        at = slice(t * blocks, (t + 1) * blocks)
        tab_ref[at, :] = value
        inc_ref[at, :] = weight_ref[...] * value - 0.5 * added

    table = table_of(tab_ref)
    group = 8

    def step(k, _):
        r = pl.multiple_of(k * group, group)
        place = flat(ids_ref, r, group).astype(jnp.int32) - 1
        in_block = rows_at(blocks, group * herd) == (place >> 7)
        found = dot(table, one_hot(place & 127, 128))
        found = found[:half] + found[half:]
        for t in range(here):
            value = pick(found, in_block, t)
            vals_ref[pl.ds(t * CAP + r, group), :] = jnp.concatenate(
                [value[:, j * herd : (j + 1) * herd] for j in range(group)], axis=0
            )
        return 0

    lax.fori_loop(0, CAP // group, step, 0)
    values = here * CAP
    for j in range(values // 128):
        at = slice(j * 128, (j + 1) * 128)
        out_ref[:, :nz, at] = vals_ref[at, :].T.reshape(ny * nc, nz, 128)

    for x in range(nx):
        for s in range(here):
            at = traits + half + s * blocks
            rows_ref[x * here + s : x * here + s + 1, :] = all_ref[x, at : at + 1, :]
    total = all_ref[0, :traits, :]
    for x in range(1, nx):
        total = total + all_ref[x, :traits, :]
    lane = lax.broadcasted_iota(jnp.int32, (traits, 128), 1)
    weight = jnp.sum(jnp.where(lane == genotyped, total, 0.0), axis=1, keepdims=True)
    resid = jnp.where(lane < genotyped, weight * (rows_ref[...] - total), 0.0)
    resid_ref[...] = resid
    stack = jnp.concatenate([p.astype(BF16) for p in parts(resid, 3)], axis=0)[:, :genotyped]
    summed = jnp.sum(resid, axis=1, keepdims=True)
    width = nz * nc * columns
    for y in range(ny):
        at = slice(y * width, (y + 1) * width)
        found = dot(stack, geno_ref[:, at])
        found = found[:traits] + found[traits : 2 * traits] + found[2 * traits :]
        summed_ref[...] = (found - summed * (2.0 * freq_ref[:, at])) * scale
        for c in range(nc):
            pieces = [(0, (z * nc + c) * columns, z * columns, columns) for z in range(nz)]
            load = lambda _, k: summed_ref[:, k * 128 : (k + 1) * 128]
            for k, tile in moved(nz * columns, pieces, load, traits):
                out_ref[y * nc + c, :, values + k * 128 : values + (k + 1) * 128] = tile


def backward_kernel(in_ref, out_ref, *, columns, values):
    nz, near, _ = out_ref.shape
    traits = in_ref.shape[1]
    for g in range(near):
        out_ref[:, g, :values] = in_ref[g, :nz, :values]
    total = in_ref[0, :, values:]
    for g in range(1, near):
        total = total + in_ref[g, :, values:]
    load = lambda _, k: total[:, k * 128 : (k + 1) * 128]
    for z in range(nz):
        for _, tile in moved(128, [(0, z * columns, 0, columns)], load, traits):
            for j in range(traits // near):
                first = values + j * 128
                out_ref[z, :, first : first + 128] = tile[j * near : (j + 1) * near]


def dams_kernel(tab_ref, sire_ref, dam_ref, out_ref):
    traits, animals = out_ref.shape
    blocks = animals // 128
    half = traits * blocks
    n = CHUNK
    for t in range(traits):
        for b in range(blocks):
            out_ref[t : t + 1, b * 128 : (b + 1) * 128] = tab_ref[t * blocks + b : t * blocks + b + 1, :]
    table = table_of(tab_ref)

    def step(k, _):
        at = pl.ds(pl.multiple_of(k * n, n), n)
        dam = dam_ref[:, at]
        weight = weights(sire_ref[:, at], dam)
        block, offset = dam_place(dam, animals)
        found = dot(table, one_hot(offset, 128))
        found = found[:half] + found[half:]
        in_block = rows_at(blocks, n) == block
        for t in range(traits):
            out_ref[t : t + 1, at] = weight * (out_ref[t : t + 1, at] - 0.5 * pick(found, in_block, t))
        return 0

    lax.fori_loop(0, animals // n, step, 0)


def image_kernel(
    got_ref, c_ref, rank_ref, sire_ref, dam_ref, inc_ref, resid_ref,
    dir_ref, rec_ref, res_ref, inv_ref, ridge_ref, dir_a_ref, res_a_ref, inv_a_ref,
    image_ref, image_a_ref, sums_ref, acc_ref, tab_ref, *, shape,
):
    traits, animals = c_ref.shape
    ny, nz, nc = shape
    herd, near = ny * nz * nc, ny * nc
    blocks = animals // 128
    n = CHUNK
    half = traits * blocks
    wide = traits * CAP
    table = jnp.concatenate(
        [p.astype(BF16) for p in parts(got_ref[:, :, :wide].reshape(herd, wide))], axis=1
    )
    acc_ref[...] = jnp.zeros(acc_ref.shape, F32)

    def step(k, _):
        at = pl.ds(pl.multiple_of(k * n, n), n)
        sire = sire_ref[:, at]
        dam = dam_ref[:, at]
        weight = weights(sire, dam)
        found = dot(table, one_hot(owner_row(sire, animals, shape), herd), TN)
        found = found[:wide] + found[wide:]
        in_slot = rows_at(CAP, n) == rank_ref[:, at]
        block, offset = dam_place(dam, animals)
        high, low = [], []
        for t in range(traits):
            scaled = c_ref[t : t + 1, at] - 0.5 * weight * pick(found, in_slot, t)
            image_ref[t : t + 1, at] = scaled
            hi, lo = parts(scaled)
            high.append(hi)
            low.append(lo)
        acc_ref[...] += dot(masked(rows_at(blocks, n) == block, high + low), one_hot(offset, 128), NT)
        return 0

    lax.fori_loop(0, animals // n, step, 0)
    tab_ref[...] = inc_ref[...] - 0.5 * (acc_ref[:half, :] + acc_ref[half:, :])
    for b in range(blocks):
        for t in range(traits):
            at = (slice(t, t + 1), slice(b * 128, (b + 1) * 128))
            image_ref[at] = image_ref[at] + tab_ref[t * blocks + b : t * blocks + b + 1, :]
    image_ref[:, :128] = image_ref[:, :128] + resid_ref[...]
    direction = dir_ref[...]
    image = image_ref[...] + rec_ref[...] * direction
    image_ref[...] = image
    res = res_ref[...]
    inv = inv_ref[...]
    columns = dir_a_ref.shape[1]
    sums = jnp.sum(got_ref[:, :, wide:], axis=0)
    tiles = sums.shape[1] // 128
    back = jnp.concatenate([sums[:, j * 128 : (j + 1) * 128] for j in range(tiles)], axis=0)[:, :columns]
    dir_a = dir_a_ref[...]
    image_a = ridge_ref[...] * dir_a - back
    image_a_ref[...] = image_a
    res_a = res_a_ref[...]
    inv_a = inv_a_ref[...]
    weighted, weighted_a = inv * res, inv_a * res_a
    lane = lax.broadcasted_iota(jnp.int32, (1, 128), 1)
    pairs = (
        (weighted * res, weighted_a * res_a),
        (direction * image, dir_a * image_a),
        (weighted * image, weighted_a * image_a),
        (inv * image * image, inv_a * image_a * image_a),
    )
    total = jnp.zeros((1, 128), F32)
    for j, (one, two) in enumerate(pairs):
        value = jnp.sum(one, keepdims=True) + jnp.sum(two, keepdims=True)
        total = jnp.where(lane == j, value, total)
    sums_ref[...] = total


def update_kernel(
    sums_ref, sol_ref, res_ref, dir_ref, inv_ref, image_ref,
    sol_a_ref, res_a_ref, dir_a_ref, inv_a_ref, image_a_ref,
    nsol_ref, nres_ref, ndir_ref, nsol_a_ref, nres_a_ref, ndir_a_ref,
):
    total = jnp.sum(sums_ref[...], axis=0)
    norm, curve, cross, square = (total[:, j : j + 1] for j in range(4))
    size = norm / curve
    following = norm - 2.0 * size * cross + size * size * square
    ratio = following / norm
    for sol, res, dire, inv, image, nsol, nres, ndir in (
        (sol_ref, res_ref, dir_ref, inv_ref, image_ref, nsol_ref, nres_ref, ndir_ref),
        (sol_a_ref, res_a_ref, dir_a_ref, inv_a_ref, image_a_ref, nsol_a_ref, nres_a_ref, ndir_a_ref),
    ):
        d = dire[...]
        nsol[...] = sol[...] + size * d
        left = res[...] - size * image[...]
        nres[...] = left
        ndir[...] = inv[...] * left + ratio * d


def pedigree_by_blocks(field, sire, dam, herd_count, herd_index):
    traits_here, animals = field.shape
    block_count = animals // 128
    span = SLOTS * 128
    has_sire = sire >= 0
    has_dam = dam >= 0
    sire_known = has_sire.astype(F32)
    dam_known = has_dam.astype(F32)
    owner_herd = jnp.where(has_sire, sire // animals, 0)
    block_index = jnp.where(has_sire, sire % animals // 128, 0)
    offset = jnp.where(has_sire, sire % 128, 0)
    flat_block = jnp.where(
        has_sire, owner_herd * block_count + block_index, herd_count * block_count
    )
    present = jnp.zeros((herd_count * block_count + 1,), jnp.int32).at[flat_block].max(1)
    present = present[:-1].reshape(herd_count, block_count)
    slot_order = jnp.cumsum(present, axis=1) - 1
    slot_range = jnp.arange(SLOTS, dtype=jnp.int32)
    slot_match = (present[:, :, None] == 1) & (slot_order[:, :, None] == slot_range[None, None, :])
    block_ids = jnp.arange(block_count, dtype=jnp.int32)[None, :, None] + 1
    wanted = jnp.sum(jnp.where(slot_match, block_ids, 0), axis=1) - 1
    requests = lax.all_to_all(wanted, HERD, split_axis=0, concat_axis=0, tiled=True)
    live_slot = requests >= 0
    field_tiles = field.reshape(traits_here, block_count, 128)
    outgoing = field_tiles[:, jnp.where(live_slot, requests, 0), :]
    outgoing = jnp.where(live_slot[None, :, :, None], outgoing, 0.0).reshape(
        traits_here, herd_count, span
    )
    fetched = lax.all_to_all(outgoing, HERD, split_axis=1, concat_axis=1, tiled=True).reshape(
        traits_here, herd_count * span
    )
    slot_index = slot_order[owner_herd, block_index]
    buffer_place = owner_herd * span + slot_index * 128 + offset
    sire_values = fetched[:, jnp.where(has_sire, buffer_place, 0)]
    local_dam = jnp.where(has_dam, dam - herd_index * animals, 0)
    dam_values = field[:, local_dam]
    weight = 4.0 / (4.0 - sire_known - dam_known)
    scaled = weight * (field - 0.5 * sire_known * sire_values - 0.5 * dam_known * dam_values)
    dam_target = jnp.where(has_dam, local_dam, animals)
    dam_terms = (
        jnp.zeros((traits_here, animals + 1), F32).at[:, dam_target].add(-0.5 * dam_known * scaled)
    )
    result = scaled + dam_terms[:, :animals]
    sire_target = jnp.where(has_sire, buffer_place, herd_count * span)
    outbound = (
        jnp.zeros((traits_here, herd_count * span + 1), F32)
        .at[:, sire_target]
        .add(-0.5 * sire_known * scaled)
    )
    outbound = outbound[:, :-1].reshape(traits_here, herd_count, span)
    returned = lax.all_to_all(outbound, HERD, split_axis=1, concat_axis=1, tiled=True).reshape(
        traits_here, herd_count * SLOTS, 128
    )
    block_target = jnp.where(live_slot, requests, block_count).reshape(herd_count * SLOTS)
    incoming = (
        jnp.zeros((traits_here, block_count + 1, 128), F32).at[:, block_target, :].add(returned)
    )
    return result + incoming[:, :block_count, :].reshape(traits_here, animals)


def body(
    sol_u, res_u, dir_u, rec_weight, inv_diag_u, sol_a, res_a, dir_a, inv_diag_a,
    genotypes, allele_freq, geno_weight, snp_ridge, genetic_inv, sire, dam,
):
    shape = ny, nz, nc = tuple(lax.axis_size(a) for a in HERD)
    nx = lax.axis_size("x")
    herd, near = ny * nz * nc, ny * nc
    herd_index = lax.axis_index(HERD)
    x_index = lax.axis_index("x")
    here, animals = dir_u.shape
    traits, _, columns = dir_a.shape
    genotyped, snps = genotypes.shape
    blocks = animals // 128
    half = here * blocks
    lists, values = (2 + here) * CAP, here * CAP
    spare = traits // near * 128
    scale = 2.0 / math.sqrt(snps * nx)
    sds = lambda *s: jax.ShapeDtypeStruct(s, F32)
    vmem = lambda *s: pltpu.VMEM(s, F32)
    d_a, r_a, s_a, i_a = (a[:, 0, :] for a in (dir_a, res_a, sol_a, inv_diag_a))
    freq = allele_freq[None, :]
    sire_row, dam_row = sire[None, :], dam[None, :]
    weight_here = lax.dynamic_update_slice(
        jnp.zeros((traits, 1), F32), geno_weight[:, None], (x_index * here, 0)
    )

    out_z, rank, table = call(
        functools.partial(lists_kernel, shape=shape),
        (sds(nz, near, lists + spare), jax.ShapeDtypeStruct((1, animals), jnp.int32), sds(half, 128)),
        scratch=[vmem(2 * lists, herd)],
    )(dir_u, d_a, sire_row, dam_row)
    in_z = lax.all_to_all(out_z, "z", 0, 0, tiled=True)
    out_near = call(
        functools.partial(forward_kernel, columns=columns, lists=lists),
        sds(near, traits, lists + nz * columns),
    )(in_z)
    in_near = lax.all_to_all(out_near, ("y", "c"), 0, 0, tiled=True)

    to_x, turned, weight_sum, over = call(
        functools.partial(gather_kernel, shape=shape, columns=columns, lists=lists, scale=scale),
        (sds(traits + 2 * half, 128), sds(lists, herd), sds(blocks, 128), sds(8, 128)),
        scratch=[vmem(traits, nz * nc * columns), vmem(2 * half + blocks, 128)],
    )(in_near, table, genotypes, freq, weight_here)
    from_x = lax.all_gather(to_x, "x", axis=0)

    on_chip = pl.BlockSpec(memory_space=pltpu.VMEM)
    back_near, mixed_table, incoming, resid = call(
        functools.partial(reply_kernel, shape=shape, columns=columns, scale=scale),
        (sds(near, traits, values + nz * columns), sds(half, 128), sds(half, 128), sds(traits, 128)),
        scratch=[vmem(values, herd), vmem(traits, 128), vmem(traits, nz * nc * columns)],
        in_specs=[pl.BlockSpec(memory_space=pltpu.SMEM)] + [on_chip] * 5,
    )(genetic_inv, from_x, turned, weight_sum, genotypes, freq)
    got_near = lax.all_to_all(back_near, ("y", "c"), 0, 0, tiled=True)
    back_z = call(
        functools.partial(backward_kernel, columns=columns, values=values), sds(nz, near, values + spare)
    )(got_near)
    got_z = lax.all_to_all(back_z, "z", 0, 0, tiled=True)

    c_term = call(dams_kernel, sds(here, animals))(mixed_table, sire_row, dam_row)
    own_resid = lax.dynamic_slice_in_dim(resid, x_index * here, here, 0)
    image_u, image_a, sums = call(
        functools.partial(image_kernel, shape=shape),
        (sds(here, animals), sds(traits, columns), sds(1, 128)),
        scratch=[vmem(2 * half, 128), vmem(half, 128)],
    )(
        got_z, c_term, rank, sire_row, dam_row, incoming, own_resid,
        dir_u, rec_weight, res_u, inv_diag_u, snp_ridge[:, None], d_a, r_a, i_a,
    )

    def by_blocks():
        dir_all = from_x[:, traits + half :, :].reshape(traits, animals)
        mixed = jnp.dot(genetic_inv, dir_all, precision=lax.Precision.HIGHEST)
        image = rec_weight * dir_u + pedigree_by_blocks(mixed, sire, dam, herd, herd_index)
        image = image.at[:, :genotyped].add(own_resid[:, :genotyped])
        cells = [
            jnp.sum(inv_diag_u * res_u * res_u) + jnp.sum(i_a * r_a * r_a),
            jnp.sum(dir_u * image) + jnp.sum(d_a * image_a),
            jnp.sum(inv_diag_u * res_u * image) + jnp.sum(i_a * r_a * image_a),
            jnp.sum(inv_diag_u * image * image) + jnp.sum(i_a * image_a * image_a),
        ]
        return image, jnp.pad(jnp.stack(cells), (0, 124))[None, :]

    image_u, sums = lax.cond(over[0, 0] > 0.5, by_blocks, lambda: (image_u, sums))

    close = lax.all_to_all(
        jnp.broadcast_to(sums[None], (near * nx, 1, 128)), ("y", "c", "x"), 0, 0, tiled=True
    )
    close = jnp.sum(close, axis=0, keepdims=True)
    far = lax.all_to_all(jnp.broadcast_to(close, (nz, 1, 128)), "z", 0, 0, tiled=True)

    u, a = sds(here, animals), sds(traits, columns)
    outs = call(update_kernel, (u, u, u, a, a, a))(
        far, sol_u, res_u, dir_u, inv_diag_u, image_u, s_a, r_a, d_a, i_a, image_a
    )
    return tuple(outs[:3]) + tuple(o[:, None, :] for o in outs[3:])


def solution(mesh):
    herd, nx = mesh.devices.shape
    ny, nc = 4, 2
    grid = Mesh(mesh.devices.reshape(ny, herd // (ny * nc), nc, nx), HERD + ("x",))
    u = P("x", HERD)
    a = P(None, "x", HERD)
    return jax.shard_map(
        body,
        mesh=grid,
        in_specs=(
            u, u, u, u, u, a, a, a, a,
            P(HERD, "x"), P("x"), P("x"), P(), P("x", None), P(HERD), P(HERD),
        ),
        out_specs=(u, u, u, a, a, a),
        check_vma=False,
    )
```

```python
import functools
import math

import jax
import jax.numpy as jnp
from jax import lax
from jax.experimental import pallas as pl
from jax.experimental.pallas import tpu as pltpu
from jax.sharding import Mesh, PartitionSpec as P

SLOTS = 2
CAP = 64
LIST = CAP - 1
CHUNK = 512
HERD = ("y", "z", "c")
F32 = jnp.float32
BF16 = jnp.bfloat16
NT = (((1,), (1,)), ((), ()))
NN = (((1,), (0,)), ((), ()))


def call(kernel, out, scratch=(), **kw):
    return pl.pallas_call(
        kernel,
        out_shape=out,
        scratch_shapes=list(scratch),
        compiler_params=pltpu.CompilerParams(vmem_limit_bytes=40 * 2**20),
        **kw,
    )


def dot(a, b, dims=NN):
    return lax.dot_general(a, b, dims, preferred_element_type=F32)


def parts(x, n=2):
    out = []
    for _ in range(n):
        p = x.astype(BF16).astype(F32)
        out.append(p)
        x = x - p
    return out


def rows_at(n, cols):
    return lax.broadcasted_iota(jnp.int32, (n, cols), 0)


def weights(sire, dam):
    known = (sire >= 0).astype(jnp.int32) + (dam >= 0).astype(jnp.int32)
    return jnp.where(known == 2, 2.0, jnp.where(known == 1, 4.0 / 3.0, 1.0)).astype(F32)


def place_in(local, known):
    return jnp.where(known, (local >> 7) & 15, -1), ((local >> 11) << 7) + (local & 127)


def one_hot(index, rows):
    return (rows_at(rows, index.shape[1]) == index).astype(F32).astype(BF16)


def pick(found, in_group, t):
    rows = in_group.shape[0]
    return jnp.sum(jnp.where(in_group, found[t * rows : (t + 1) * rows], 0.0), axis=0, keepdims=True)


def side_by_side(table):
    return jnp.concatenate([p.astype(BF16) for p in parts(table)], axis=1)


def look_up(table, index, rows):
    hit = one_hot(index, rows)
    return dot(table, jnp.concatenate([hit, hit], axis=0))


def both_halves(acc_ref, first, rows):
    at = slice(first, first + rows)
    return jnp.concatenate([acc_ref[at, :128], acc_ref[at, 128:]], axis=0)


def masked(in_group, fields):
    return jnp.concatenate([jnp.where(in_group, f, 0.0).astype(BF16) for f in fields], axis=0)


def moved(width, pieces, load, rows):
    lane = lax.broadcasted_iota(jnp.int32, (rows, 128), 1)
    for k in range(width // 128):
        tile = jnp.zeros((rows, 128), F32)
        for source, first, at, length in pieces:
            lo, hi = max(at, k * 128), min(at + length, (k + 1) * 128)
            while lo < hi:
                src = first + lo - at
                end = min(hi, lo + 128 - src % 128)
                turn = (lo - src) % 128
                value = load(source, src // 128)
                if turn:
                    value = pltpu.roll(value, turn, 1)
                a, b = lo - k * 128, end - k * 128
                tile = value if (a, b) == (0, 128) else jnp.where((lane >= a) & (lane < b), value, tile)
                lo = end
        yield k, tile


def lists_kernel(dir_ref, dir_a_ref, sire_ref, dam_ref, out_ref, rank_ref, tab_ref, acc_ref, *, shape):
    ny, nz, nc = shape
    traits, animals = dir_ref.shape
    herd = ny * nz * nc
    blocks = animals // 128
    n = CHUNK
    for t in range(traits):
        for b in range(blocks):
            tab_ref[t * blocks + b : t * blocks + b + 1, :] = dir_ref[t : t + 1, b * 128 : (b + 1) * 128]
    table = side_by_side(tab_ref[...])
    before = (rows_at(n, n) < lax.broadcasted_iota(jnp.int32, (n, n), 1)).astype(F32).astype(BF16)
    acc_ref[...] = jnp.zeros(acc_ref.shape, F32)
    short = CAP // 2

    def step(k, carry):
        at = pl.ds(pl.multiple_of(k * n, n), n)
        sire = sire_ref[:, at]
        dam = dam_ref[:, at]
        weight = weights(sire, dam)
        local_dam = dam & (animals - 1)
        found = look_up(table, local_dam & 127, 128)
        in_block = rows_at(blocks, n) == jnp.where(dam >= 0, local_dam >> 7, -1)
        own = dir_ref[:, at]
        row = owner_row(sire, animals, shape)
        is_owner = rows_at(herd, n) == row
        owners = is_owner.astype(F32).astype(BF16)
        earlier = dot(owners, before) + carry
        rank = jnp.sum(jnp.where(is_owner, earlier, 0.0), axis=0, keepdims=True).astype(jnp.int32)
        rank = jnp.where((sire >= 0) & (rank < LIST), rank, -1)
        rank_ref[:, at] = rank
        local = (sire & (animals - 1)) + 1
        fields = [(local & ~63).astype(F32), (local & 63).astype(F32), weight * 1.5]
        for t in range(traits):
            fields += parts(weight * (own[t : t + 1] - 0.5 * pick(found, in_block, t)))
        in_row = rows_at(short, n) == jnp.where(rank >= 0, rank & (short - 1), -1)
        target = one_hot((rank >> (short.bit_length() - 1)) * herd + row, 2 * herd)
        acc_ref[...] += dot(masked(in_row, fields), target, NT)
        return earlier[:, n - 1 :] + owners[:, n - 1 :].astype(F32)

    count = lax.fori_loop(0, animals // n, step, jnp.zeros((herd, 1), F32), unroll=True)
    width = (2 + traits) * CAP
    overflow = jnp.where(jnp.max(count, axis=0, keepdims=True) > LIST + 0.5, 1.0, 0.0)
    lane = lax.broadcasted_iota(jnp.int32, (herd, 128), 1)

    def slots(f):
        at = slice(f * short, (f + 1) * short)
        return jnp.concatenate([acc_ref[at, :herd], acc_ref[at, herd:]], axis=0)

    lines = [slots(0) + slots(1), slots(2)] + [slots(3 + 2 * t) + slots(4 + 2 * t) for t in range(traits)]
    for j in range(width // 128):
        block = jnp.concatenate(lines[2 * j : 2 * j + 2], axis=0).T
        if j == 0:
            block = jnp.where(lane == 127, overflow, block)
        out_ref[:, :, j * 128 : (j + 1) * 128] = block.reshape(nz, ny * nc, 128)
    rows = ny * nc
    columns = dir_a_ref.shape[1]
    for j in range(dir_a_ref.shape[0] // rows):
        piece = dir_a_ref[j * rows : (j + 1) * rows, :]
        for z in range(nz):
            out_ref[z, :, width + j * 128 : width + j * 128 + columns] = piece


def owner_row(sire, animals, shape):
    ny, nz, nc = shape
    owner = sire >> (animals.bit_length() - 1)
    low = nc.bit_length() - 1
    c = owner & (nc - 1)
    z = (owner >> low) & (nz - 1)
    y = owner >> (low + nz.bit_length() - 1)
    return jnp.where(sire >= 0, z * (ny * nc) + y * nc + c, -1)


def forward_kernel(in_ref, out_ref, *, columns, lists):
    nz, near, _ = in_ref.shape
    traits = out_ref.shape[1]
    for g in range(near):
        out_ref[g, :nz, :lists] = in_ref[:, g, :lists]
    pieces = [(z, 0, z * columns, columns) for z in range(nz)]
    for j in range(traits // near):
        first = lists + j * 128
        load = lambda z, _: in_ref[z, :, first : first + 128]
        for k, tile in moved(nz * columns, pieces, load, near):
            for g in range(near):
                out_ref[g, j * near : (j + 1) * near, lists + k * 128 : lists + (k + 1) * 128] = tile


def gather_kernel(
    in_ref, geno_ref, freq_ref, gw_ref, out_ref, added_ref, turned_ref, weight_ref, over_ref,
    joined_ref, acc_ref, wide_ref, *, shape, columns, lists, scale,
):
    ny, nz, nc = shape
    herd = ny * nz * nc
    traits = in_ref.shape[1]
    blocks = weight_ref.shape[0]
    short = blocks // 2
    here = added_ref.shape[0] // blocks
    genotyped = geno_ref.shape[0]
    for j in range(lists // 128):
        at = slice(j * 128, (j + 1) * 128)
        turned_ref[at, :] = in_ref[:, :nz, at].reshape(herd, 128).T
    over_ref[...] = jnp.broadcast_to(jnp.max(turned_ref[127:128, :], keepdims=True), over_ref.shape)
    acc_ref[...] = jnp.zeros(acc_ref.shape, F32)
    group = 8

    def step(k, _):
        r = pl.multiple_of(k * group, group)
        place = flat(turned_ref, r, group).astype(jnp.int32) - 1
        row, column = place_in(place, place >= 0)
        fields = [flat(turned_ref, CAP + r, group)]
        for t in range(here):
            fields += parts(flat(turned_ref, (2 + t) * CAP + r, group))
        acc_ref[...] += dot(masked(rows_at(short, group * herd) == row, fields), one_hot(column, 256), NT)
        return 0

    lax.fori_loop(0, CAP // group, step, 0, unroll=True)
    weight_ref[...] = both_halves(acc_ref, 0, short) * (0.25 / 1.5)
    for t in range(here):
        first = (1 + 2 * t) * short
        added_ref[t * blocks : (t + 1) * blocks, :] = both_halves(acc_ref, first, short) + both_halves(
            acc_ref, first + short, short
        )

    width = nz * nc * columns
    total = jnp.zeros((3 * traits, genotyped), F32)
    bias = jnp.zeros((traits, 1), F32)
    for y in range(ny):
        pieces = [
            (y * nc + c, z * columns, (z * nc + c) * columns, columns) for z in range(nz) for c in range(nc)
        ]
        load = lambda g, k: in_ref[g, :, lists + k * 128 : lists + (k + 1) * 128]
        for k, tile in moved(width, pieces, load, traits):
            joined_ref[:, k * 128 : (k + 1) * 128] = tile
        at = slice(y * width, (y + 1) * width)
        values = joined_ref[...]
        stack = jnp.concatenate([p.astype(BF16) for p in parts(values, 3)], axis=0)
        total = total + dot(stack, geno_ref[:, at], NT)
        bias = bias + jnp.sum(values * (2.0 * freq_ref[:, at]), axis=1, keepdims=True)
    rows = total[:traits] + total[traits : 2 * traits] + total[2 * traits :]
    wide_ref[...] = jnp.zeros((traits, 128), F32)
    wide_ref[:, :genotyped] = (rows - bias) * scale
    packed = together([wide_ref[x * here : (x + 1) * here, :] for x in range(traits // here)], genotyped)
    for x in range(out_ref.shape[0]):
        out_ref[x, :here, :] = packed
        out_ref[x, here:, :] = gw_ref[...]


def together(groups, width):
    total = groups[0]
    for x in range(1, len(groups)):
        total = total + pltpu.roll(groups[x], x * width, 1)
    return total


def flat(ref, first, group):
    tile = ref[pl.ds(first, group), :]
    return jnp.concatenate([tile[j : j + 1] for j in range(group)], axis=1)


def mixed(mix_ref, all_ref, t, blocks):
    total = jnp.zeros((blocks, 128), F32)
    here = all_ref.shape[1] // blocks
    for x in range(all_ref.shape[0]):
        for s in range(here):
            total = total + mix_ref[t, x * here + s] * all_ref[x, s * blocks : (s + 1) * blocks, :]
    return total


def reply_kernel(
    mix_ref, all_ref, pred_ref, ids_ref, geno_ref, freq_ref,
    out_ref, tab_ref, resid_ref, vals_ref, summed_ref, *, shape, columns, scale,
):
    ny, nz, nc = shape
    herd = ny * nz * nc
    nx = all_ref.shape[0]
    traits = resid_ref.shape[0]
    half = tab_ref.shape[0]
    blocks = 32
    here = half // blocks
    genotyped = geno_ref.shape[0]
    for t in range(here):
        tab_ref[t * blocks : (t + 1) * blocks, :] = mixed(mix_ref, all_ref, t, blocks)

    table = side_by_side(tab_ref[...])
    group = 8

    def step(k, _):
        r = pl.multiple_of(k * group, group)
        place = flat(ids_ref, r, group).astype(jnp.int32) - 1
        in_block = rows_at(blocks, group * herd) == (place >> 7)
        found = look_up(table, place & 127, 128)
        for t in range(here):
            value = pick(found, in_block, t)
            vals_ref[pl.ds(t * CAP + r, group), :] = jnp.concatenate(
                [value[:, j * herd : (j + 1) * herd] for j in range(group)], axis=0
            )
        return 0

    lax.fori_loop(0, CAP // group, step, 0, unroll=True)
    values = here * CAP
    for j in range(values // 128):
        at = slice(j * 128, (j + 1) * 128)
        out_ref[:, :nz, at] = vals_ref[at, :].T.reshape(ny * nc, nz, 128)

    total = pred_ref[0]
    for x in range(1, nx):
        total = total + pred_ref[x]
    lane = lax.broadcasted_iota(jnp.int32, (here, 128), 1)
    own = [
        jnp.concatenate([all_ref[x, s * blocks : s * blocks + 1, :] for s in range(here)], axis=0)
        for x in range(nx)
    ]
    own = together([jnp.where(lane < genotyped, o, 0.0) for o in own], genotyped)
    packed = total[here:] * (own - total[:here])
    for x in range(nx):
        rows = pltpu.roll(packed, 128 - x * genotyped, 1) if x else packed
        resid_ref[x * here : (x + 1) * here, :] = jnp.where(lane < genotyped, rows, 0.0)
    resid = resid_ref[...]
    stack = jnp.concatenate([p.astype(BF16) for p in parts(resid, 3)], axis=0)[:, :genotyped]
    summed = jnp.sum(resid, axis=1, keepdims=True)
    width = nz * nc * columns
    for y in range(ny):
        at = slice(y * width, (y + 1) * width)
        found = dot(stack, geno_ref[:, at])
        found = found[:traits] + found[traits : 2 * traits] + found[2 * traits :]
        summed_ref[...] = (found - summed * (2.0 * freq_ref[:, at])) * scale
        for c in range(nc):
            pieces = [(0, (z * nc + c) * columns, z * columns, columns) for z in range(nz)]
            load = lambda _, k: summed_ref[:, k * 128 : (k + 1) * 128]
            for k, tile in moved(nz * columns, pieces, load, traits):
                out_ref[y * nc + c, :, values + k * 128 : values + (k + 1) * 128] = tile


def backward_kernel(in_ref, out_ref, *, columns, values):
    nz, near, _ = out_ref.shape
    traits = in_ref.shape[1]
    for g in range(near):
        out_ref[:, g, :values] = in_ref[g, :nz, :values]
    total = in_ref[0, :, values:]
    for g in range(1, near):
        total = total + in_ref[g, :, values:]
    load = lambda _, k: total[:, k * 128 : (k + 1) * 128]
    for z in range(nz):
        for _, tile in moved(128, [(0, z * columns, 0, columns)], load, traits):
            for j in range(traits // near):
                first = values + j * 128
                out_ref[z, :, first : first + 128] = tile[j * near : (j + 1) * near]


def dams_kernel(tab_ref, sire_ref, dam_ref, out_ref):
    traits, animals = out_ref.shape
    blocks = animals // 128
    n = CHUNK
    for t in range(traits):
        for b in range(blocks):
            out_ref[t : t + 1, b * 128 : (b + 1) * 128] = tab_ref[t * blocks + b : t * blocks + b + 1, :]
    table = side_by_side(tab_ref[...])

    def step(k, _):
        at = pl.ds(pl.multiple_of(k * n, n), n)
        dam = dam_ref[:, at]
        weight = weights(sire_ref[:, at], dam)
        local = dam & (animals - 1)
        found = look_up(table, local & 127, 128)
        in_block = rows_at(blocks, n) == jnp.where(dam >= 0, local >> 7, -1)
        for t in range(traits):
            out_ref[t : t + 1, at] = weight * (out_ref[t : t + 1, at] - 0.5 * pick(found, in_block, t))
        return 0

    lax.fori_loop(0, animals // n, step, 0, unroll=True)


def image_kernel(
    mix_ref, got_ref, c_ref, rank_ref, sire_ref, dam_ref, added_ref, weight_ref, mixed_ref, resid_ref,
    dir_ref, rec_ref, res_ref, inv_ref, ridge_ref, dir_a_ref, res_a_ref, inv_a_ref,
    image_ref, image_a_ref, sums_ref, acc_ref, tab_ref, *, shape,
):
    traits, animals = c_ref.shape
    ny, nz, nc = shape
    herd, near = ny * nz * nc, ny * nc
    blocks = animals // 128
    n = CHUNK
    short = blocks // 2
    wide = traits * CAP
    table = side_by_side(got_ref[:, :, :wide].reshape(herd, wide).T)
    acc_ref[...] = jnp.zeros(acc_ref.shape, F32)

    def step(k, _):
        at = pl.ds(pl.multiple_of(k * n, n), n)
        sire = sire_ref[:, at]
        dam = dam_ref[:, at]
        weight = weights(sire, dam)
        found = look_up(table, owner_row(sire, animals, shape), herd)
        in_slot = rows_at(CAP, n) == rank_ref[:, at]
        row, column = place_in(dam & (animals - 1), dam >= 0)
        fields = []
        for t in range(traits):
            scaled = c_ref[t : t + 1, at] - 0.5 * weight * pick(found, in_slot, t)
            image_ref[t : t + 1, at] = scaled
            fields += parts(scaled)
        acc_ref[...] += dot(masked(rows_at(short, n) == row, fields), one_hot(column, 256), NT)
        return 0

    lax.fori_loop(0, animals // n, step, 0, unroll=True)
    for t in range(traits):
        at = slice(t * blocks, (t + 1) * blocks)
        first = 2 * t * short
        down = both_halves(acc_ref, first, short) + both_halves(acc_ref, first + short, short)
        down = down + mixed(mix_ref, added_ref, t, blocks)
        tab_ref[at, :] = weight_ref[...] * mixed_ref[at, :] - 0.5 * down
    for b in range(blocks):
        for t in range(traits):
            at = (slice(t, t + 1), slice(b * 128, (b + 1) * 128))
            image_ref[at] = image_ref[at] + tab_ref[t * blocks + b : t * blocks + b + 1, :]
    image_ref[:, :128] = image_ref[:, :128] + resid_ref[...]
    direction = dir_ref[...]
    image = image_ref[...] + rec_ref[...] * direction
    image_ref[...] = image
    res = res_ref[...]
    inv = inv_ref[...]
    columns = dir_a_ref.shape[1]
    sums = jnp.sum(got_ref[:, :, wide:], axis=0)
    tiles = sums.shape[1] // 128
    back = jnp.concatenate([sums[:, j * 128 : (j + 1) * 128] for j in range(tiles)], axis=0)[:, :columns]
    dir_a = dir_a_ref[...]
    image_a = ridge_ref[...] * dir_a - back
    image_a_ref[...] = image_a
    res_a = res_a_ref[...]
    inv_a = inv_a_ref[...]
    weighted, weighted_a = inv * res, inv_a * res_a
    lane = lax.broadcasted_iota(jnp.int32, (1, 128), 1)
    pairs = (
        (weighted * res, weighted_a * res_a),
        (direction * image, dir_a * image_a),
        (weighted * image, weighted_a * image_a),
        (inv * image * image, inv_a * image_a * image_a),
    )
    total = jnp.zeros((1, 128), F32)
    for j, (one, two) in enumerate(pairs):
        value = jnp.sum(one, keepdims=True) + jnp.sum(two, keepdims=True)
        total = jnp.where(lane == j, value, total)
    sums_ref[...] = total


def update_kernel(
    sums_ref, sol_ref, res_ref, dir_ref, inv_ref, image_ref,
    sol_a_ref, res_a_ref, dir_a_ref, inv_a_ref, image_a_ref,
    nsol_ref, nres_ref, ndir_ref, nsol_a_ref, nres_a_ref, ndir_a_ref,
):
    total = jnp.sum(sums_ref[...], axis=0)
    norm, curve, cross, square = (total[:, j : j + 1] for j in range(4))
    size = norm / curve
    following = norm - 2.0 * size * cross + size * size * square
    ratio = following / norm
    for sol, res, dire, inv, image, nsol, nres, ndir in (
        (sol_ref, res_ref, dir_ref, inv_ref, image_ref, nsol_ref, nres_ref, ndir_ref),
        (sol_a_ref, res_a_ref, dir_a_ref, inv_a_ref, image_a_ref, nsol_a_ref, nres_a_ref, ndir_a_ref),
    ):
        d = dire[...]
        nsol[...] = sol[...] + size * d
        left = res[...] - size * image[...]
        nres[...] = left
        ndir[...] = inv[...] * left + ratio * d


def pedigree_by_blocks(field, sire, dam, herd_count, herd_index):
    traits_here, animals = field.shape
    block_count = animals // 128
    span = SLOTS * 128
    has_sire = sire >= 0
    has_dam = dam >= 0
    sire_known = has_sire.astype(F32)
    dam_known = has_dam.astype(F32)
    owner_herd = jnp.where(has_sire, sire // animals, 0)
    block_index = jnp.where(has_sire, sire % animals // 128, 0)
    offset = jnp.where(has_sire, sire % 128, 0)
    flat_block = jnp.where(
        has_sire, owner_herd * block_count + block_index, herd_count * block_count
    )
    present = jnp.zeros((herd_count * block_count + 1,), jnp.int32).at[flat_block].max(1)
    present = present[:-1].reshape(herd_count, block_count)
    slot_order = jnp.cumsum(present, axis=1) - 1
    slot_range = jnp.arange(SLOTS, dtype=jnp.int32)
    slot_match = (present[:, :, None] == 1) & (slot_order[:, :, None] == slot_range[None, None, :])
    block_ids = jnp.arange(block_count, dtype=jnp.int32)[None, :, None] + 1
    wanted = jnp.sum(jnp.where(slot_match, block_ids, 0), axis=1) - 1
    requests = lax.all_to_all(wanted, HERD, split_axis=0, concat_axis=0, tiled=True)
    live_slot = requests >= 0
    field_tiles = field.reshape(traits_here, block_count, 128)
    outgoing = field_tiles[:, jnp.where(live_slot, requests, 0), :]
    outgoing = jnp.where(live_slot[None, :, :, None], outgoing, 0.0).reshape(
        traits_here, herd_count, span
    )
    fetched = lax.all_to_all(outgoing, HERD, split_axis=1, concat_axis=1, tiled=True).reshape(
        traits_here, herd_count * span
    )
    slot_index = slot_order[owner_herd, block_index]
    buffer_place = owner_herd * span + slot_index * 128 + offset
    sire_values = fetched[:, jnp.where(has_sire, buffer_place, 0)]
    local_dam = jnp.where(has_dam, dam - herd_index * animals, 0)
    dam_values = field[:, local_dam]
    weight = 4.0 / (4.0 - sire_known - dam_known)
    scaled = weight * (field - 0.5 * sire_known * sire_values - 0.5 * dam_known * dam_values)
    dam_target = jnp.where(has_dam, local_dam, animals)
    dam_terms = (
        jnp.zeros((traits_here, animals + 1), F32).at[:, dam_target].add(-0.5 * dam_known * scaled)
    )
    result = scaled + dam_terms[:, :animals]
    sire_target = jnp.where(has_sire, buffer_place, herd_count * span)
    outbound = (
        jnp.zeros((traits_here, herd_count * span + 1), F32)
        .at[:, sire_target]
        .add(-0.5 * sire_known * scaled)
    )
    outbound = outbound[:, :-1].reshape(traits_here, herd_count, span)
    returned = lax.all_to_all(outbound, HERD, split_axis=1, concat_axis=1, tiled=True).reshape(
        traits_here, herd_count * SLOTS, 128
    )
    block_target = jnp.where(live_slot, requests, block_count).reshape(herd_count * SLOTS)
    incoming = (
        jnp.zeros((traits_here, block_count + 1, 128), F32).at[:, block_target, :].add(returned)
    )
    return result + incoming[:, :block_count, :].reshape(traits_here, animals)


def body(
    sol_u, res_u, dir_u, rec_weight, inv_diag_u, sol_a, res_a, dir_a, inv_diag_a,
    genotypes, allele_freq, geno_weight, snp_ridge, genetic_inv, sire, dam,
):
    shape = ny, nz, nc = tuple(lax.axis_size(a) for a in HERD)
    nx = lax.axis_size("x")
    herd, near = ny * nz * nc, ny * nc
    herd_index = lax.axis_index(HERD)
    x_index = lax.axis_index("x")
    here, animals = dir_u.shape
    traits, _, columns = dir_a.shape
    genotyped, snps = genotypes.shape
    blocks = animals // 128
    half = here * blocks
    lists, values = (2 + here) * CAP, here * CAP
    spare = traits // near * 128
    scale = 2.0 / math.sqrt(snps * nx)
    sds = lambda *s: jax.ShapeDtypeStruct(s, F32)
    vmem = lambda *s: pltpu.VMEM(s, F32)
    d_a, r_a, s_a, i_a = (a[:, 0, :] for a in (dir_a, res_a, sol_a, inv_diag_a))
    freq = allele_freq[None, :]
    sire_row, dam_row = sire[None, :], dam[None, :]
    mine = jnp.arange(128) // genotyped == x_index
    weight_here = jnp.where(mine[None, :], geno_weight[:, None], 0.0)

    out_z, rank, table = call(
        functools.partial(lists_kernel, shape=shape),
        (sds(nz, near, lists + spare), jax.ShapeDtypeStruct((1, animals), jnp.int32), sds(half, 128)),
        scratch=[vmem((3 + 2 * here) * CAP // 2, 2 * herd)],
    )(dir_u, d_a, sire_row, dam_row)
    in_z = lax.all_to_all(out_z, "z", 0, 0, tiled=True)
    all_tables = lax.all_gather(table, "x", axis=0)
    in_z, all_tables = lax.optimization_barrier((in_z, all_tables))
    out_near = call(
        functools.partial(forward_kernel, columns=columns, lists=lists),
        sds(near, traits, lists + nz * columns),
    )(in_z)
    in_near = lax.all_to_all(out_near, ("y", "c"), 0, 0, tiled=True)

    to_x, added, turned, weight_sum, over = call(
        functools.partial(gather_kernel, shape=shape, columns=columns, lists=lists, scale=scale),
        (sds(nx, 2 * here, 128), sds(half, 128), sds(lists, herd), sds(blocks, 128), sds(8, 128)),
        scratch=[vmem(traits, nz * nc * columns), vmem((1 + 2 * here) * blocks // 2, 256), vmem(traits, 128)],
    )(in_near, genotypes, freq, weight_here)
    from_x = lax.all_to_all(to_x, "x", 0, 0, tiled=True)

    on_chip = pl.BlockSpec(memory_space=pltpu.VMEM)
    scalars = pl.BlockSpec(memory_space=pltpu.SMEM)
    back_near, mixed_table, resid = call(
        functools.partial(reply_kernel, shape=shape, columns=columns, scale=scale),
        (sds(near, traits, values + nz * columns), sds(half, 128), sds(traits, 128)),
        scratch=[vmem(values, herd), vmem(traits, nz * nc * columns)],
        in_specs=[scalars] + [on_chip] * 5,
    )(genetic_inv, all_tables, from_x, turned, genotypes, freq)
    got_near = lax.all_to_all(back_near, ("y", "c"), 0, 0, tiled=True)
    back_z = call(
        functools.partial(backward_kernel, columns=columns, values=values), sds(nz, near, values + spare)
    )(got_near)
    back_z, added = lax.optimization_barrier((back_z, added))
    got_z = lax.all_to_all(back_z, "z", 0, 0, tiled=True)
    all_added = lax.all_gather(added, "x", axis=0)

    c_term = call(dams_kernel, sds(here, animals))(mixed_table, sire_row, dam_row)
    own_resid = lax.dynamic_slice_in_dim(resid, x_index * here, here, 0)
    image_u, image_a, sums = call(
        functools.partial(image_kernel, shape=shape),
        (sds(here, animals), sds(traits, columns), sds(1, 128)),
        scratch=[vmem(here * blocks, 256), vmem(half, 128)],
        in_specs=[scalars] + [on_chip] * 17,
    )(
        genetic_inv, got_z, c_term, rank, sire_row, dam_row, all_added, weight_sum, mixed_table, own_resid,
        dir_u, rec_weight, res_u, inv_diag_u, snp_ridge[:, None], d_a, r_a, i_a,
    )

    def by_blocks():
        dir_all = all_tables.reshape(traits, animals)
        mixed = jnp.dot(genetic_inv, dir_all, precision=lax.Precision.HIGHEST)
        image = rec_weight * dir_u + pedigree_by_blocks(mixed, sire, dam, herd, herd_index)
        image = image.at[:, :genotyped].add(own_resid[:, :genotyped])
        cells = [
            jnp.sum(inv_diag_u * res_u * res_u) + jnp.sum(i_a * r_a * r_a),
            jnp.sum(dir_u * image) + jnp.sum(d_a * image_a),
            jnp.sum(inv_diag_u * res_u * image) + jnp.sum(i_a * r_a * image_a),
            jnp.sum(inv_diag_u * image * image) + jnp.sum(i_a * image_a * image_a),
        ]
        return image, jnp.pad(jnp.stack(cells), (0, 124))[None, :]

    image_u, sums = lax.cond(over[0, 0] > 0.5, by_blocks, lambda: (image_u, sums))

    close = lax.all_to_all(
        jnp.broadcast_to(sums[None], (near * nx, 1, 128)), ("y", "c", "x"), 0, 0, tiled=True
    )
    close = jnp.sum(close, axis=0, keepdims=True)
    far = lax.all_to_all(jnp.broadcast_to(close, (nz, 1, 128)), "z", 0, 0, tiled=True)

    u, a = sds(here, animals), sds(traits, columns)
    outs = call(update_kernel, (u, u, u, a, a, a))(
        far, sol_u, res_u, dir_u, inv_diag_u, image_u, s_a, r_a, d_a, i_a, image_a
    )
    return tuple(outs[:3]) + tuple(o[:, None, :] for o in outs[3:])


def solution(mesh):
    herd, nx = mesh.devices.shape
    ny, nc = 4, 2
    grid = Mesh(mesh.devices.reshape(ny, herd // (ny * nc), nc, nx), HERD + ("x",))
    u = P("x", HERD)
    a = P(None, "x", HERD)
    return jax.shard_map(
        body,
        mesh=grid,
        in_specs=(
            u, u, u, u, u, a, a, a, a,
            P(HERD, "x"), P("x"), P("x"), P(), P("x", None), P(HERD), P(HERD),
        ),
        out_specs=(u, u, u, a, a, a),
        check_vma=False,
    )
```

```python
import functools
import math

import jax
import jax.numpy as jnp
import numpy as np
from jax import lax
from jax.experimental import pallas as pl
from jax.experimental.pallas import tpu as pltpu
from jax.sharding import Mesh, PartitionSpec as P

SLOTS = 2
CAP = 64
LIST = CAP - 1
CHUNK = 512
HERD = ("y", "z", "c")
F32 = jnp.float32
BF16 = jnp.bfloat16

NT = (((1,), (1,)), ((), ()))
NN = (((1,), (0,)), ((), ()))


def call(kernel, out, scratch=(), **kw):
    return pl.pallas_call(
        kernel,
        out_shape=out,
        scratch_shapes=list(scratch),
        compiler_params=pltpu.CompilerParams(vmem_limit_bytes=20 * 2**20),
        **kw,
    )


def dot(a, b, dims=NN):
    return lax.dot_general(a, b, dims, preferred_element_type=F32)


def parts(x, n=2):
    out = []
    for _ in range(n):
        p = x.astype(BF16).astype(F32)
        out.append(p)
        x = x - p
    return out


def rows_at(n, cols):
    return lax.broadcasted_iota(jnp.int32, (n, cols), 0)


def weights(sire, dam):
    known = (sire >= 0).astype(jnp.int32) + (dam >= 0).astype(jnp.int32)
    return jnp.where(known == 2, 2.0, jnp.where(known == 1, 4.0 / 3.0, 1.0)).astype(F32)


def place_in(local, known):
    return jnp.where(known, (local >> 7) & 15, -1), ((local >> 11) << 7) + (local & 127)


def one_hot(index, rows):
    return jnp.where(counted(rows, index.shape[1]) == index.astype(F32).astype(BF16), jnp.ones((), BF16), jnp.zeros((), BF16))


def counted(rows, n):
    column = rows_at(rows, 128).astype(F32).astype(BF16)
    return jnp.concatenate([column] * (n // 128), axis=1)


def pick(found, in_group, t):
    rows = in_group.shape[0]
    return jnp.sum(jnp.where(in_group, found[t * rows : (t + 1) * rows], 0.0), axis=0, keepdims=True)


def side_by_side(table):
    return jnp.concatenate([p.astype(BF16) for p in parts(table)], axis=1)


def look_up(table, index, rows):
    hit = one_hot(index, rows)
    return dot(table, jnp.concatenate([hit, hit], axis=0))


def both_halves(acc_ref, first, rows):
    at = slice(first, first + rows)
    return jnp.concatenate([acc_ref[at, :128], acc_ref[at, 128:]], axis=0)


def masked(index, rows, fields):
    here = counted(rows, index.shape[1]) == index.astype(F32).astype(BF16)
    return jnp.concatenate([jnp.where(here, f.astype(BF16), jnp.zeros((), BF16)) for f in fields], axis=0)


def moved(width, pieces, load, rows):
    lane = lax.broadcasted_iota(jnp.int32, (rows, 128), 1)
    for k in range(width // 128):
        tile = jnp.zeros((rows, 128), F32)
        for source, first, at, length in pieces:
            lo, hi = max(at, k * 128), min(at + length, (k + 1) * 128)
            while lo < hi:
                src = first + lo - at
                end = min(hi, lo + 128 - src % 128)
                turn = (lo - src) % 128
                value = load(source, src // 128)
                if turn:
                    value = pltpu.roll(value, turn, 1)
                a, b = lo - k * 128, end - k * 128
                tile = value if (a, b) == (0, 128) else jnp.where((lane >= a) & (lane < b), value, tile)
                lo = end
        yield k, tile


def lists_kernel(dir_ref, dir_a_ref, sire_ref, dam_ref, out_ref, rank_ref, tab_ref, acc_ref, *, shape):
    ny, nz, nc = shape
    traits, animals = dir_ref.shape
    herd = ny * nz * nc
    blocks = animals // 128
    n = CHUNK
    for t in range(traits):
        for b in range(blocks):
            tab_ref[t * blocks + b : t * blocks + b + 1, :] = dir_ref[t : t + 1, b * 128 : (b + 1) * 128]
    before = (rows_at(n, n) < lax.broadcasted_iota(jnp.int32, (n, n), 1)).astype(F32).astype(BF16)
    acc_ref[...] = jnp.zeros(acc_ref.shape, F32)

    def step(k, carry):
        at = pl.ds(pl.multiple_of(k * n, n), n)
        sire = sire_ref[:, at]
        row = owner_row(sire, animals, shape)
        is_owner = rows_at(herd, n) == row
        owners = is_owner.astype(F32).astype(BF16)
        earlier = dot(owners, before) + carry
        rank = jnp.sum(jnp.where(is_owner, earlier, 0.0), axis=0, keepdims=True).astype(jnp.int32)
        rank = jnp.where((sire >= 0) & (rank < LIST), rank, -1)
        rank_ref[:, at] = rank
        local = (sire & (animals - 1)) + 1
        weight = weights(sire, dam_ref[:, at]) * 1.5
        in_row, target = slot_of(rank, row, herd)
        fields = masked(in_row, CAP // 2, [(local & ~63).astype(F32), (local & 63).astype(F32), weight])
        acc_ref[...] += dot(fields, target, NT)
        return earlier[:, n - 1 :] + owners[:, n - 1 :].astype(F32)

    count = lax.fori_loop(0, animals // n, step, jnp.zeros((herd, 1), F32), unroll=True)
    overflow = jnp.where(jnp.max(count, axis=0, keepdims=True) > LIST + 0.5, 1.0, 0.0)
    lane = lax.broadcasted_iota(jnp.int32, (herd, 128), 1)
    ids = slots(acc_ref, 0, herd) + slots(acc_ref, 1, herd)
    block = jnp.concatenate([ids, slots(acc_ref, 2, herd)], axis=0).T
    block = jnp.where(lane == 127, overflow, block)
    out_ref[:, :, :128] = block.reshape(nz, ny * nc, 128)
    rows = ny * nc
    columns = dir_a_ref.shape[1]
    for j in range(dir_a_ref.shape[0] // rows):
        piece = dir_a_ref[j * rows : (j + 1) * rows, :]
        for z in range(nz):
            out_ref[z, :, 128 + j * 128 : 128 + j * 128 + columns] = piece


def slot_of(rank, row, herd):
    short = CAP // 2
    return jnp.where(rank >= 0, rank & (short - 1), -1), one_hot((rank >> (short.bit_length() - 1)) * herd + row, 2 * herd)


def slots(acc_ref, f, herd):
    at = slice(f * (CAP // 2), (f + 1) * (CAP // 2))
    return jnp.concatenate([acc_ref[at, :herd], acc_ref[at, herd:]], axis=0)


def owner_parts(sire, animals, shape):
    _, nz, nc = shape
    owner = sire >> (animals.bit_length() - 1)
    low = nc.bit_length() - 1
    c = owner & (nc - 1)
    z = (owner >> low) & (nz - 1)
    y = owner >> (low + nz.bit_length() - 1)
    return y * nc + c, z


def owner_row(sire, animals, shape):
    g, z = owner_parts(sire, animals, shape)
    return jnp.where(sire >= 0, z * (shape[0] * shape[2]) + g, -1)


def mixed(mix_ref, all_ref, t, blocks):
    total = jnp.zeros((blocks, 128), F32)
    here = all_ref.shape[1] // blocks
    for x in range(all_ref.shape[0]):
        for s in range(here):
            total = total + mix_ref[t, x * here + s] * all_ref[x, s * blocks : (s + 1) * blocks, :]
    return total


def offspring_kernel(mix_ref, all_ref, sire_ref, dam_ref, rank_ref, tab_ref, c_ref, out_ref, acc_ref, *, shape):
    ny, nz, nc = shape
    herd = ny * nz * nc
    traits, animals = c_ref.shape
    blocks = animals // 128
    n = CHUNK
    for t in range(traits):
        tab_ref[t * blocks : (t + 1) * blocks, :] = mixed(mix_ref, all_ref, t, blocks)
    for t in range(traits):
        for b in range(blocks):
            c_ref[t : t + 1, b * 128 : (b + 1) * 128] = tab_ref[t * blocks + b : t * blocks + b + 1, :]
    table = side_by_side(tab_ref[...])
    acc_ref[...] = jnp.zeros(acc_ref.shape, F32)

    def step(k, _):
        at = pl.ds(pl.multiple_of(k * n, n), n)
        sire = sire_ref[:, at]
        dam = dam_ref[:, at]
        weight = weights(sire, dam)
        local = dam & (animals - 1)
        found = look_up(table, local & 127, 128)
        in_block = rows_at(blocks, n) == jnp.where(dam >= 0, local >> 7, -1)
        fields = []
        for t in range(traits):
            value = weight * (c_ref[t : t + 1, at] - 0.5 * pick(found, in_block, t))
            c_ref[t : t + 1, at] = value
            fields += parts(value)
        g, z = owner_parts(sire, animals, shape)
        in_row, target = slot_of(rank_ref[:, at], g * nz + z, herd)
        acc_ref[...] += dot(masked(in_row, CAP // 2, fields), target, NT)
        return 0

    lax.fori_loop(0, animals // n, step, 0, unroll=True)
    lines = [slots(acc_ref, 2 * t, herd) + slots(acc_ref, 2 * t + 1, herd) for t in range(traits)]
    for j in range(traits * CAP // 128):
        block = jnp.concatenate(lines[2 * j : 2 * j + 2], axis=0).T
        out_ref[:, :, j * 128 : (j + 1) * 128] = block.reshape(ny * nc, nz, 128)


def forward_kernel(in_ref, out_ref, *, columns, lists):
    nz, near, _ = in_ref.shape
    ny, traits, _ = out_ref.shape
    cores = near // ny
    for g in range(near):
        at = g % cores * lists
        out_ref[g // cores, :nz, at : at + lists] = in_ref[:, g, :lists]
    pieces = [(z, 0, z * columns, columns) for z in range(nz)]
    for j in range(traits // near):
        first = lists + j * 128
        load = lambda z, _: in_ref[z, :, first : first + 128]
        for k, tile in moved(nz * columns, pieces, load, near):
            at = cores * lists + k * 128
            for y in range(ny):
                out_ref[y, j * near : (j + 1) * near, at : at + 128] = tile


def predict_kernel(
    core_ref, in_ref, geno_ref, freq_ref, gw_ref, out_ref, lists_ref, turned_ref, over_ref,
    joined_ref, wide_ref, *, shape, columns, lists, scale,
):
    ny, nz, nc = shape
    herd = ny * nz * nc
    traits = in_ref.shape[2]
    here = gw_ref.shape[0]
    genotyped = geno_ref.shape[0]
    mine = lax.broadcasted_iota(jnp.int32, (nz, lists), 0) * 0 + core_ref[0]
    for g in range(ny * nc):
        rows = in_ref[g % nc, g // nc, :nz, :lists]
        for c in range(1, nc):
            rows = jnp.where(mine == c, in_ref[g % nc, g // nc, :nz, c * lists : (c + 1) * lists], rows)
        lists_ref[g] = rows
    turned_ref[...] = lists_ref[...].reshape(herd, lists).T
    over_ref[...] = jnp.broadcast_to(jnp.max(turned_ref[127:128, :], keepdims=True), over_ref.shape)
    width = nz * nc * columns
    total = jnp.zeros((3 * traits, genotyped), F32)
    bias = jnp.zeros((traits, 1), F32)
    for y in range(ny):
        pieces = [
            (c, z * columns, (z * nc + c) * columns, columns) for z in range(nz) for c in range(nc)
        ]
        load = lambda c, k: in_ref[c, y, :, nc * lists + k * 128 : nc * lists + (k + 1) * 128]
        for k, tile in moved(width, pieces, load, traits):
            joined_ref[:, k * 128 : (k + 1) * 128] = tile
        at = slice(y * width, (y + 1) * width)
        values = joined_ref[...]
        stack = jnp.concatenate([p.astype(BF16) for p in parts(values, 3)], axis=0)
        total = total + dot(stack, geno_ref[:, at], NT)
        bias = bias + jnp.sum(values * (2.0 * freq_ref[:, at]), axis=1, keepdims=True)
    rows = total[:traits] + total[traits : 2 * traits] + total[2 * traits :]
    wide_ref[...] = jnp.zeros((traits, 128), F32)
    wide_ref[:, :genotyped] = (rows - bias) * scale
    packed = together([wide_ref[x * here : (x + 1) * here, :] for x in range(traits // here)], genotyped)
    for x in range(out_ref.shape[0]):
        out_ref[x, :here, :] = packed
        out_ref[x, here:, :] = gw_ref[...]


def together(groups, width):
    total = groups[0]
    for x in range(1, len(groups)):
        total = total + pltpu.roll(groups[x], x * width, 1)
    return total


def flat(ref, first, group):
    tile = ref[pl.ds(first, group), :]
    return jnp.concatenate([tile[j : j + 1] for j in range(group)], axis=1)


def reply_kernel(
    tab_ref, add_ref, all_ref, pred_ref, ids_ref, geno_ref, freq_ref,
    out_ref, resid_ref, vals_ref, summed_ref, *, shape, columns, scale,
):
    ny, nz, nc = shape
    herd = ny * nz * nc
    nx = all_ref.shape[0]
    traits = resid_ref.shape[0]
    half = tab_ref.shape[0]
    blocks = 32
    here = half // blocks
    genotyped = geno_ref.shape[0]
    table = side_by_side(tab_ref[...])
    group = 8

    def step(k, _):
        r = pl.multiple_of(k * group, group)
        place = flat(ids_ref, r, group).astype(jnp.int32) - 1
        in_block = rows_at(blocks, group * herd) == (place >> 7)
        found = look_up(table, place & 127, 128)
        for t in range(here):
            value = pick(found, in_block, t)
            vals_ref[pl.ds(t * CAP + r, group), :] = jnp.concatenate(
                [value[:, j * herd : (j + 1) * herd] for j in range(group)], axis=0
            )
        return 0

    lax.fori_loop(0, CAP // group, step, 0, unroll=True)
    values = here * CAP
    for j in range(values // 128):
        at = slice(j * 128, (j + 1) * 128)
        out_ref[:, :nz, at] = vals_ref[at, :].T.reshape(ny * nc, nz, 128)
    out_ref[:, :nz, values : 2 * values] = add_ref[...]
    values = 2 * values

    total = pred_ref[0]
    for x in range(1, nx):
        total = total + pred_ref[x]
    lane = lax.broadcasted_iota(jnp.int32, (here, 128), 1)
    own = [
        jnp.concatenate([all_ref[x, s * blocks : s * blocks + 1, :] for s in range(here)], axis=0)
        for x in range(nx)
    ]
    own = together([jnp.where(lane < genotyped, o, 0.0) for o in own], genotyped)
    packed = total[here:] * (own - total[:here])
    for x in range(nx):
        rows = pltpu.roll(packed, 128 - x * genotyped, 1) if x else packed
        resid_ref[x * here : (x + 1) * here, :] = jnp.where(lane < genotyped, rows, 0.0)
    resid = resid_ref[...]
    stack = jnp.concatenate([p.astype(BF16) for p in parts(resid, 3)], axis=0)[:, :genotyped]
    summed = jnp.sum(resid, axis=1, keepdims=True)
    width = nz * nc * columns
    for y in range(ny):
        at = slice(y * width, (y + 1) * width)
        found = dot(stack, geno_ref[:, at])
        found = found[:traits] + found[traits : 2 * traits] + found[2 * traits :]
        summed_ref[...] = (found - summed * (2.0 * freq_ref[:, at])) * scale
        for c in range(nc):
            pieces = [(0, (z * nc + c) * columns, z * columns, columns) for z in range(nz)]
            load = lambda _, k: summed_ref[:, k * 128 : (k + 1) * 128]
            for k, tile in moved(nz * columns, pieces, load, traits):
                out_ref[y * nc + c, :, values + k * 128 : values + (k + 1) * 128] = tile


def backward_kernel(in_ref, out_ref, *, columns, values):
    nz, near, _ = out_ref.shape
    traits = in_ref.shape[1]
    for g in range(near):
        out_ref[:, g, :values] = in_ref[g, :nz, :values]
    total = in_ref[0, :, values:]
    for g in range(1, near):
        total = total + in_ref[g, :, values:]
    load = lambda _, k: total[:, k * 128 : (k + 1) * 128]
    for z in range(nz):
        for _, tile in moved(128, [(0, z * columns, 0, columns)], load, traits):
            for j in range(traits // near):
                first = values + j * 128
                out_ref[z, :, first : first + 128] = tile[j * near : (j + 1) * near]


def order_kernel(in_ref, out_ref, swapped_ref):
    near, nz, lists = in_ref.shape
    for g in range(near):
        swapped_ref[:, g, :] = in_ref[g]
    out_ref[...] = swapped_ref[...].reshape(near * nz, lists).T


def image_kernel(
    got_ref, c_ref, rank_ref, sire_ref, dam_ref, lists_ref, mixed_ref, resid_ref,
    dir_ref, rec_ref, res_ref, inv_ref, ridge_ref, dir_a_ref, res_a_ref, inv_a_ref,
    image_ref, image_a_ref, sums_ref, acc_ref, tab_ref, turned_ref, weight_ref, *, shape,
):
    traits, animals = c_ref.shape
    ny, nz, nc = shape
    herd, near = ny * nz * nc, ny * nc
    blocks = animals // 128
    n = CHUNK
    short = blocks // 2
    wide = traits * CAP
    table = side_by_side(got_ref[:, :, :wide].reshape(herd, wide).T)
    for j in range(wide // 128):
        first = wide + j * 128
        turned_ref[j * 128 : (j + 1) * 128, :] = got_ref[:, :, first : first + 128].reshape(herd, 128).T
    acc_ref[...] = jnp.zeros(acc_ref.shape, F32)
    weight_ref[...] = jnp.zeros(weight_ref.shape, F32)
    group = 8

    def add(k, _):
        r = pl.multiple_of(k * group, group)
        place = flat(lists_ref, r, group).astype(jnp.int32) - 1
        row, column = place_in(place, place >= 0)
        fields = []
        for t in range(traits):
            fields += parts(flat(turned_ref, t * CAP + r, group))
        fields = masked(row, short, fields + [flat(lists_ref, CAP + r, group)])
        sums = dot(fields, one_hot(column, 256), NT)
        acc_ref[...] += sums[: 2 * traits * short]
        weight_ref[...] += sums[2 * traits * short :]
        return 0

    lax.fori_loop(0, CAP // group, add, 0, unroll=True)

    def step(k, _):
        at = pl.ds(pl.multiple_of(k * n, n), n)
        sire = sire_ref[:, at]
        dam = dam_ref[:, at]
        weight = weights(sire, dam)
        found = look_up(table, owner_row(sire, animals, shape), herd)
        in_slot = rows_at(CAP, n) == rank_ref[:, at]
        row, column = place_in(dam & (animals - 1), dam >= 0)
        fields = []
        for t in range(traits):
            scaled = c_ref[t : t + 1, at] - 0.5 * weight * pick(found, in_slot, t)
            image_ref[t : t + 1, at] = scaled
            fields += parts(scaled)
        acc_ref[...] += dot(masked(row, short, fields), one_hot(column, 256), NT)
        return 0

    lax.fori_loop(0, animals // n, step, 0, unroll=True)
    for t in range(traits):
        at = slice(t * blocks, (t + 1) * blocks)
        first = 2 * t * short
        down = both_halves(acc_ref, first, short) + both_halves(acc_ref, first + short, short)
        tab_ref[at, :] = (0.25 / 1.5) * both_halves(weight_ref, 0, short) * mixed_ref[at, :] - 0.5 * down
    for b in range(blocks):
        for t in range(traits):
            at = (slice(t, t + 1), slice(b * 128, (b + 1) * 128))
            image_ref[at] = image_ref[at] + tab_ref[t * blocks + b : t * blocks + b + 1, :]
    image_ref[:, :128] = image_ref[:, :128] + resid_ref[...]
    direction = dir_ref[...]
    image = image_ref[...] + rec_ref[...] * direction
    image_ref[...] = image
    res = res_ref[...]
    inv = inv_ref[...]
    columns = dir_a_ref.shape[1]
    sums = jnp.sum(got_ref[:, :, 2 * wide :], axis=0)
    tiles = sums.shape[1] // 128
    back = jnp.concatenate([sums[:, j * 128 : (j + 1) * 128] for j in range(tiles)], axis=0)[:, :columns]
    dir_a = dir_a_ref[...]
    image_a = ridge_ref[...] * dir_a - back
    image_a_ref[...] = image_a
    res_a = res_a_ref[...]
    inv_a = inv_a_ref[...]
    weighted, weighted_a = inv * res, inv_a * res_a
    lane = lax.broadcasted_iota(jnp.int32, (1, 128), 1)
    pairs = (
        (weighted * res, weighted_a * res_a),
        (direction * image, dir_a * image_a),
        (weighted * image, weighted_a * image_a),
        (inv * image * image, inv_a * image_a * image_a),
    )
    total = jnp.zeros((1, 128), F32)
    for j, (one, two) in enumerate(pairs):
        value = jnp.sum(one, keepdims=True) + jnp.sum(two, keepdims=True)
        total = jnp.where(lane == j, value, total)
    sums_ref[...] = total


def update_kernel(
    sums_ref, sol_ref, res_ref, dir_ref, inv_ref, image_ref,
    sol_a_ref, res_a_ref, dir_a_ref, inv_a_ref, image_a_ref,
    nsol_ref, nres_ref, ndir_ref, nsol_a_ref, nres_a_ref, ndir_a_ref,
):
    total = jnp.sum(sums_ref[...], axis=0)
    norm, curve, cross, square = (total[:, j : j + 1] for j in range(4))
    size = norm / curve
    following = norm - 2.0 * size * cross + size * size * square
    ratio = following / norm
    for sol, res, dire, inv, image, nsol, nres, ndir in (
        (sol_ref, res_ref, dir_ref, inv_ref, image_ref, nsol_ref, nres_ref, ndir_ref),
        (sol_a_ref, res_a_ref, dir_a_ref, inv_a_ref, image_a_ref, nsol_a_ref, nres_a_ref, ndir_a_ref),
    ):
        d = dire[...]
        nsol[...] = sol[...] + size * d
        left = res[...] - size * image[...]
        nres[...] = left
        ndir[...] = inv[...] * left + ratio * d


def pedigree_by_blocks(field, sire, dam, herd_count, herd_index):
    traits_here, animals = field.shape
    block_count = animals // 128
    span = SLOTS * 128
    has_sire = sire >= 0
    has_dam = dam >= 0
    sire_known = has_sire.astype(F32)
    dam_known = has_dam.astype(F32)
    owner_herd = jnp.where(has_sire, sire // animals, 0)
    block_index = jnp.where(has_sire, sire % animals // 128, 0)
    offset = jnp.where(has_sire, sire % 128, 0)
    flat_block = jnp.where(
        has_sire, owner_herd * block_count + block_index, herd_count * block_count
    )
    present = jnp.zeros((herd_count * block_count + 1,), jnp.int32).at[flat_block].max(1)
    present = present[:-1].reshape(herd_count, block_count)
    slot_order = jnp.cumsum(present, axis=1) - 1
    slot_range = jnp.arange(SLOTS, dtype=jnp.int32)
    slot_match = (present[:, :, None] == 1) & (slot_order[:, :, None] == slot_range[None, None, :])
    block_ids = jnp.arange(block_count, dtype=jnp.int32)[None, :, None] + 1
    wanted = jnp.sum(jnp.where(slot_match, block_ids, 0), axis=1) - 1
    requests = lax.all_to_all(wanted, HERD, split_axis=0, concat_axis=0, tiled=True)
    live_slot = requests >= 0
    field_tiles = field.reshape(traits_here, block_count, 128)
    outgoing = field_tiles[:, jnp.where(live_slot, requests, 0), :]
    outgoing = jnp.where(live_slot[None, :, :, None], outgoing, 0.0).reshape(
        traits_here, herd_count, span
    )
    fetched = lax.all_to_all(outgoing, HERD, split_axis=1, concat_axis=1, tiled=True).reshape(
        traits_here, herd_count * span
    )
    slot_index = slot_order[owner_herd, block_index]
    buffer_place = owner_herd * span + slot_index * 128 + offset
    sire_values = fetched[:, jnp.where(has_sire, buffer_place, 0)]
    local_dam = jnp.where(has_dam, dam - herd_index * animals, 0)
    dam_values = field[:, local_dam]
    weight = 4.0 / (4.0 - sire_known - dam_known)
    scaled = weight * (field - 0.5 * sire_known * sire_values - 0.5 * dam_known * dam_values)
    dam_target = jnp.where(has_dam, local_dam, animals)
    dam_terms = (
        jnp.zeros((traits_here, animals + 1), F32).at[:, dam_target].add(-0.5 * dam_known * scaled)
    )
    result = scaled + dam_terms[:, :animals]
    sire_target = jnp.where(has_sire, buffer_place, herd_count * span)
    outbound = (
        jnp.zeros((traits_here, herd_count * span + 1), F32)
        .at[:, sire_target]
        .add(-0.5 * sire_known * scaled)
    )
    outbound = outbound[:, :-1].reshape(traits_here, herd_count, span)
    returned = lax.all_to_all(outbound, HERD, split_axis=1, concat_axis=1, tiled=True).reshape(
        traits_here, herd_count * SLOTS, 128
    )
    block_target = jnp.where(live_slot, requests, block_count).reshape(herd_count * SLOTS)
    incoming = (
        jnp.zeros((traits_here, block_count + 1, 128), F32).at[:, block_target, :].add(returned)
    )
    return result + incoming[:, :block_count, :].reshape(traits_here, animals)


def body(
    sol_u, res_u, dir_u, rec_weight, inv_diag_u, sol_a, res_a, dir_a, inv_diag_a,
    genotypes, allele_freq, geno_weight, snp_ridge, genetic_inv, sire, dam,
):
    shape = ny, nz, nc = tuple(lax.axis_size(a) for a in HERD)
    nx = lax.axis_size("x")
    herd, near = ny * nz * nc, ny * nc
    x_index = lax.axis_index("x")
    here, animals = dir_u.shape
    traits, _, columns = dir_a.shape
    genotyped, snps = genotypes.shape
    blocks = animals // 128
    half = here * blocks
    lists, values = 2 * CAP, here * CAP
    spare = traits // near * 128
    scale = 2.0 / math.sqrt(snps * nx)
    sds = lambda *s: jax.ShapeDtypeStruct(s, F32)
    vmem = lambda *s: pltpu.VMEM(s, F32)
    d_a, r_a, s_a, i_a = (a[:, 0, :] for a in (dir_a, res_a, sol_a, inv_diag_a))
    freq = allele_freq[None, :]
    sire_row, dam_row = sire[None, :], dam[None, :]
    mine = jnp.arange(128) // genotyped == x_index
    weight_here = jnp.where(mine[None, :], geno_weight[:, None], 0.0)

    out_z, rank, table = call(
        functools.partial(lists_kernel, shape=shape),
        (sds(nz, near, lists + spare), jax.ShapeDtypeStruct((1, animals), jnp.int32), sds(half, 128)),
        scratch=[vmem(3 * CAP // 2, 2 * herd)],
    )(dir_u, d_a, sire_row, dam_row)
    in_z = lax.all_to_all(out_z, "z", 0, 0, tiled=True)
    all_tables = lax.all_gather(table, "x", axis=0)
    in_z, all_tables = lax.optimization_barrier((in_z, all_tables))
    out_near = call(
        functools.partial(forward_kernel, columns=columns, lists=lists),
        sds(ny, traits, nc * lists + nz * columns),
    )(in_z)
    out_near, all_tables = lax.optimization_barrier((out_near, all_tables))
    in_y = lax.all_to_all(out_near, "y", 0, 0, tiled=True)

    on_chip = pl.BlockSpec(memory_space=pltpu.VMEM)
    scalars = pl.BlockSpec(memory_space=pltpu.SMEM)
    mixed_table, c_term, add = call(
        functools.partial(offspring_kernel, shape=shape),
        (sds(half, 128), sds(here, animals), sds(near, nz, values)),
        scratch=[vmem(here * CAP, 2 * herd)],
        in_specs=[scalars] + [on_chip] * 4,
    )(genetic_inv, all_tables, sire_row, dam_row, rank)
    in_y, mixed_table, c_term, add = lax.optimization_barrier((in_y, mixed_table, c_term, add))
    in_near = lax.all_gather(in_y, "c", axis=0)

    to_x, asked, turned, over = call(
        functools.partial(predict_kernel, shape=shape, columns=columns, lists=lists, scale=scale),
        (sds(nx, 2 * here, 128), sds(near, nz, lists), sds(lists, herd), sds(8, 128)),
        scratch=[vmem(traits, nz * nc * columns), vmem(traits, 128)],
        in_specs=[scalars] + [on_chip] * 4,
    )(lax.axis_index("c").reshape(1), in_near, genotypes, freq, weight_here)
    from_x = lax.all_to_all(to_x, "x", 0, 0, tiled=True)

    back_near, resid = call(
        functools.partial(reply_kernel, shape=shape, columns=columns, scale=scale),
        (sds(near, traits, 2 * values + nz * columns), sds(traits, 128)),
        scratch=[vmem(values, herd), vmem(traits, nz * nc * columns)],
    )(mixed_table, add, all_tables, from_x, turned, genotypes, freq)
    got_near = lax.all_to_all(back_near, ("y", "c"), 0, 0, tiled=True)
    back_z = call(
        functools.partial(backward_kernel, columns=columns, values=2 * values),
        sds(nz, near, 2 * values + spare),
    )(got_near)
    back_z, asked = lax.optimization_barrier((back_z, asked))
    got_z = lax.all_to_all(back_z, "z", 0, 0, tiled=True)
    ordered = call(order_kernel, sds(lists, herd), scratch=[vmem(nz, near, lists)])(asked)
    too_long = over[0, 0] > 0.5
    got_z, ordered, too_long = lax.optimization_barrier((got_z, ordered, too_long))

    own_resid = lax.dynamic_slice_in_dim(resid, x_index * here, here, 0)
    image_u, image_a, sums = call(
        functools.partial(image_kernel, shape=shape),
        (sds(here, animals), sds(traits, columns), sds(1, 128)),
        scratch=[vmem(here * blocks, 256), vmem(half, 128), vmem(values, herd), vmem(blocks // 2, 256)],
    )(
        got_z, c_term, rank, sire_row, dam_row, ordered, mixed_table, own_resid,
        dir_u, rec_weight, res_u, inv_diag_u, snp_ridge[:, None], d_a, r_a, i_a,
    )

    u, a = sds(here, animals), sds(traits, columns)

    def reduced(sums):
        close = lax.all_to_all(
            jnp.broadcast_to(sums[None], (near * nx, 1, 128)), ("y", "c", "x"), 0, 0, tiled=True
        )
        close = jnp.sum(close, axis=0, keepdims=True)
        return lax.all_to_all(jnp.broadcast_to(close, (nz, 1, 128)), "z", 0, 0, tiled=True)

    def finish(image, far):
        return tuple(
            call(update_kernel, (u, u, u, a, a, a))(
                far, sol_u, res_u, dir_u, inv_diag_u, image, s_a, r_a, d_a, i_a, image_a
            )
        )

    def by_blocks(_):
        dir_all = all_tables.reshape(traits, animals)
        mixed = jnp.dot(genetic_inv, dir_all, precision=lax.Precision.HIGHEST)
        image = rec_weight * dir_u + pedigree_by_blocks(mixed, sire, dam, herd, lax.axis_index(HERD))
        image = image.at[:, :genotyped].add(own_resid[:, :genotyped])
        cells = [
            jnp.sum(inv_diag_u * res_u * res_u) + jnp.sum(i_a * r_a * r_a),
            jnp.sum(dir_u * image) + jnp.sum(d_a * image_a),
            jnp.sum(inv_diag_u * res_u * image) + jnp.sum(i_a * r_a * image_a),
            jnp.sum(inv_diag_u * image * image) + jnp.sum(i_a * image_a * image_a),
        ]
        return finish(image, reduced(jnp.pad(jnp.stack(cells), (0, 124))[None, :]))

    far, too_long = lax.optimization_barrier((reduced(sums), too_long))
    outs = finish(image_u, far)
    outs = lax.cond(too_long, by_blocks, lambda done: done, outs)
    return outs[:3] + tuple(o[:, None, :] for o in outs[3:])


def solution(mesh):
    herd, nx = mesh.devices.shape
    ny, nc = 4, 2
    grid = Mesh(mesh.devices.reshape(ny, herd // (ny * nc), nc, nx), HERD + ("x",))
    u = P("x", HERD)
    a = P(None, "x", HERD)
    return jax.shard_map(
        body,
        mesh=grid,
        in_specs=(
            u, u, u, u, u, a, a, a, a,
            P(HERD, "x"), P("x"), P("x"), P(), P("x", None), P(HERD), P(HERD),
        ),
        out_specs=(u, u, u, a, a, a),
        check_vma=False,
    )
```

```python
import functools
import math

import jax
import jax.numpy as jnp
import numpy as np
from jax import lax
from jax.experimental import pallas as pl
from jax.experimental.pallas import tpu as pltpu
from jax.sharding import Mesh, PartitionSpec as P

SLOTS = 2
CAP = 64
LIST = CAP - 1
CHUNK = 512
HERD = ("y", "z", "c")
F32 = jnp.float32
BF16 = jnp.bfloat16

NT = (((1,), (1,)), ((), ()))
NN = (((1,), (0,)), ((), ()))


def call(kernel, out, scratch=(), **kw):
    return pl.pallas_call(
        kernel,
        out_shape=out,
        scratch_shapes=list(scratch),
        compiler_params=pltpu.CompilerParams(vmem_limit_bytes=20 * 2**20),
        **kw,
    )


def dot(a, b, dims=NN):
    return lax.dot_general(a, b, dims, preferred_element_type=F32)


def parts(x, n=2):
    out = []
    for _ in range(n):
        p = x.astype(BF16).astype(F32)
        out.append(p)
        x = x - p
    return out


def rows_at(n, cols):
    return lax.broadcasted_iota(jnp.int32, (n, cols), 0)


def weights(sire, dam):
    known = (sire >= 0).astype(jnp.int32) + (dam >= 0).astype(jnp.int32)
    return jnp.where(known == 2, 2.0, jnp.where(known == 1, 4.0 / 3.0, 1.0)).astype(F32)


def place_in(local, known):
    return jnp.where(known, (local >> 7) & 15, -1), ((local >> 11) << 7) + (local & 127)


def one_hot(index, rows):
    return jnp.where(counted(rows, index.shape[1]) == index.astype(F32).astype(BF16), jnp.ones((), BF16), jnp.zeros((), BF16))


def counted(rows, n):
    column = rows_at(rows, 128).astype(F32).astype(BF16)
    return jnp.concatenate([column] * (n // 128), axis=1)


def pick(found, in_group, t):
    rows = in_group.shape[0]
    return jnp.sum(jnp.where(in_group, found[t * rows : (t + 1) * rows], 0.0), axis=0, keepdims=True)


def side_by_side(table):
    return jnp.concatenate([p.astype(BF16) for p in parts(table)], axis=1)


def look_up(table, index, rows):
    hit = one_hot(index, rows)
    return dot(table, jnp.concatenate([hit, hit], axis=0))


def both_halves(acc_ref, first, rows):
    at = slice(first, first + rows)
    return jnp.concatenate([acc_ref[at, :128], acc_ref[at, 128:]], axis=0)


def masked(index, rows, fields):
    here = counted(rows, index.shape[1]) == index.astype(F32).astype(BF16)
    return jnp.concatenate([jnp.where(here, f.astype(BF16), jnp.zeros((), BF16)) for f in fields], axis=0)


def moved(width, pieces, load, rows):
    lane = lax.broadcasted_iota(jnp.int32, (rows, 128), 1)
    for k in range(width // 128):
        tile = jnp.zeros((rows, 128), F32)
        for source, first, at, length in pieces:
            lo, hi = max(at, k * 128), min(at + length, (k + 1) * 128)
            while lo < hi:
                src = first + lo - at
                end = min(hi, lo + 128 - src % 128)
                turn = (lo - src) % 128
                value = load(source, src // 128)
                if turn:
                    value = pltpu.roll(value, turn, 1)
                a, b = lo - k * 128, end - k * 128
                tile = value if (a, b) == (0, 128) else jnp.where((lane >= a) & (lane < b), value, tile)
                lo = end
        yield k, tile


def lists_kernel(dir_ref, dir_a_ref, sire_ref, dam_ref, out_ref, rank_ref, tab_ref, acc_ref, *, shape):
    ny, nz, nc = shape
    traits, animals = dir_ref.shape
    herd = ny * nz * nc
    blocks = animals // 128
    n = CHUNK
    for t in range(traits):
        for b in range(blocks):
            tab_ref[t * blocks + b : t * blocks + b + 1, :] = dir_ref[t : t + 1, b * 128 : (b + 1) * 128]
    before = (rows_at(n, n) < lax.broadcasted_iota(jnp.int32, (n, n), 1)).astype(F32).astype(BF16)
    acc_ref[...] = jnp.zeros(acc_ref.shape, F32)

    def step(k, carry):
        at = pl.ds(pl.multiple_of(k * n, n), n)
        sire = sire_ref[:, at]
        row = owner_row(sire, animals, shape)
        is_owner = rows_at(herd, n) == row
        owners = is_owner.astype(F32).astype(BF16)
        earlier = dot(owners, before) + carry
        rank = jnp.sum(jnp.where(is_owner, earlier, 0.0), axis=0, keepdims=True).astype(jnp.int32)
        rank = jnp.where((sire >= 0) & (rank < LIST), rank, -1)
        rank_ref[:, at] = rank
        local = (sire & (animals - 1)) + 1
        weight = weights(sire, dam_ref[:, at]) * 1.5
        in_row, target = slot_of(rank, row, herd)
        fields = masked(in_row, CAP // 2, [(local & ~63).astype(F32), (local & 63).astype(F32), weight])
        acc_ref[...] += dot(fields, target, NT)
        return earlier[:, n - 1 :] + owners[:, n - 1 :].astype(F32)

    count = lax.fori_loop(0, animals // n, step, jnp.zeros((herd, 1), F32), unroll=True)
    overflow = jnp.where(jnp.max(count, axis=0, keepdims=True) > LIST + 0.5, 1.0, 0.0)
    lane = lax.broadcasted_iota(jnp.int32, (herd, 128), 1)
    ids = slots(acc_ref, 0, herd) + slots(acc_ref, 1, herd)
    block = jnp.concatenate([ids, slots(acc_ref, 2, herd)], axis=0).T
    block = jnp.where(lane == 127, overflow, block)
    out_ref[:, :, :128] = block.reshape(nz, ny * nc, 128)
    rows = ny * nc
    columns = dir_a_ref.shape[1]
    for j in range(dir_a_ref.shape[0] // rows):
        piece = dir_a_ref[j * rows : (j + 1) * rows, :]
        for z in range(nz):
            out_ref[z, :, 128 + j * 128 : 128 + j * 128 + columns] = piece


def slot_of(rank, row, herd):
    short = CAP // 2
    return jnp.where(rank >= 0, rank & (short - 1), -1), one_hot((rank >> (short.bit_length() - 1)) * herd + row, 2 * herd)


def slots(acc_ref, f, herd):
    at = slice(f * (CAP // 2), (f + 1) * (CAP // 2))
    return jnp.concatenate([acc_ref[at, :herd], acc_ref[at, herd:]], axis=0)


def owner_parts(sire, animals, shape):
    _, nz, nc = shape
    owner = sire >> (animals.bit_length() - 1)
    low = nc.bit_length() - 1
    c = owner & (nc - 1)
    z = (owner >> low) & (nz - 1)
    y = owner >> (low + nz.bit_length() - 1)
    return y * nc + c, z


def owner_row(sire, animals, shape):
    g, z = owner_parts(sire, animals, shape)
    return jnp.where(sire >= 0, z * (shape[0] * shape[2]) + g, -1)


def mixed(mix_ref, all_ref, t, blocks):
    total = jnp.zeros((blocks, 128), F32)
    here = all_ref.shape[1] // blocks
    for x in range(all_ref.shape[0]):
        for s in range(here):
            total = total + mix_ref[t, x * here + s] * all_ref[x, s * blocks : (s + 1) * blocks, :]
    return total


def offspring_kernel(mix_ref, all_ref, sire_ref, dam_ref, rank_ref, tab_ref, c_ref, out_ref, acc_ref, *, shape):
    ny, nz, nc = shape
    herd = ny * nz * nc
    traits, animals = c_ref.shape
    blocks = animals // 128
    n = CHUNK
    for t in range(traits):
        tab_ref[t * blocks : (t + 1) * blocks, :] = mixed(mix_ref, all_ref, t, blocks)
    for t in range(traits):
        for b in range(blocks):
            c_ref[t : t + 1, b * 128 : (b + 1) * 128] = tab_ref[t * blocks + b : t * blocks + b + 1, :]
    table = side_by_side(tab_ref[...])
    acc_ref[...] = jnp.zeros(acc_ref.shape, F32)

    def step(k, _):
        at = pl.ds(pl.multiple_of(k * n, n), n)
        sire = sire_ref[:, at]
        dam = dam_ref[:, at]
        weight = weights(sire, dam)
        local = dam & (animals - 1)
        found = look_up(table, local & 127, 128)
        in_block = rows_at(blocks, n) == jnp.where(dam >= 0, local >> 7, -1)
        fields = []
        for t in range(traits):
            value = weight * (c_ref[t : t + 1, at] - 0.5 * pick(found, in_block, t))
            c_ref[t : t + 1, at] = value
            fields += parts(value)
        g, z = owner_parts(sire, animals, shape)
        in_row, target = slot_of(rank_ref[:, at], g * nz + z, herd)
        acc_ref[...] += dot(masked(in_row, CAP // 2, fields), target, NT)
        return 0

    lax.fori_loop(0, animals // n, step, 0, unroll=True)
    lines = [slots(acc_ref, 2 * t, herd) + slots(acc_ref, 2 * t + 1, herd) for t in range(traits)]
    for j in range(traits * CAP // 128):
        block = jnp.concatenate(lines[2 * j : 2 * j + 2], axis=0).T
        out_ref[:, :, j * 128 : (j + 1) * 128] = block.reshape(ny * nc, nz, 128)


def forward_kernel(in_ref, out_ref, *, columns, lists):
    nz, near, _ = in_ref.shape
    ny, traits, _ = out_ref.shape
    cores = near // ny
    for g in range(near):
        at = g % cores * lists
        out_ref[g // cores, :nz, at : at + lists] = in_ref[:, g, :lists]
    pieces = [(z, 0, z * columns, columns) for z in range(nz)]
    for j in range(traits // near):
        first = lists + j * 128
        load = lambda z, _: in_ref[z, :, first : first + 128]
        for k, tile in moved(nz * columns, pieces, load, near):
            at = cores * lists + k * 128
            for y in range(ny):
                out_ref[y, j * near : (j + 1) * near, at : at + 128] = tile


def predict_kernel(
    core_ref, in_ref, geno_ref, freq_ref, gw_ref, out_ref, lists_ref, turned_ref, over_ref,
    joined_ref, wide_ref, *, shape, columns, lists, scale,
):
    ny, nz, nc = shape
    herd = ny * nz * nc
    traits = in_ref.shape[2]
    here = gw_ref.shape[0]
    genotyped = geno_ref.shape[0]
    mine = lax.broadcasted_iota(jnp.int32, (nz, lists), 0) * 0 + core_ref[0]
    for g in range(ny * nc):
        rows = in_ref[g % nc, g // nc, :nz, :lists]
        for c in range(1, nc):
            rows = jnp.where(mine == c, in_ref[g % nc, g // nc, :nz, c * lists : (c + 1) * lists], rows)
        lists_ref[g] = rows
    turned_ref[...] = lists_ref[...].reshape(herd, lists).T
    over_ref[...] = jnp.broadcast_to(jnp.max(turned_ref[127:128, :], keepdims=True), over_ref.shape)
    width = nz * nc * columns
    total = jnp.zeros((3 * traits, genotyped), F32)
    bias = jnp.zeros((traits, 1), F32)
    for y in range(ny):
        pieces = [
            (c, z * columns, (z * nc + c) * columns, columns) for z in range(nz) for c in range(nc)
        ]
        load = lambda c, k: in_ref[c, y, :, nc * lists + k * 128 : nc * lists + (k + 1) * 128]
        for k, tile in moved(width, pieces, load, traits):
            joined_ref[:, k * 128 : (k + 1) * 128] = tile
        at = slice(y * width, (y + 1) * width)
        values = joined_ref[...]
        stack = jnp.concatenate([p.astype(BF16) for p in parts(values, 3)], axis=0)
        total = total + dot(stack, geno_ref[:, at], NT)
        bias = bias + jnp.sum(values * (2.0 * freq_ref[:, at]), axis=1, keepdims=True)
    rows = total[:traits] + total[traits : 2 * traits] + total[2 * traits :]
    wide_ref[...] = jnp.zeros((traits, 128), F32)
    wide_ref[:, :genotyped] = (rows - bias) * scale
    packed = together([wide_ref[x * here : (x + 1) * here, :] for x in range(traits // here)], genotyped)
    for x in range(out_ref.shape[0]):
        out_ref[x, :here, :] = packed
        out_ref[x, here:, :] = gw_ref[...]


def together(groups, width):
    total = groups[0]
    for x in range(1, len(groups)):
        total = total + pltpu.roll(groups[x], x * width, 1)
    return total


def flat(ref, first, group):
    tile = ref[pl.ds(first, group), :]
    return jnp.concatenate([tile[j : j + 1] for j in range(group)], axis=1)


def reply_kernel(
    tab_ref, add_ref, all_ref, pred_ref, ids_ref, geno_ref, freq_ref,
    out_ref, resid_ref, vals_ref, summed_ref, *, shape, columns, scale,
):
    ny, nz, nc = shape
    herd = ny * nz * nc
    nx = all_ref.shape[0]
    traits = resid_ref.shape[0]
    half = tab_ref.shape[0]
    blocks = 32
    here = half // blocks
    genotyped = geno_ref.shape[0]
    table = side_by_side(tab_ref[...])
    group = 8

    def step(k, _):
        r = pl.multiple_of(k * group, group)
        place = flat(ids_ref, r, group).astype(jnp.int32) - 1
        in_block = rows_at(blocks, group * herd) == (place >> 7)
        found = look_up(table, place & 127, 128)
        for t in range(here):
            value = pick(found, in_block, t)
            vals_ref[pl.ds(t * CAP + r, group), :] = jnp.concatenate(
                [value[:, j * herd : (j + 1) * herd] for j in range(group)], axis=0
            )
        return 0

    lax.fori_loop(0, CAP // group, step, 0, unroll=True)
    values = here * CAP
    for j in range(values // 128):
        at = slice(j * 128, (j + 1) * 128)
        out_ref[:, :nz, at] = vals_ref[at, :].T.reshape(ny * nc, nz, 128)
    out_ref[:, :nz, values : 2 * values] = add_ref[...]
    values = 2 * values

    total = pred_ref[0]
    for x in range(1, nx):
        total = total + pred_ref[x]
    lane = lax.broadcasted_iota(jnp.int32, (here, 128), 1)
    own = [
        jnp.concatenate([all_ref[x, s * blocks : s * blocks + 1, :] for s in range(here)], axis=0)
        for x in range(nx)
    ]
    own = together([jnp.where(lane < genotyped, o, 0.0) for o in own], genotyped)
    packed = total[here:] * (own - total[:here])
    for x in range(nx):
        rows = pltpu.roll(packed, 128 - x * genotyped, 1) if x else packed
        resid_ref[x * here : (x + 1) * here, :] = jnp.where(lane < genotyped, rows, 0.0)
    resid = resid_ref[...]
    stack = jnp.concatenate([p.astype(BF16) for p in parts(resid, 3)], axis=0)[:, :genotyped]
    summed = jnp.sum(resid, axis=1, keepdims=True)
    width = nz * nc * columns
    for y in range(ny):
        at = slice(y * width, (y + 1) * width)
        found = dot(stack, geno_ref[:, at])
        found = found[:traits] + found[traits : 2 * traits] + found[2 * traits :]
        summed_ref[...] = (found - summed * (2.0 * freq_ref[:, at])) * scale
        for c in range(nc):
            pieces = [(0, (z * nc + c) * columns, z * columns, columns) for z in range(nz)]
            load = lambda _, k: summed_ref[:, k * 128 : (k + 1) * 128]
            for k, tile in moved(nz * columns, pieces, load, traits):
                out_ref[y * nc + c, :, values + k * 128 : values + (k + 1) * 128] = tile


def backward_kernel(in_ref, out_ref, *, columns, values):
    nz, near, _ = out_ref.shape
    traits = in_ref.shape[1]
    for g in range(near):
        out_ref[:, g, :values] = in_ref[g, :nz, :values]
    total = in_ref[0, :, values:]
    for g in range(1, near):
        total = total + in_ref[g, :, values:]
    load = lambda _, k: total[:, k * 128 : (k + 1) * 128]
    for z in range(nz):
        for _, tile in moved(128, [(0, z * columns, 0, columns)], load, traits):
            for j in range(traits // near):
                first = values + j * 128
                out_ref[z, :, first : first + 128] = tile[j * near : (j + 1) * near]


def order_kernel(in_ref, out_ref, swapped_ref):
    near, nz, lists = in_ref.shape
    for g in range(near):
        swapped_ref[:, g, :] = in_ref[g]
    out_ref[...] = swapped_ref[...].reshape(near * nz, lists).T


def image_kernel(
    got_ref, c_ref, rank_ref, sire_ref, dam_ref, lists_ref, mixed_ref, resid_ref,
    dir_ref, rec_ref, res_ref, inv_ref, ridge_ref, dir_a_ref, res_a_ref, inv_a_ref,
    image_ref, image_a_ref, sums_ref, acc_ref, tab_ref, turned_ref, weight_ref, *, shape,
):
    traits, animals = c_ref.shape
    ny, nz, nc = shape
    herd, near = ny * nz * nc, ny * nc
    blocks = animals // 128
    n = CHUNK
    short = blocks // 2
    wide = traits * CAP
    table = side_by_side(got_ref[:, :, :wide].reshape(herd, wide).T)
    for j in range(wide // 128):
        first = wide + j * 128
        turned_ref[j * 128 : (j + 1) * 128, :] = got_ref[:, :, first : first + 128].reshape(herd, 128).T
    acc_ref[...] = jnp.zeros(acc_ref.shape, F32)
    weight_ref[...] = jnp.zeros(weight_ref.shape, F32)
    group = 8

    def add(k, _):
        r = pl.multiple_of(k * group, group)
        place = flat(lists_ref, r, group).astype(jnp.int32) - 1
        row, column = place_in(place, place >= 0)
        fields = []
        for t in range(traits):
            fields += parts(flat(turned_ref, t * CAP + r, group))
        fields = masked(row, short, fields + [flat(lists_ref, CAP + r, group)])
        sums = dot(fields, one_hot(column, 256), NT)
        acc_ref[...] += sums[: 2 * traits * short]
        weight_ref[...] += sums[2 * traits * short :]
        return 0

    lax.fori_loop(0, CAP // group, add, 0, unroll=True)

    def step(k, _):
        at = pl.ds(pl.multiple_of(k * n, n), n)
        sire = sire_ref[:, at]
        dam = dam_ref[:, at]
        weight = weights(sire, dam)
        found = look_up(table, owner_row(sire, animals, shape), herd)
        in_slot = rows_at(CAP, n) == rank_ref[:, at]
        row, column = place_in(dam & (animals - 1), dam >= 0)
        fields = []
        for t in range(traits):
            scaled = c_ref[t : t + 1, at] - 0.5 * weight * pick(found, in_slot, t)
            image_ref[t : t + 1, at] = scaled
            fields += parts(scaled)
        acc_ref[...] += dot(masked(row, short, fields), one_hot(column, 256), NT)
        return 0

    lax.fori_loop(0, animals // n, step, 0, unroll=True)
    for t in range(traits):
        at = slice(t * blocks, (t + 1) * blocks)
        first = 2 * t * short
        down = both_halves(acc_ref, first, short) + both_halves(acc_ref, first + short, short)
        tab_ref[at, :] = (0.25 / 1.5) * both_halves(weight_ref, 0, short) * mixed_ref[at, :] - 0.5 * down
    for b in range(blocks):
        for t in range(traits):
            at = (slice(t, t + 1), slice(b * 128, (b + 1) * 128))
            image_ref[at] = image_ref[at] + tab_ref[t * blocks + b : t * blocks + b + 1, :]
    image_ref[:, :128] = image_ref[:, :128] + resid_ref[...]
    direction = dir_ref[...]
    image = image_ref[...] + rec_ref[...] * direction
    image_ref[...] = image
    res = res_ref[...]
    inv = inv_ref[...]
    columns = dir_a_ref.shape[1]
    sums = jnp.sum(got_ref[:, :, 2 * wide :], axis=0)
    tiles = sums.shape[1] // 128
    back = jnp.concatenate([sums[:, j * 128 : (j + 1) * 128] for j in range(tiles)], axis=0)[:, :columns]
    dir_a = dir_a_ref[...]
    image_a = ridge_ref[...] * dir_a - back
    image_a_ref[...] = image_a
    res_a = res_a_ref[...]
    inv_a = inv_a_ref[...]
    weighted, weighted_a = inv * res, inv_a * res_a
    lane = lax.broadcasted_iota(jnp.int32, (1, 128), 1)
    pairs = (
        (weighted * res, weighted_a * res_a),
        (direction * image, dir_a * image_a),
        (weighted * image, weighted_a * image_a),
        (inv * image * image, inv_a * image_a * image_a),
    )
    total = jnp.zeros((1, 128), F32)
    for j, (one, two) in enumerate(pairs):
        value = jnp.sum(one, keepdims=True) + jnp.sum(two, keepdims=True)
        total = jnp.where(lane == j, value, total)
    sums_ref[...] = total


def update_kernel(
    sums_ref, sol_ref, res_ref, dir_ref, inv_ref, image_ref,
    sol_a_ref, res_a_ref, dir_a_ref, inv_a_ref, image_a_ref,
    nsol_ref, nres_ref, ndir_ref, nsol_a_ref, nres_a_ref, ndir_a_ref,
):
    total = jnp.sum(sums_ref[...], axis=0)
    norm, curve, cross, square = (total[:, j : j + 1] for j in range(4))
    size = norm / curve
    following = norm - 2.0 * size * cross + size * size * square
    ratio = following / norm
    for sol, res, dire, inv, image, nsol, nres, ndir in (
        (sol_ref, res_ref, dir_ref, inv_ref, image_ref, nsol_ref, nres_ref, ndir_ref),
        (sol_a_ref, res_a_ref, dir_a_ref, inv_a_ref, image_a_ref, nsol_a_ref, nres_a_ref, ndir_a_ref),
    ):
        d = dire[...]
        nsol[...] = sol[...] + size * d
        left = res[...] - size * image[...]
        nres[...] = left
        ndir[...] = inv[...] * left + ratio * d


def pedigree_by_blocks(field, sire, dam, herd_count, herd_index):
    traits_here, animals = field.shape
    block_count = animals // 128
    span = SLOTS * 128
    has_sire = sire >= 0
    has_dam = dam >= 0
    sire_known = has_sire.astype(F32)
    dam_known = has_dam.astype(F32)
    owner_herd = jnp.where(has_sire, sire // animals, 0)
    block_index = jnp.where(has_sire, sire % animals // 128, 0)
    offset = jnp.where(has_sire, sire % 128, 0)
    flat_block = jnp.where(
        has_sire, owner_herd * block_count + block_index, herd_count * block_count
    )
    present = jnp.zeros((herd_count * block_count + 1,), jnp.int32).at[flat_block].max(1)
    present = present[:-1].reshape(herd_count, block_count)
    slot_order = jnp.cumsum(present, axis=1) - 1
    slot_range = jnp.arange(SLOTS, dtype=jnp.int32)
    slot_match = (present[:, :, None] == 1) & (slot_order[:, :, None] == slot_range[None, None, :])
    block_ids = jnp.arange(block_count, dtype=jnp.int32)[None, :, None] + 1
    wanted = jnp.sum(jnp.where(slot_match, block_ids, 0), axis=1) - 1
    requests = lax.all_to_all(wanted, HERD, split_axis=0, concat_axis=0, tiled=True)
    live_slot = requests >= 0
    field_tiles = field.reshape(traits_here, block_count, 128)
    outgoing = field_tiles[:, jnp.where(live_slot, requests, 0), :]
    outgoing = jnp.where(live_slot[None, :, :, None], outgoing, 0.0).reshape(
        traits_here, herd_count, span
    )
    fetched = lax.all_to_all(outgoing, HERD, split_axis=1, concat_axis=1, tiled=True).reshape(
        traits_here, herd_count * span
    )
    slot_index = slot_order[owner_herd, block_index]
    buffer_place = owner_herd * span + slot_index * 128 + offset
    sire_values = fetched[:, jnp.where(has_sire, buffer_place, 0)]
    local_dam = jnp.where(has_dam, dam - herd_index * animals, 0)
    dam_values = field[:, local_dam]
    weight = 4.0 / (4.0 - sire_known - dam_known)
    scaled = weight * (field - 0.5 * sire_known * sire_values - 0.5 * dam_known * dam_values)
    dam_target = jnp.where(has_dam, local_dam, animals)
    dam_terms = (
        jnp.zeros((traits_here, animals + 1), F32).at[:, dam_target].add(-0.5 * dam_known * scaled)
    )
    result = scaled + dam_terms[:, :animals]
    sire_target = jnp.where(has_sire, buffer_place, herd_count * span)
    outbound = (
        jnp.zeros((traits_here, herd_count * span + 1), F32)
        .at[:, sire_target]
        .add(-0.5 * sire_known * scaled)
    )
    outbound = outbound[:, :-1].reshape(traits_here, herd_count, span)
    returned = lax.all_to_all(outbound, HERD, split_axis=1, concat_axis=1, tiled=True).reshape(
        traits_here, herd_count * SLOTS, 128
    )
    block_target = jnp.where(live_slot, requests, block_count).reshape(herd_count * SLOTS)
    incoming = (
        jnp.zeros((traits_here, block_count + 1, 128), F32).at[:, block_target, :].add(returned)
    )
    return result + incoming[:, :block_count, :].reshape(traits_here, animals)


def body(
    sol_u, res_u, dir_u, rec_weight, inv_diag_u, sol_a, res_a, dir_a, inv_diag_a,
    genotypes, allele_freq, geno_weight, snp_ridge, genetic_inv, sire, dam,
):
    shape = ny, nz, nc = tuple(lax.axis_size(a) for a in HERD)
    nx = lax.axis_size("x")
    herd, near = ny * nz * nc, ny * nc
    x_index = lax.axis_index("x")
    here, animals = dir_u.shape
    traits, _, columns = dir_a.shape
    genotyped, snps = genotypes.shape
    blocks = animals // 128
    half = here * blocks
    lists, values = 2 * CAP, here * CAP
    spare = traits // near * 128
    scale = 2.0 / math.sqrt(snps * nx)
    sds = lambda *s: jax.ShapeDtypeStruct(s, F32)
    vmem = lambda *s: pltpu.VMEM(s, F32)
    d_a, r_a, s_a, i_a = (a[:, 0, :] for a in (dir_a, res_a, sol_a, inv_diag_a))
    freq = allele_freq[None, :]
    sire_row, dam_row = sire[None, :], dam[None, :]
    mine = jnp.arange(128) // genotyped == x_index
    weight_here = jnp.where(mine[None, :], geno_weight[:, None], 0.0)

    out_z, rank, table = call(
        functools.partial(lists_kernel, shape=shape),
        (sds(nz, near, lists + spare), jax.ShapeDtypeStruct((1, animals), jnp.int32), sds(half, 128)),
        scratch=[vmem(3 * CAP // 2, 2 * herd)],
    )(dir_u, d_a, sire_row, dam_row)
    in_z = lax.all_to_all(out_z, "z", 0, 0, tiled=True)
    from_others = [
        lax.ppermute(table, "x", [(i, (i + k) % nx) for i in range(nx)]) for k in range(1, nx)
    ]
    out_near = call(
        functools.partial(forward_kernel, columns=columns, lists=lists),
        sds(ny, traits, nc * lists + nz * columns),
    )(in_z)
    out_near, place = lax.optimization_barrier((out_near, x_index))
    all_tables = []
    for j in range(nx):
        chosen = table
        for k in range(1, nx):
            chosen = jnp.where(place == (j + k) % nx, from_others[k - 1], chosen)
        all_tables.append(chosen)
    all_tables = jnp.stack(all_tables)
    in_y = lax.all_to_all(out_near, "y", 0, 0, tiled=True)

    on_chip = pl.BlockSpec(memory_space=pltpu.VMEM)
    scalars = pl.BlockSpec(memory_space=pltpu.SMEM)
    mixed_table, c_term, add = call(
        functools.partial(offspring_kernel, shape=shape),
        (sds(half, 128), sds(here, animals), sds(near, nz, values)),
        scratch=[vmem(here * CAP, 2 * herd)],
        in_specs=[scalars] + [on_chip] * 4,
    )(genetic_inv, all_tables, sire_row, dam_row, rank)
    in_y, mixed_table, c_term, add = lax.optimization_barrier((in_y, mixed_table, c_term, add))
    in_near = lax.all_gather(in_y, "c", axis=0)

    to_x, asked, turned, over = call(
        functools.partial(predict_kernel, shape=shape, columns=columns, lists=lists, scale=scale),
        (sds(nx, 2 * here, 128), sds(near, nz, lists), sds(lists, herd), sds(8, 128)),
        scratch=[vmem(traits, nz * nc * columns), vmem(traits, 128)],
        in_specs=[scalars] + [on_chip] * 4,
    )(lax.axis_index("c").reshape(1), in_near, genotypes, freq, weight_here)
    from_x = lax.all_to_all(to_x, "x", 0, 0, tiled=True)

    back_near, resid = call(
        functools.partial(reply_kernel, shape=shape, columns=columns, scale=scale),
        (sds(near, traits, 2 * values + nz * columns), sds(traits, 128)),
        scratch=[vmem(values, herd), vmem(traits, nz * nc * columns)],
    )(mixed_table, add, all_tables, from_x, turned, genotypes, freq)
    got_near = lax.all_to_all(back_near, ("y", "c"), 0, 0, tiled=True)
    back_z = call(
        functools.partial(backward_kernel, columns=columns, values=2 * values),
        sds(nz, near, 2 * values + spare),
    )(got_near)
    back_z, asked = lax.optimization_barrier((back_z, asked))
    got_z = lax.all_to_all(back_z, "z", 0, 0, tiled=True)
    ordered = call(order_kernel, sds(lists, herd), scratch=[vmem(nz, near, lists)])(asked)
    too_long = over[0, 0] > 0.5
    got_z, ordered, too_long = lax.optimization_barrier((got_z, ordered, too_long))

    own_resid = lax.dynamic_slice_in_dim(resid, x_index * here, here, 0)
    image_u, image_a, sums = call(
        functools.partial(image_kernel, shape=shape),
        (sds(here, animals), sds(traits, columns), sds(1, 128)),
        scratch=[vmem(here * blocks, 256), vmem(half, 128), vmem(values, herd), vmem(blocks // 2, 256)],
    )(
        got_z, c_term, rank, sire_row, dam_row, ordered, mixed_table, own_resid,
        dir_u, rec_weight, res_u, inv_diag_u, snp_ridge[:, None], d_a, r_a, i_a,
    )

    u, a = sds(here, animals), sds(traits, columns)

    def reduced(sums):
        close = lax.all_to_all(
            jnp.broadcast_to(sums[None], (near * nx, 1, 128)), ("y", "c", "x"), 0, 0, tiled=True
        )
        close = jnp.sum(close, axis=0, keepdims=True)
        return lax.all_to_all(jnp.broadcast_to(close, (nz, 1, 128)), "z", 0, 0, tiled=True)

    def finish(image, far):
        return tuple(
            call(update_kernel, (u, u, u, a, a, a))(
                far, sol_u, res_u, dir_u, inv_diag_u, image, s_a, r_a, d_a, i_a, image_a
            )
        )

    def by_blocks(_):
        dir_all = all_tables.reshape(traits, animals)
        mixed = jnp.dot(genetic_inv, dir_all, precision=lax.Precision.HIGHEST)
        image = rec_weight * dir_u + pedigree_by_blocks(mixed, sire, dam, herd, lax.axis_index(HERD))
        image = image.at[:, :genotyped].add(own_resid[:, :genotyped])
        cells = [
            jnp.sum(inv_diag_u * res_u * res_u) + jnp.sum(i_a * r_a * r_a),
            jnp.sum(dir_u * image) + jnp.sum(d_a * image_a),
            jnp.sum(inv_diag_u * res_u * image) + jnp.sum(i_a * r_a * image_a),
            jnp.sum(inv_diag_u * image * image) + jnp.sum(i_a * image_a * image_a),
        ]
        return finish(image, reduced(jnp.pad(jnp.stack(cells), (0, 124))[None, :]))

    far, too_long = lax.optimization_barrier((reduced(sums), too_long))
    outs = finish(image_u, far)
    outs = lax.cond(too_long, by_blocks, lambda done: done, outs)
    return outs[:3] + tuple(o[:, None, :] for o in outs[3:])


def solution(mesh):
    herd, nx = mesh.devices.shape
    ny, nc = 4, 2
    grid = Mesh(mesh.devices.reshape(ny, herd // (ny * nc), nc, nx), HERD + ("x",))
    u = P("x", HERD)
    a = P(None, "x", HERD)
    return jax.shard_map(
        body,
        mesh=grid,
        in_specs=(
            u, u, u, u, u, a, a, a, a,
            P(HERD, "x"), P("x"), P("x"), P(), P("x", None), P(HERD), P(HERD),
        ),
        out_specs=(u, u, u, a, a, a),
        check_vma=False,
    )
```

```python
import functools
import math

import jax
import jax.numpy as jnp
import numpy as np
from jax import lax
from jax.experimental import pallas as pl
from jax.experimental.pallas import tpu as pltpu
from jax.sharding import Mesh, PartitionSpec as P

SLOTS = 2
CAP = 64
LIST = CAP - 1
CHUNK = 512
HERD = ("y", "z", "c")
F32 = jnp.float32
BF16 = jnp.bfloat16

NT = (((1,), (1,)), ((), ()))
NN = (((1,), (0,)), ((), ()))


def call(kernel, out, scratch=(), **kw):
    return pl.pallas_call(
        kernel,
        out_shape=out,
        scratch_shapes=list(scratch),
        compiler_params=pltpu.CompilerParams(vmem_limit_bytes=20 * 2**20),
        **kw,
    )


def dot(a, b, dims=NN):
    return lax.dot_general(a, b, dims, preferred_element_type=F32)


def parts(x, n=2):
    out = []
    for _ in range(n):
        p = x.astype(BF16).astype(F32)
        out.append(p)
        x = x - p
    return out


def rows_at(n, cols):
    return lax.broadcasted_iota(jnp.int32, (n, cols), 0)


def weights(sire, dam):
    known = (sire >= 0).astype(jnp.int32) + (dam >= 0).astype(jnp.int32)
    return jnp.where(known == 2, 2.0, jnp.where(known == 1, 4.0 / 3.0, 1.0)).astype(F32)


def place_in(local, known):
    return jnp.where(known, (local >> 7) & 15, -1), ((local >> 11) << 7) + (local & 127)


def one_hot(index, rows):
    return jnp.where(counted(rows, index.shape[1]) == index.astype(F32).astype(BF16), jnp.ones((), BF16), jnp.zeros((), BF16))


def counted(rows, n):
    column = rows_at(rows, 128).astype(F32).astype(BF16)
    return jnp.concatenate([column] * (n // 128), axis=1)


def pick(found, in_group, t):
    rows = in_group.shape[0]
    return jnp.sum(jnp.where(in_group, found[t * rows : (t + 1) * rows], 0.0), axis=0, keepdims=True)


def side_by_side(table):
    return jnp.concatenate([p.astype(BF16) for p in parts(table)], axis=1)


def look_up(table, index, rows):
    hit = one_hot(index, rows)
    return dot(table, jnp.concatenate([hit, hit], axis=0))


def both_halves(acc_ref, first, rows):
    at = slice(first, first + rows)
    return jnp.concatenate([acc_ref[at, :128], acc_ref[at, 128:]], axis=0)


def masked(index, rows, fields):
    here = counted(rows, index.shape[1]) == index.astype(F32).astype(BF16)
    return jnp.concatenate([jnp.where(here, f.astype(BF16), jnp.zeros((), BF16)) for f in fields], axis=0)


def moved(width, pieces, load, rows):
    lane = lax.broadcasted_iota(jnp.int32, (rows, 128), 1)
    for k in range(width // 128):
        tile = jnp.zeros((rows, 128), F32)
        for source, first, at, length in pieces:
            lo, hi = max(at, k * 128), min(at + length, (k + 1) * 128)
            while lo < hi:
                src = first + lo - at
                end = min(hi, lo + 128 - src % 128)
                turn = (lo - src) % 128
                value = load(source, src // 128)
                if turn:
                    value = pltpu.roll(value, turn, 1)
                a, b = lo - k * 128, end - k * 128
                tile = value if (a, b) == (0, 128) else jnp.where((lane >= a) & (lane < b), value, tile)
                lo = end
        yield k, tile


def lists_kernel(dir_ref, dir_a_ref, sire_ref, dam_ref, out_ref, rank_ref, tab_ref, acc_ref, *, shape):
    ny, nz, nc = shape
    traits, animals = dir_ref.shape
    herd = ny * nz * nc
    blocks = animals // 128
    n = CHUNK
    for t in range(traits):
        for b in range(blocks):
            tab_ref[t * blocks + b : t * blocks + b + 1, :] = dir_ref[t : t + 1, b * 128 : (b + 1) * 128]
    before = (rows_at(n, n) < lax.broadcasted_iota(jnp.int32, (n, n), 1)).astype(F32).astype(BF16)
    acc_ref[...] = jnp.zeros(acc_ref.shape, F32)

    def step(k, carry):
        at = pl.ds(pl.multiple_of(k * n, n), n)
        sire = sire_ref[:, at]
        row = owner_row(sire, animals, shape)
        is_owner = rows_at(herd, n) == row
        owners = is_owner.astype(F32).astype(BF16)
        earlier = dot(owners, before) + carry
        rank = jnp.sum(jnp.where(is_owner, earlier, 0.0), axis=0, keepdims=True).astype(jnp.int32)
        rank = jnp.where((sire >= 0) & (rank < LIST), rank, -1)
        rank_ref[:, at] = rank
        local = (sire & (animals - 1)) + 1
        weight = weights(sire, dam_ref[:, at]) * 1.5
        in_row, target = slot_of(rank, row, herd)
        fields = masked(in_row, CAP // 2, [(local & ~63).astype(F32), (local & 63).astype(F32), weight])
        acc_ref[...] += dot(fields, target, NT)
        return earlier[:, n - 1 :] + owners[:, n - 1 :].astype(F32)

    count = lax.fori_loop(0, animals // n, step, jnp.zeros((herd, 1), F32), unroll=True)
    overflow = jnp.where(jnp.max(count, axis=0, keepdims=True) > LIST + 0.5, 1.0, 0.0)
    lane = lax.broadcasted_iota(jnp.int32, (herd, 128), 1)
    ids = slots(acc_ref, 0, herd) + slots(acc_ref, 1, herd)
    block = jnp.concatenate([ids, slots(acc_ref, 2, herd)], axis=0).T
    block = jnp.where(lane == 127, overflow, block)
    out_ref[:, :, :128] = block.reshape(nz, ny * nc, 128)
    rows = ny * nc
    columns = dir_a_ref.shape[1]
    for j in range(dir_a_ref.shape[0] // rows):
        piece = dir_a_ref[j * rows : (j + 1) * rows, :]
        for z in range(nz):
            out_ref[z, :, 128 + j * 128 : 128 + j * 128 + columns] = piece


def slot_of(rank, row, herd):
    short = CAP // 2
    return jnp.where(rank >= 0, rank & (short - 1), -1), one_hot((rank >> (short.bit_length() - 1)) * herd + row, 2 * herd)


def slots(acc_ref, f, herd):
    at = slice(f * (CAP // 2), (f + 1) * (CAP // 2))
    return jnp.concatenate([acc_ref[at, :herd], acc_ref[at, herd:]], axis=0)


def owner_parts(sire, animals, shape):
    _, nz, nc = shape
    owner = sire >> (animals.bit_length() - 1)
    low = nc.bit_length() - 1
    c = owner & (nc - 1)
    z = (owner >> low) & (nz - 1)
    y = owner >> (low + nz.bit_length() - 1)
    return y * nc + c, z


def owner_row(sire, animals, shape):
    g, z = owner_parts(sire, animals, shape)
    return jnp.where(sire >= 0, z * (shape[0] * shape[2]) + g, -1)


def mixed(mix_ref, all_ref, t, blocks):
    total = jnp.zeros((blocks, 128), F32)
    here = all_ref.shape[1] // blocks
    for x in range(all_ref.shape[0]):
        for s in range(here):
            total = total + mix_ref[t, x * here + s] * all_ref[x, s * blocks : (s + 1) * blocks, :]
    return total


def offspring_kernel(mix_ref, all_ref, sire_ref, dam_ref, rank_ref, tab_ref, c_ref, out_ref, acc_ref, *, shape):
    ny, nz, nc = shape
    herd = ny * nz * nc
    traits, animals = c_ref.shape
    blocks = animals // 128
    n = CHUNK
    for t in range(traits):
        tab_ref[t * blocks : (t + 1) * blocks, :] = mixed(mix_ref, all_ref, t, blocks)
    for t in range(traits):
        for b in range(blocks):
            c_ref[t : t + 1, b * 128 : (b + 1) * 128] = tab_ref[t * blocks + b : t * blocks + b + 1, :]
    table = side_by_side(tab_ref[...])
    acc_ref[...] = jnp.zeros(acc_ref.shape, F32)

    def step(k, _):
        at = pl.ds(pl.multiple_of(k * n, n), n)
        sire = sire_ref[:, at]
        dam = dam_ref[:, at]
        weight = weights(sire, dam)
        local = dam & (animals - 1)
        found = look_up(table, local & 127, 128)
        in_block = rows_at(blocks, n) == jnp.where(dam >= 0, local >> 7, -1)
        fields = []
        for t in range(traits):
            value = weight * (c_ref[t : t + 1, at] - 0.5 * pick(found, in_block, t))
            c_ref[t : t + 1, at] = value
            fields += parts(value)
        g, z = owner_parts(sire, animals, shape)
        in_row, target = slot_of(rank_ref[:, at], g * nz + z, herd)
        acc_ref[...] += dot(masked(in_row, CAP // 2, fields), target, NT)
        return 0

    lax.fori_loop(0, animals // n, step, 0, unroll=True)
    lines = [slots(acc_ref, 2 * t, herd) + slots(acc_ref, 2 * t + 1, herd) for t in range(traits)]
    for j in range(traits * CAP // 128):
        block = jnp.concatenate(lines[2 * j : 2 * j + 2], axis=0).T
        out_ref[:, :, j * 128 : (j + 1) * 128] = block.reshape(ny * nc, nz, 128)


def forward_kernel(in_ref, out_ref, *, columns, lists):
    nz, near, _ = in_ref.shape
    ny, traits, _ = out_ref.shape
    cores = near // ny
    for g in range(near):
        at = g % cores * lists
        out_ref[g // cores, :nz, at : at + lists] = in_ref[:, g, :lists]
    pieces = [(z, 0, z * columns, columns) for z in range(nz)]
    for j in range(traits // near):
        first = lists + j * 128
        load = lambda z, _: in_ref[z, :, first : first + 128]
        for k, tile in moved(nz * columns, pieces, load, near):
            at = cores * lists + k * 128
            for y in range(ny):
                out_ref[y, j * near : (j + 1) * near, at : at + 128] = tile


def predict_kernel(
    core_ref, in_ref, geno_ref, freq_ref, gw_ref, out_ref, lists_ref, turned_ref, over_ref,
    joined_ref, wide_ref, *, shape, columns, lists, scale,
):
    ny, nz, nc = shape
    herd = ny * nz * nc
    traits = in_ref.shape[2]
    here = gw_ref.shape[0]
    genotyped = geno_ref.shape[0]
    mine = lax.broadcasted_iota(jnp.int32, (nz, lists), 0) * 0 + core_ref[0]
    for g in range(ny * nc):
        rows = in_ref[g % nc, g // nc, :nz, :lists]
        for c in range(1, nc):
            rows = jnp.where(mine == c, in_ref[g % nc, g // nc, :nz, c * lists : (c + 1) * lists], rows)
        lists_ref[g] = rows
    turned_ref[...] = lists_ref[...].reshape(herd, lists).T
    over_ref[...] = jnp.broadcast_to(jnp.max(turned_ref[127:128, :], keepdims=True), over_ref.shape)
    width = nz * nc * columns
    total = jnp.zeros((3 * traits, genotyped), F32)
    bias = jnp.zeros((traits, 1), F32)
    for y in range(ny):
        pieces = [
            (c, z * columns, (z * nc + c) * columns, columns) for z in range(nz) for c in range(nc)
        ]
        load = lambda c, k: in_ref[c, y, :, nc * lists + k * 128 : nc * lists + (k + 1) * 128]
        for k, tile in moved(width, pieces, load, traits):
            joined_ref[:, k * 128 : (k + 1) * 128] = tile
        at = slice(y * width, (y + 1) * width)
        values = joined_ref[...]
        stack = jnp.concatenate([p.astype(BF16) for p in parts(values, 3)], axis=0)
        total = total + dot(stack, geno_ref[:, at], NT)
        bias = bias + jnp.sum(values * (2.0 * freq_ref[:, at]), axis=1, keepdims=True)
    rows = total[:traits] + total[traits : 2 * traits] + total[2 * traits :]
    wide_ref[...] = jnp.zeros((traits, 128), F32)
    wide_ref[:, :genotyped] = (rows - bias) * scale
    packed = together([wide_ref[x * here : (x + 1) * here, :] for x in range(traits // here)], genotyped)
    for x in range(out_ref.shape[0]):
        out_ref[x, :here, :] = packed
        out_ref[x, here:, :] = gw_ref[...]


def together(groups, width):
    total = groups[0]
    for x in range(1, len(groups)):
        total = total + pltpu.roll(groups[x], x * width, 1)
    return total


def flat(ref, first, group):
    tile = ref[pl.ds(first, group), :]
    return jnp.concatenate([tile[j : j + 1] for j in range(group)], axis=1)


def reply_kernel(
    tab_ref, add_ref, all_ref, pred_ref, ids_ref, geno_ref, freq_ref,
    out_ref, resid_ref, vals_ref, summed_ref, *, shape, columns, scale,
):
    ny, nz, nc = shape
    herd = ny * nz * nc
    nx = all_ref.shape[0]
    traits = resid_ref.shape[0]
    half = tab_ref.shape[0]
    blocks = 32
    here = half // blocks
    genotyped = geno_ref.shape[0]
    table = side_by_side(tab_ref[...])
    group = 8

    def step(k, _):
        r = pl.multiple_of(k * group, group)
        place = flat(ids_ref, r, group).astype(jnp.int32) - 1
        in_block = rows_at(blocks, group * herd) == (place >> 7)
        found = look_up(table, place & 127, 128)
        for t in range(here):
            value = pick(found, in_block, t)
            vals_ref[pl.ds(t * CAP + r, group), :] = jnp.concatenate(
                [value[:, j * herd : (j + 1) * herd] for j in range(group)], axis=0
            )
        return 0

    lax.fori_loop(0, CAP // group, step, 0, unroll=True)
    values = here * CAP
    for j in range(values // 128):
        at = slice(j * 128, (j + 1) * 128)
        out_ref[:, :nz, at] = vals_ref[at, :].T.reshape(ny * nc, nz, 128)
    out_ref[:, :nz, values : 2 * values] = add_ref[...]
    values = 2 * values

    total = pred_ref[0]
    for x in range(1, nx):
        total = total + pred_ref[x]
    lane = lax.broadcasted_iota(jnp.int32, (here, 128), 1)
    own = [
        jnp.concatenate([all_ref[x, s * blocks : s * blocks + 1, :] for s in range(here)], axis=0)
        for x in range(nx)
    ]
    own = together([jnp.where(lane < genotyped, o, 0.0) for o in own], genotyped)
    packed = total[here:] * (own - total[:here])
    for x in range(nx):
        rows = pltpu.roll(packed, 128 - x * genotyped, 1) if x else packed
        resid_ref[x * here : (x + 1) * here, :] = jnp.where(lane < genotyped, rows, 0.0)
    resid = resid_ref[...]
    stack = jnp.concatenate([p.astype(BF16) for p in parts(resid, 3)], axis=0)[:, :genotyped]
    summed = jnp.sum(resid, axis=1, keepdims=True)
    width = nz * nc * columns
    for y in range(ny):
        at = slice(y * width, (y + 1) * width)
        found = dot(stack, geno_ref[:, at])
        found = found[:traits] + found[traits : 2 * traits] + found[2 * traits :]
        summed_ref[...] = (found - summed * (2.0 * freq_ref[:, at])) * scale
        for c in range(nc):
            pieces = [(0, (z * nc + c) * columns, z * columns, columns) for z in range(nz)]
            load = lambda _, k: summed_ref[:, k * 128 : (k + 1) * 128]
            for k, tile in moved(nz * columns, pieces, load, traits):
                out_ref[y * nc + c, :, values + k * 128 : values + (k + 1) * 128] = tile


def backward_kernel(in_ref, out_ref, *, columns, values):
    nz, near, _ = out_ref.shape
    traits = in_ref.shape[1]
    for g in range(near):
        out_ref[:, g, :values] = in_ref[g, :nz, :values]
    total = in_ref[0, :, values:]
    for g in range(1, near):
        total = total + in_ref[g, :, values:]
    load = lambda _, k: total[:, k * 128 : (k + 1) * 128]
    for z in range(nz):
        for _, tile in moved(128, [(0, z * columns, 0, columns)], load, traits):
            for j in range(traits // near):
                first = values + j * 128
                out_ref[z, :, first : first + 128] = tile[j * near : (j + 1) * near]


def order_kernel(in_ref, out_ref, swapped_ref):
    near, nz, lists = in_ref.shape
    for g in range(near):
        swapped_ref[:, g, :] = in_ref[g]
    out_ref[...] = swapped_ref[...].reshape(near * nz, lists).T


def image_kernel(
    got_ref, c_ref, rank_ref, sire_ref, dam_ref, lists_ref, mixed_ref, resid_ref,
    dir_ref, rec_ref, res_ref, inv_ref, ridge_ref, dir_a_ref, res_a_ref, inv_a_ref,
    image_ref, image_a_ref, sums_ref, acc_ref, tab_ref, turned_ref, weight_ref, *, shape,
):
    traits, animals = c_ref.shape
    ny, nz, nc = shape
    herd, near = ny * nz * nc, ny * nc
    blocks = animals // 128
    n = CHUNK
    short = blocks // 2
    wide = traits * CAP
    table = side_by_side(got_ref[:, :, :wide].reshape(herd, wide).T)
    for j in range(wide // 128):
        first = wide + j * 128
        turned_ref[j * 128 : (j + 1) * 128, :] = got_ref[:, :, first : first + 128].reshape(herd, 128).T
    acc_ref[...] = jnp.zeros(acc_ref.shape, F32)
    weight_ref[...] = jnp.zeros(weight_ref.shape, F32)
    group = 8

    def add(k):
        r = pl.multiple_of(k * group, group)
        place = flat(lists_ref, r, group).astype(jnp.int32) - 1
        row, column = place_in(place, place >= 0)
        fields = []
        for t in range(traits):
            fields += parts(flat(turned_ref, t * CAP + r, group))
        return masked(row, short, fields + [flat(lists_ref, CAP + r, group)]), one_hot(column, 256)

    def step(k):
        at = pl.ds(pl.multiple_of(k * n, n), n)
        sire = sire_ref[:, at]
        dam = dam_ref[:, at]
        weight = weights(sire, dam)
        found = look_up(table, owner_row(sire, animals, shape), herd)
        in_slot = rows_at(CAP, n) == rank_ref[:, at]
        row, column = place_in(dam & (animals - 1), dam >= 0)
        fields = []
        for t in range(traits):
            scaled = c_ref[t : t + 1, at] - 0.5 * weight * pick(found, in_slot, t)
            image_ref[t : t + 1, at] = scaled
            fields += parts(scaled)
        fields.append(jnp.zeros((1, n), F32))
        return masked(row, short, fields), one_hot(column, 256)

    def both(k, _):
        fields, hits = zip(add(k), step(k))
        sums = dot(jnp.concatenate(fields, axis=1), jnp.concatenate(hits, axis=1), NT)
        acc_ref[...] += sums[: 2 * traits * short]
        weight_ref[...] += sums[2 * traits * short :]
        return 0

    assert animals // n == CAP // group
    lax.fori_loop(0, animals // n, both, 0, unroll=True)
    for t in range(traits):
        at = slice(t * blocks, (t + 1) * blocks)
        first = 2 * t * short
        down = both_halves(acc_ref, first, short) + both_halves(acc_ref, first + short, short)
        tab_ref[at, :] = (0.25 / 1.5) * both_halves(weight_ref, 0, short) * mixed_ref[at, :] - 0.5 * down
    for b in range(blocks):
        for t in range(traits):
            at = (slice(t, t + 1), slice(b * 128, (b + 1) * 128))
            image_ref[at] = image_ref[at] + tab_ref[t * blocks + b : t * blocks + b + 1, :]
    image_ref[:, :128] = image_ref[:, :128] + resid_ref[...]
    direction = dir_ref[...]
    image = image_ref[...] + rec_ref[...] * direction
    image_ref[...] = image
    res = res_ref[...]
    inv = inv_ref[...]
    columns = dir_a_ref.shape[1]
    sums = jnp.sum(got_ref[:, :, 2 * wide :], axis=0)
    tiles = sums.shape[1] // 128
    back = jnp.concatenate([sums[:, j * 128 : (j + 1) * 128] for j in range(tiles)], axis=0)[:, :columns]
    dir_a = dir_a_ref[...]
    image_a = ridge_ref[...] * dir_a - back
    image_a_ref[...] = image_a
    res_a = res_a_ref[...]
    inv_a = inv_a_ref[...]
    weighted, weighted_a = inv * res, inv_a * res_a
    lane = lax.broadcasted_iota(jnp.int32, (1, 128), 1)
    pairs = (
        (weighted * res, weighted_a * res_a),
        (direction * image, dir_a * image_a),
        (weighted * image, weighted_a * image_a),
        (inv * image * image, inv_a * image_a * image_a),
    )
    total = jnp.zeros((1, 128), F32)
    for j, (one, two) in enumerate(pairs):
        value = jnp.sum(one, keepdims=True) + jnp.sum(two, keepdims=True)
        total = jnp.where(lane == j, value, total)
    sums_ref[...] = total


def update_kernel(
    sums_ref, sol_ref, res_ref, dir_ref, inv_ref, image_ref,
    sol_a_ref, res_a_ref, dir_a_ref, inv_a_ref, image_a_ref,
    nsol_ref, nres_ref, ndir_ref, nsol_a_ref, nres_a_ref, ndir_a_ref,
):
    total = jnp.sum(sums_ref[...], axis=0)
    norm, curve, cross, square = (total[:, j : j + 1] for j in range(4))
    size = norm / curve
    following = norm - 2.0 * size * cross + size * size * square
    ratio = following / norm
    for sol, res, dire, inv, image, nsol, nres, ndir in (
        (sol_ref, res_ref, dir_ref, inv_ref, image_ref, nsol_ref, nres_ref, ndir_ref),
        (sol_a_ref, res_a_ref, dir_a_ref, inv_a_ref, image_a_ref, nsol_a_ref, nres_a_ref, ndir_a_ref),
    ):
        d = dire[...]
        nsol[...] = sol[...] + size * d
        left = res[...] - size * image[...]
        nres[...] = left
        ndir[...] = inv[...] * left + ratio * d


def pedigree_by_blocks(field, sire, dam, herd_count, herd_index):
    traits_here, animals = field.shape
    block_count = animals // 128
    span = SLOTS * 128
    has_sire = sire >= 0
    has_dam = dam >= 0
    sire_known = has_sire.astype(F32)
    dam_known = has_dam.astype(F32)
    owner_herd = jnp.where(has_sire, sire // animals, 0)
    block_index = jnp.where(has_sire, sire % animals // 128, 0)
    offset = jnp.where(has_sire, sire % 128, 0)
    flat_block = jnp.where(
        has_sire, owner_herd * block_count + block_index, herd_count * block_count
    )
    present = jnp.zeros((herd_count * block_count + 1,), jnp.int32).at[flat_block].max(1)
    present = present[:-1].reshape(herd_count, block_count)
    slot_order = jnp.cumsum(present, axis=1) - 1
    slot_range = jnp.arange(SLOTS, dtype=jnp.int32)
    slot_match = (present[:, :, None] == 1) & (slot_order[:, :, None] == slot_range[None, None, :])
    block_ids = jnp.arange(block_count, dtype=jnp.int32)[None, :, None] + 1
    wanted = jnp.sum(jnp.where(slot_match, block_ids, 0), axis=1) - 1
    requests = lax.all_to_all(wanted, HERD, split_axis=0, concat_axis=0, tiled=True)
    live_slot = requests >= 0
    field_tiles = field.reshape(traits_here, block_count, 128)
    outgoing = field_tiles[:, jnp.where(live_slot, requests, 0), :]
    outgoing = jnp.where(live_slot[None, :, :, None], outgoing, 0.0).reshape(
        traits_here, herd_count, span
    )
    fetched = lax.all_to_all(outgoing, HERD, split_axis=1, concat_axis=1, tiled=True).reshape(
        traits_here, herd_count * span
    )
    slot_index = slot_order[owner_herd, block_index]
    buffer_place = owner_herd * span + slot_index * 128 + offset
    sire_values = fetched[:, jnp.where(has_sire, buffer_place, 0)]
    local_dam = jnp.where(has_dam, dam - herd_index * animals, 0)
    dam_values = field[:, local_dam]
    weight = 4.0 / (4.0 - sire_known - dam_known)
    scaled = weight * (field - 0.5 * sire_known * sire_values - 0.5 * dam_known * dam_values)
    dam_target = jnp.where(has_dam, local_dam, animals)
    dam_terms = (
        jnp.zeros((traits_here, animals + 1), F32).at[:, dam_target].add(-0.5 * dam_known * scaled)
    )
    result = scaled + dam_terms[:, :animals]
    sire_target = jnp.where(has_sire, buffer_place, herd_count * span)
    outbound = (
        jnp.zeros((traits_here, herd_count * span + 1), F32)
        .at[:, sire_target]
        .add(-0.5 * sire_known * scaled)
    )
    outbound = outbound[:, :-1].reshape(traits_here, herd_count, span)
    returned = lax.all_to_all(outbound, HERD, split_axis=1, concat_axis=1, tiled=True).reshape(
        traits_here, herd_count * SLOTS, 128
    )
    block_target = jnp.where(live_slot, requests, block_count).reshape(herd_count * SLOTS)
    incoming = (
        jnp.zeros((traits_here, block_count + 1, 128), F32).at[:, block_target, :].add(returned)
    )
    return result + incoming[:, :block_count, :].reshape(traits_here, animals)


def body(
    sol_u, res_u, dir_u, rec_weight, inv_diag_u, sol_a, res_a, dir_a, inv_diag_a,
    genotypes, allele_freq, geno_weight, snp_ridge, genetic_inv, sire, dam,
):
    shape = ny, nz, nc = tuple(lax.axis_size(a) for a in HERD)
    nx = lax.axis_size("x")
    herd, near = ny * nz * nc, ny * nc
    x_index = lax.axis_index("x")
    here, animals = dir_u.shape
    traits, _, columns = dir_a.shape
    genotyped, snps = genotypes.shape
    blocks = animals // 128
    half = here * blocks
    lists, values = 2 * CAP, here * CAP
    spare = traits // near * 128
    scale = 2.0 / math.sqrt(snps * nx)
    sds = lambda *s: jax.ShapeDtypeStruct(s, F32)
    vmem = lambda *s: pltpu.VMEM(s, F32)
    d_a, r_a, s_a, i_a = (a[:, 0, :] for a in (dir_a, res_a, sol_a, inv_diag_a))
    freq = allele_freq[None, :]
    sire_row, dam_row = sire[None, :], dam[None, :]
    mine = jnp.arange(128) // genotyped == x_index
    weight_here = jnp.where(mine[None, :], geno_weight[:, None], 0.0)

    out_z, rank, table = call(
        functools.partial(lists_kernel, shape=shape),
        (sds(nz, near, lists + spare), jax.ShapeDtypeStruct((1, animals), jnp.int32), sds(half, 128)),
        scratch=[vmem(3 * CAP // 2, 2 * herd)],
    )(dir_u, d_a, sire_row, dam_row)
    in_z = lax.all_to_all(out_z, "z", 0, 0, tiled=True)
    from_others = [
        lax.ppermute(table, "x", [(i, (i + k) % nx) for i in range(nx)]) for k in range(1, nx)
    ]
    out_near = call(
        functools.partial(forward_kernel, columns=columns, lists=lists),
        sds(ny, traits, nc * lists + nz * columns),
    )(in_z)
    out_near, place = lax.optimization_barrier((out_near, x_index))
    all_tables = []
    for j in range(nx):
        chosen = table
        for k in range(1, nx):
            chosen = jnp.where(place == (j + k) % nx, from_others[k - 1], chosen)
        all_tables.append(chosen)
    all_tables = jnp.stack(all_tables)
    in_y = lax.all_to_all(out_near, "y", 0, 0, tiled=True)

    on_chip = pl.BlockSpec(memory_space=pltpu.VMEM)
    scalars = pl.BlockSpec(memory_space=pltpu.SMEM)
    mixed_table, c_term, add = call(
        functools.partial(offspring_kernel, shape=shape),
        (sds(half, 128), sds(here, animals), sds(near, nz, values)),
        scratch=[vmem(here * CAP, 2 * herd)],
        in_specs=[scalars] + [on_chip] * 4,
    )(genetic_inv, all_tables, sire_row, dam_row, rank)
    in_y, mixed_table, c_term, add = lax.optimization_barrier((in_y, mixed_table, c_term, add))
    in_near = lax.all_gather(in_y, "c", axis=0)

    to_x, asked, turned, over = call(
        functools.partial(predict_kernel, shape=shape, columns=columns, lists=lists, scale=scale),
        (sds(nx, 2 * here, 128), sds(near, nz, lists), sds(lists, herd), sds(8, 128)),
        scratch=[vmem(traits, nz * nc * columns), vmem(traits, 128)],
        in_specs=[scalars] + [on_chip] * 4,
    )(lax.axis_index("c").reshape(1), in_near, genotypes, freq, weight_here)
    from_x = lax.all_to_all(to_x, "x", 0, 0, tiled=True)

    back_near, resid = call(
        functools.partial(reply_kernel, shape=shape, columns=columns, scale=scale),
        (sds(near, traits, 2 * values + nz * columns), sds(traits, 128)),
        scratch=[vmem(values, herd), vmem(traits, nz * nc * columns)],
    )(mixed_table, add, all_tables, from_x, turned, genotypes, freq)
    got_near = lax.all_to_all(back_near, ("y", "c"), 0, 0, tiled=True)
    back_z = call(
        functools.partial(backward_kernel, columns=columns, values=2 * values),
        sds(nz, near, 2 * values + spare),
    )(got_near)
    back_z, asked = lax.optimization_barrier((back_z, asked))
    got_z = lax.all_to_all(back_z, "z", 0, 0, tiled=True)
    ordered = call(order_kernel, sds(lists, herd), scratch=[vmem(nz, near, lists)])(asked)
    too_long = over[0, 0] > 0.5
    got_z, ordered, too_long = lax.optimization_barrier((got_z, ordered, too_long))

    own_resid = lax.dynamic_slice_in_dim(resid, x_index * here, here, 0)
    image_u, image_a, sums = call(
        functools.partial(image_kernel, shape=shape),
        (sds(here, animals), sds(traits, columns), sds(1, 128)),
        scratch=[vmem(here * blocks, 256), vmem(half, 128), vmem(values, herd), vmem(blocks // 2, 256)],
    )(
        got_z, c_term, rank, sire_row, dam_row, ordered, mixed_table, own_resid,
        dir_u, rec_weight, res_u, inv_diag_u, snp_ridge[:, None], d_a, r_a, i_a,
    )

    u, a = sds(here, animals), sds(traits, columns)

    def reduced(sums):
        close = lax.all_to_all(
            jnp.broadcast_to(sums[None], (near * nx, 1, 128)), ("y", "c", "x"), 0, 0, tiled=True
        )
        close = jnp.sum(close, axis=0, keepdims=True)
        return lax.all_to_all(jnp.broadcast_to(close, (nz, 1, 128)), "z", 0, 0, tiled=True)

    def finish(image, far):
        return tuple(
            call(update_kernel, (u, u, u, a, a, a))(
                far, sol_u, res_u, dir_u, inv_diag_u, image, s_a, r_a, d_a, i_a, image_a
            )
        )

    def by_blocks(_):
        dir_all = all_tables.reshape(traits, animals)
        mixed = jnp.dot(genetic_inv, dir_all, precision=lax.Precision.HIGHEST)
        image = rec_weight * dir_u + pedigree_by_blocks(mixed, sire, dam, herd, lax.axis_index(HERD))
        image = image.at[:, :genotyped].add(own_resid[:, :genotyped])
        cells = [
            jnp.sum(inv_diag_u * res_u * res_u) + jnp.sum(i_a * r_a * r_a),
            jnp.sum(dir_u * image) + jnp.sum(d_a * image_a),
            jnp.sum(inv_diag_u * res_u * image) + jnp.sum(i_a * r_a * image_a),
            jnp.sum(inv_diag_u * image * image) + jnp.sum(i_a * image_a * image_a),
        ]
        return finish(image, reduced(jnp.pad(jnp.stack(cells), (0, 124))[None, :]))

    far, too_long = lax.optimization_barrier((reduced(sums), too_long))
    outs = finish(image_u, far)
    outs = lax.cond(too_long, by_blocks, lambda done: done, outs)
    return outs[:3] + tuple(o[:, None, :] for o in outs[3:])


def solution(mesh):
    herd, nx = mesh.devices.shape
    ny, nc = 4, 2
    grid = Mesh(mesh.devices.reshape(ny, herd // (ny * nc), nc, nx), HERD + ("x",))
    u = P("x", HERD)
    a = P(None, "x", HERD)
    return jax.shard_map(
        body,
        mesh=grid,
        in_specs=(
            u, u, u, u, u, a, a, a, a,
            P(HERD, "x"), P("x"), P("x"), P(), P("x", None), P(HERD), P(HERD),
        ),
        out_specs=(u, u, u, a, a, a),
        check_vma=False,
    )
```

```python
import functools
import math

import jax
import jax.numpy as jnp
import numpy as np
from jax import lax
from jax.experimental import pallas as pl
from jax.experimental.pallas import tpu as pltpu
from jax.sharding import Mesh, PartitionSpec as P

SLOTS = 2
CAP = 64
LIST = CAP - 1
CHUNK = 512
HERD = ("y", "z", "c")
F32 = jnp.float32
BF16 = jnp.bfloat16

NT = (((1,), (1,)), ((), ()))
NN = (((1,), (0,)), ((), ()))


def call(kernel, out, scratch=(), **kw):
    return pl.pallas_call(
        kernel,
        out_shape=out,
        scratch_shapes=list(scratch),
        compiler_params=pltpu.CompilerParams(vmem_limit_bytes=20 * 2**20),
        **kw,
    )


def dot(a, b, dims=NN):
    return lax.dot_general(a, b, dims, preferred_element_type=F32)


def parts(x, n=2):
    out = []
    for _ in range(n):
        p = x.astype(BF16).astype(F32)
        out.append(p)
        x = x - p
    return out


def rows_at(n, cols):
    return lax.broadcasted_iota(jnp.int32, (n, cols), 0)


def weights(sire, dam):
    known = (sire >= 0).astype(jnp.int32) + (dam >= 0).astype(jnp.int32)
    return jnp.where(known == 2, 2.0, jnp.where(known == 1, 4.0 / 3.0, 1.0)).astype(F32)


def place_in(local, known):
    return jnp.where(known, (local >> 7) & 15, -1), ((local >> 11) << 7) + (local & 127)


def one_hot(index, rows):
    return jnp.where(counted(rows, index.shape[1]) == index.astype(F32).astype(BF16), jnp.ones((), BF16), jnp.zeros((), BF16))


def counted(rows, n):
    column = rows_at(rows, 128).astype(F32).astype(BF16)
    return jnp.concatenate([column] * (n // 128), axis=1)


def pick(found, in_group, t):
    rows = in_group.shape[0]
    return jnp.sum(jnp.where(in_group, found[t * rows : (t + 1) * rows], 0.0), axis=0, keepdims=True)


def side_by_side(table):
    return jnp.concatenate([p.astype(BF16) for p in parts(table)], axis=1)


def look_up(table, index, rows):
    hit = one_hot(index, rows)
    return dot(table, jnp.concatenate([hit, hit], axis=0))


def both_halves(acc_ref, first, rows):
    at = slice(first, first + rows)
    return jnp.concatenate([acc_ref[at, :128], acc_ref[at, 128:]], axis=0)


def masked(index, rows, fields):
    here = counted(rows, index.shape[1]) == index.astype(F32).astype(BF16)
    return jnp.concatenate([jnp.where(here, f.astype(BF16), jnp.zeros((), BF16)) for f in fields], axis=0)


def moved(width, pieces, load, rows):
    lane = lax.broadcasted_iota(jnp.int32, (rows, 128), 1)
    for k in range(width // 128):
        tile = jnp.zeros((rows, 128), F32)
        for source, first, at, length in pieces:
            lo, hi = max(at, k * 128), min(at + length, (k + 1) * 128)
            while lo < hi:
                src = first + lo - at
                end = min(hi, lo + 128 - src % 128)
                turn = (lo - src) % 128
                value = load(source, src // 128)
                if turn:
                    value = pltpu.roll(value, turn, 1)
                a, b = lo - k * 128, end - k * 128
                tile = value if (a, b) == (0, 128) else jnp.where((lane >= a) & (lane < b), value, tile)
                lo = end
        yield k, tile


def lists_kernel(dir_ref, dir_a_ref, sire_ref, dam_ref, out_ref, rank_ref, tab_ref, acc_ref, *, shape):
    ny, nz, nc = shape
    traits, animals = dir_ref.shape
    herd = ny * nz * nc
    blocks = animals // 128
    n = CHUNK
    for t in range(traits):
        for b in range(blocks):
            tab_ref[t * blocks + b : t * blocks + b + 1, :] = dir_ref[t : t + 1, b * 128 : (b + 1) * 128]
    before = (rows_at(n, n) < lax.broadcasted_iota(jnp.int32, (n, n), 1)).astype(F32).astype(BF16)
    acc_ref[...] = jnp.zeros(acc_ref.shape, F32)

    def step(k, carry):
        at = pl.ds(pl.multiple_of(k * n, n), n)
        sire = sire_ref[:, at]
        row = owner_row(sire, animals, shape)
        is_owner = rows_at(herd, n) == row
        owners = is_owner.astype(F32).astype(BF16)
        earlier = dot(owners, before) + carry
        rank = jnp.sum(jnp.where(is_owner, earlier, 0.0), axis=0, keepdims=True).astype(jnp.int32)
        rank = jnp.where((sire >= 0) & (rank < LIST), rank, -1)
        rank_ref[:, at] = rank
        local = (sire & (animals - 1)) + 1
        weight = weights(sire, dam_ref[:, at]) * 1.5
        in_row, target = slot_of(rank, row, herd)
        fields = masked(in_row, CAP // 2, [(local & ~63).astype(F32), (local & 63).astype(F32), weight])
        acc_ref[...] += dot(fields, target, NT)
        return earlier[:, n - 1 :] + owners[:, n - 1 :].astype(F32)

    count = lax.fori_loop(0, animals // n, step, jnp.zeros((herd, 1), F32), unroll=True)
    overflow = jnp.where(jnp.max(count, axis=0, keepdims=True) > LIST + 0.5, 1.0, 0.0)
    lane = lax.broadcasted_iota(jnp.int32, (herd, 128), 1)
    ids = slots(acc_ref, 0, herd) + slots(acc_ref, 1, herd)
    block = jnp.concatenate([ids, slots(acc_ref, 2, herd)], axis=0).T
    block = jnp.where(lane == 127, overflow, block)
    out_ref[:, :, :128] = block.reshape(nz, ny * nc, 128)
    rows = ny * nc
    columns = dir_a_ref.shape[1]
    for j in range(dir_a_ref.shape[0] // rows):
        piece = dir_a_ref[j * rows : (j + 1) * rows, :]
        for z in range(nz):
            out_ref[z, :, 128 + j * 128 : 128 + j * 128 + columns] = piece


def slot_of(rank, row, herd):
    short = CAP // 2
    return jnp.where(rank >= 0, rank & (short - 1), -1), one_hot((rank >> (short.bit_length() - 1)) * herd + row, 2 * herd)


def slots(acc_ref, f, herd):
    at = slice(f * (CAP // 2), (f + 1) * (CAP // 2))
    return jnp.concatenate([acc_ref[at, :herd], acc_ref[at, herd:]], axis=0)


def owner_parts(sire, animals, shape):
    _, nz, nc = shape
    owner = sire >> (animals.bit_length() - 1)
    low = nc.bit_length() - 1
    c = owner & (nc - 1)
    z = (owner >> low) & (nz - 1)
    y = owner >> (low + nz.bit_length() - 1)
    return y * nc + c, z


def owner_row(sire, animals, shape):
    g, z = owner_parts(sire, animals, shape)
    return jnp.where(sire >= 0, z * (shape[0] * shape[2]) + g, -1)


def mixed(mix_ref, all_ref, t, blocks):
    total = jnp.zeros((blocks, 128), F32)
    here = all_ref.shape[1] // blocks
    for x in range(all_ref.shape[0]):
        for s in range(here):
            total = total + mix_ref[t, x * here + s] * all_ref[x, s * blocks : (s + 1) * blocks, :]
    return total


def offspring_kernel(mix_ref, all_ref, sire_ref, dam_ref, rank_ref, tab_ref, c_ref, out_ref, acc_ref, *, shape):
    ny, nz, nc = shape
    herd = ny * nz * nc
    traits, animals = c_ref.shape
    blocks = animals // 128
    n = CHUNK
    for t in range(traits):
        tab_ref[t * blocks : (t + 1) * blocks, :] = mixed(mix_ref, all_ref, t, blocks)
    for t in range(traits):
        for b in range(blocks):
            c_ref[t : t + 1, b * 128 : (b + 1) * 128] = tab_ref[t * blocks + b : t * blocks + b + 1, :]
    table = side_by_side(tab_ref[...])
    acc_ref[...] = jnp.zeros(acc_ref.shape, F32)

    def step(k, _):
        at = pl.ds(pl.multiple_of(k * n, n), n)
        sire = sire_ref[:, at]
        dam = dam_ref[:, at]
        weight = weights(sire, dam)
        local = dam & (animals - 1)
        found = look_up(table, local & 127, 128)
        in_block = rows_at(blocks, n) == jnp.where(dam >= 0, local >> 7, -1)
        fields = []
        for t in range(traits):
            value = weight * (c_ref[t : t + 1, at] - 0.5 * pick(found, in_block, t))
            c_ref[t : t + 1, at] = value
            fields += parts(value)
        g, z = owner_parts(sire, animals, shape)
        in_row, target = slot_of(rank_ref[:, at], g * nz + z, herd)
        acc_ref[...] += dot(masked(in_row, CAP // 2, fields), target, NT)
        return 0

    lax.fori_loop(0, animals // n, step, 0, unroll=True)
    lines = [slots(acc_ref, 2 * t, herd) + slots(acc_ref, 2 * t + 1, herd) for t in range(traits)]
    for j in range(traits * CAP // 128):
        block = jnp.concatenate(lines[2 * j : 2 * j + 2], axis=0).T
        out_ref[:, :, j * 128 : (j + 1) * 128] = block.reshape(ny * nc, nz, 128)


def forward_kernel(in_ref, out_ref, *, columns, lists):
    nz, near, _ = in_ref.shape
    ny, traits, _ = out_ref.shape
    cores = near // ny
    for g in range(near):
        at = g % cores * lists
        out_ref[g // cores, :nz, at : at + lists] = in_ref[:, g, :lists]
    pieces = [(z, 0, z * columns, columns) for z in range(nz)]
    for j in range(traits // near):
        first = lists + j * 128
        load = lambda z, _: in_ref[z, :, first : first + 128]
        for k, tile in moved(nz * columns, pieces, load, near):
            at = cores * lists + k * 128
            for y in range(ny):
                out_ref[y, j * near : (j + 1) * near, at : at + 128] = tile


def predict_kernel(
    core_ref, in_ref, geno_ref, freq_ref, gw_ref, out_ref, lists_ref, turned_ref, over_ref,
    joined_ref, wide_ref, *, shape, columns, lists, scale,
):
    ny, nz, nc = shape
    herd = ny * nz * nc
    traits = in_ref.shape[2]
    here = gw_ref.shape[0]
    genotyped = geno_ref.shape[0]
    mine = lax.broadcasted_iota(jnp.int32, (nz, lists), 0) * 0 + core_ref[0]
    for g in range(ny * nc):
        rows = in_ref[g % nc, g // nc, :nz, :lists]
        for c in range(1, nc):
            rows = jnp.where(mine == c, in_ref[g % nc, g // nc, :nz, c * lists : (c + 1) * lists], rows)
        lists_ref[g] = rows
    turned_ref[...] = lists_ref[...].reshape(herd, lists).T
    over_ref[...] = jnp.broadcast_to(jnp.max(turned_ref[127:128, :], keepdims=True), over_ref.shape)
    width = nz * nc * columns
    total = jnp.zeros((3 * traits, genotyped), F32)
    bias = jnp.zeros((traits, 1), F32)
    for y in range(ny):
        pieces = [
            (c, z * columns, (z * nc + c) * columns, columns) for z in range(nz) for c in range(nc)
        ]
        load = lambda c, k: in_ref[c, y, :, nc * lists + k * 128 : nc * lists + (k + 1) * 128]
        for k, tile in moved(width, pieces, load, traits):
            joined_ref[:, k * 128 : (k + 1) * 128] = tile
        at = slice(y * width, (y + 1) * width)
        values = joined_ref[...]
        stack = jnp.concatenate([p.astype(BF16) for p in parts(values, 3)], axis=0)
        total = total + dot(stack, geno_ref[:, at], NT)
        bias = bias + jnp.sum(values * (2.0 * freq_ref[:, at]), axis=1, keepdims=True)
    rows = total[:traits] + total[traits : 2 * traits] + total[2 * traits :]
    wide_ref[...] = jnp.zeros((traits, 128), F32)
    wide_ref[:, :genotyped] = (rows - bias) * scale
    packed = together([wide_ref[x * here : (x + 1) * here, :] for x in range(traits // here)], genotyped)
    for x in range(out_ref.shape[0]):
        out_ref[x, :here, :] = packed
        out_ref[x, here:, :] = gw_ref[...]


def together(groups, width):
    total = groups[0]
    for x in range(1, len(groups)):
        total = total + pltpu.roll(groups[x], x * width, 1)
    return total


def flat(ref, first, group):
    tile = ref[pl.ds(first, group), :]
    return jnp.concatenate([tile[j : j + 1] for j in range(group)], axis=1)


def reply_kernel(
    tab_ref, add_ref, all_ref, pred_ref, ids_ref, geno_ref, freq_ref,
    out_ref, resid_ref, vals_ref, summed_ref, *, shape, columns, scale,
):
    ny, nz, nc = shape
    herd = ny * nz * nc
    nx = all_ref.shape[0]
    traits = resid_ref.shape[0]
    half = tab_ref.shape[0]
    blocks = 32
    here = half // blocks
    genotyped = geno_ref.shape[0]
    table = side_by_side(tab_ref[...])
    group = 8

    def step(k, _):
        r = pl.multiple_of(k * group, group)
        place = flat(ids_ref, r, group).astype(jnp.int32) - 1
        in_block = rows_at(blocks, group * herd) == (place >> 7)
        found = look_up(table, place & 127, 128)
        for t in range(here):
            value = pick(found, in_block, t)
            vals_ref[pl.ds(t * CAP + r, group), :] = jnp.concatenate(
                [value[:, j * herd : (j + 1) * herd] for j in range(group)], axis=0
            )
        return 0

    lax.fori_loop(0, CAP // group, step, 0, unroll=True)
    values = here * CAP
    for j in range(values // 128):
        at = slice(j * 128, (j + 1) * 128)
        out_ref[:, :nz, at] = vals_ref[at, :].T.reshape(ny * nc, nz, 128)
    out_ref[:, :nz, values : 2 * values] = add_ref[...]
    values = 2 * values

    total = pred_ref[0]
    for x in range(1, nx):
        total = total + pred_ref[x]
    lane = lax.broadcasted_iota(jnp.int32, (here, 128), 1)
    own = [
        jnp.concatenate([all_ref[x, s * blocks : s * blocks + 1, :] for s in range(here)], axis=0)
        for x in range(nx)
    ]
    own = together([jnp.where(lane < genotyped, o, 0.0) for o in own], genotyped)
    packed = total[here:] * (own - total[:here])
    for x in range(nx):
        rows = pltpu.roll(packed, 128 - x * genotyped, 1) if x else packed
        resid_ref[x * here : (x + 1) * here, :] = jnp.where(lane < genotyped, rows, 0.0)
    resid = resid_ref[...]
    stack = jnp.concatenate([p.astype(BF16) for p in parts(resid, 3)], axis=0)[:, :genotyped]
    summed = jnp.sum(resid, axis=1, keepdims=True)
    width = nz * nc * columns
    for y in range(ny):
        at = slice(y * width, (y + 1) * width)
        found = dot(stack, geno_ref[:, at])
        found = found[:traits] + found[traits : 2 * traits] + found[2 * traits :]
        summed_ref[...] = (found - summed * (2.0 * freq_ref[:, at])) * scale
        for c in range(nc):
            pieces = [(0, (z * nc + c) * columns, z * columns, columns) for z in range(nz)]
            load = lambda _, k: summed_ref[:, k * 128 : (k + 1) * 128]
            for k, tile in moved(nz * columns, pieces, load, traits):
                out_ref[y * nc + c, :, values + k * 128 : values + (k + 1) * 128] = tile


def backward_kernel(in_ref, out_ref, *, columns, values):
    nz, near, _ = out_ref.shape
    traits = in_ref.shape[1]
    for g in range(near):
        out_ref[:, g, :values] = in_ref[g, :nz, :values]
    total = in_ref[0, :, values:]
    for g in range(1, near):
        total = total + in_ref[g, :, values:]
    load = lambda _, k: total[:, k * 128 : (k + 1) * 128]
    for z in range(nz):
        for _, tile in moved(128, [(0, z * columns, 0, columns)], load, traits):
            for j in range(traits // near):
                first = values + j * 128
                out_ref[z, :, first : first + 128] = tile[j * near : (j + 1) * near]


def order_kernel(in_ref, out_ref, swapped_ref):
    near, nz, lists = in_ref.shape
    for g in range(near):
        swapped_ref[:, g, :] = in_ref[g]
    out_ref[...] = swapped_ref[...].reshape(near * nz, lists).T


def image_kernel(
    got_ref, c_ref, rank_ref, sire_ref, dam_ref, lists_ref, mixed_ref, resid_ref,
    dir_ref, rec_ref, res_ref, inv_ref, ridge_ref, dir_a_ref, res_a_ref, inv_a_ref,
    image_ref, image_a_ref, sums_ref, acc_ref, tab_ref, turned_ref, weight_ref, dams_ref, *, shape,
):
    traits, animals = c_ref.shape
    ny, nz, nc = shape
    herd, near = ny * nz * nc, ny * nc
    blocks = animals // 128
    n = CHUNK
    short = blocks // 2
    wide = traits * CAP
    table = side_by_side(got_ref[:, :, :wide].reshape(herd, wide).T)
    for j in range(wide // 128):
        first = wide + j * 128
        turned_ref[j * 128 : (j + 1) * 128, :] = got_ref[:, :, first : first + 128].reshape(herd, 128).T
    acc_ref[...] = jnp.zeros(acc_ref.shape, F32)
    weight_ref[...] = jnp.zeros(weight_ref.shape, F32)
    dams_ref[...] = jnp.zeros(dams_ref.shape, F32)
    group = 8

    def add(k, _):
        r = pl.multiple_of(k * group, group)
        place = flat(lists_ref, r, group).astype(jnp.int32) - 1
        row, column = place_in(place, place >= 0)
        fields = []
        for t in range(traits):
            fields += parts(flat(turned_ref, t * CAP + r, group))
        fields = masked(row, short, fields + [flat(lists_ref, CAP + r, group)])
        sums = dot(fields, one_hot(column, 256), NT)
        acc_ref[...] += sums[: 2 * traits * short]
        weight_ref[...] += sums[2 * traits * short :]
        return 0

    lax.fori_loop(0, CAP // group, add, 0, unroll=True)

    def step(k, _):
        at = pl.ds(pl.multiple_of(k * n, n), n)
        sire = sire_ref[:, at]
        dam = dam_ref[:, at]
        weight = weights(sire, dam)
        found = look_up(table, owner_row(sire, animals, shape), herd)
        in_slot = rows_at(CAP, n) == rank_ref[:, at]
        row, column = place_in(dam & (animals - 1), dam >= 0)
        fields = []
        for t in range(traits):
            scaled = c_ref[t : t + 1, at] - 0.5 * weight * pick(found, in_slot, t)
            image_ref[t : t + 1, at] = scaled
            fields += parts(scaled)
        dams_ref[...] += dot(masked(row, short, fields), one_hot(column, 256), NT)
        return 0

    lax.fori_loop(0, animals // n, step, 0, unroll=True)
    for t in range(traits):
        at = slice(t * blocks, (t + 1) * blocks)
        first = 2 * t * short
        down = both_halves(acc_ref, first, short) + both_halves(acc_ref, first + short, short)
        down = down + both_halves(dams_ref, first, short) + both_halves(dams_ref, first + short, short)
        tab_ref[at, :] = (0.25 / 1.5) * both_halves(weight_ref, 0, short) * mixed_ref[at, :] - 0.5 * down
    for b in range(blocks):
        for t in range(traits):
            at = (slice(t, t + 1), slice(b * 128, (b + 1) * 128))
            image_ref[at] = image_ref[at] + tab_ref[t * blocks + b : t * blocks + b + 1, :]
    image_ref[:, :128] = image_ref[:, :128] + resid_ref[...]
    direction = dir_ref[...]
    image = image_ref[...] + rec_ref[...] * direction
    image_ref[...] = image
    res = res_ref[...]
    inv = inv_ref[...]
    columns = dir_a_ref.shape[1]
    sums = jnp.sum(got_ref[:, :, 2 * wide :], axis=0)
    tiles = sums.shape[1] // 128
    back = jnp.concatenate([sums[:, j * 128 : (j + 1) * 128] for j in range(tiles)], axis=0)[:, :columns]
    dir_a = dir_a_ref[...]
    image_a = ridge_ref[...] * dir_a - back
    image_a_ref[...] = image_a
    res_a = res_a_ref[...]
    inv_a = inv_a_ref[...]
    weighted, weighted_a = inv * res, inv_a * res_a
    lane = lax.broadcasted_iota(jnp.int32, (1, 128), 1)
    pairs = (
        (weighted * res, weighted_a * res_a),
        (direction * image, dir_a * image_a),
        (weighted * image, weighted_a * image_a),
        (inv * image * image, inv_a * image_a * image_a),
    )
    total = jnp.zeros((1, 128), F32)
    for j, (one, two) in enumerate(pairs):
        value = jnp.sum(one, keepdims=True) + jnp.sum(two, keepdims=True)
        total = jnp.where(lane == j, value, total)
    sums_ref[...] = total


def update_kernel(
    sums_ref, sol_ref, res_ref, dir_ref, inv_ref, image_ref,
    sol_a_ref, res_a_ref, dir_a_ref, inv_a_ref, image_a_ref,
    nsol_ref, nres_ref, ndir_ref, nsol_a_ref, nres_a_ref, ndir_a_ref,
):
    total = jnp.sum(sums_ref[...], axis=0)
    norm, curve, cross, square = (total[:, j : j + 1] for j in range(4))
    size = norm / curve
    following = norm - 2.0 * size * cross + size * size * square
    ratio = following / norm
    for sol, res, dire, inv, image, nsol, nres, ndir in (
        (sol_ref, res_ref, dir_ref, inv_ref, image_ref, nsol_ref, nres_ref, ndir_ref),
        (sol_a_ref, res_a_ref, dir_a_ref, inv_a_ref, image_a_ref, nsol_a_ref, nres_a_ref, ndir_a_ref),
    ):
        d = dire[...]
        nsol[...] = sol[...] + size * d
        left = res[...] - size * image[...]
        nres[...] = left
        ndir[...] = inv[...] * left + ratio * d


def pedigree_by_blocks(field, sire, dam, herd_count, herd_index):
    traits_here, animals = field.shape
    block_count = animals // 128
    span = SLOTS * 128
    has_sire = sire >= 0
    has_dam = dam >= 0
    sire_known = has_sire.astype(F32)
    dam_known = has_dam.astype(F32)
    owner_herd = jnp.where(has_sire, sire // animals, 0)
    block_index = jnp.where(has_sire, sire % animals // 128, 0)
    offset = jnp.where(has_sire, sire % 128, 0)
    flat_block = jnp.where(
        has_sire, owner_herd * block_count + block_index, herd_count * block_count
    )
    present = jnp.zeros((herd_count * block_count + 1,), jnp.int32).at[flat_block].max(1)
    present = present[:-1].reshape(herd_count, block_count)
    slot_order = jnp.cumsum(present, axis=1) - 1
    slot_range = jnp.arange(SLOTS, dtype=jnp.int32)
    slot_match = (present[:, :, None] == 1) & (slot_order[:, :, None] == slot_range[None, None, :])
    block_ids = jnp.arange(block_count, dtype=jnp.int32)[None, :, None] + 1
    wanted = jnp.sum(jnp.where(slot_match, block_ids, 0), axis=1) - 1
    requests = lax.all_to_all(wanted, HERD, split_axis=0, concat_axis=0, tiled=True)
    live_slot = requests >= 0
    field_tiles = field.reshape(traits_here, block_count, 128)
    outgoing = field_tiles[:, jnp.where(live_slot, requests, 0), :]
    outgoing = jnp.where(live_slot[None, :, :, None], outgoing, 0.0).reshape(
        traits_here, herd_count, span
    )
    fetched = lax.all_to_all(outgoing, HERD, split_axis=1, concat_axis=1, tiled=True).reshape(
        traits_here, herd_count * span
    )
    slot_index = slot_order[owner_herd, block_index]
    buffer_place = owner_herd * span + slot_index * 128 + offset
    sire_values = fetched[:, jnp.where(has_sire, buffer_place, 0)]
    local_dam = jnp.where(has_dam, dam - herd_index * animals, 0)
    dam_values = field[:, local_dam]
    weight = 4.0 / (4.0 - sire_known - dam_known)
    scaled = weight * (field - 0.5 * sire_known * sire_values - 0.5 * dam_known * dam_values)
    dam_target = jnp.where(has_dam, local_dam, animals)
    dam_terms = (
        jnp.zeros((traits_here, animals + 1), F32).at[:, dam_target].add(-0.5 * dam_known * scaled)
    )
    result = scaled + dam_terms[:, :animals]
    sire_target = jnp.where(has_sire, buffer_place, herd_count * span)
    outbound = (
        jnp.zeros((traits_here, herd_count * span + 1), F32)
        .at[:, sire_target]
        .add(-0.5 * sire_known * scaled)
    )
    outbound = outbound[:, :-1].reshape(traits_here, herd_count, span)
    returned = lax.all_to_all(outbound, HERD, split_axis=1, concat_axis=1, tiled=True).reshape(
        traits_here, herd_count * SLOTS, 128
    )
    block_target = jnp.where(live_slot, requests, block_count).reshape(herd_count * SLOTS)
    incoming = (
        jnp.zeros((traits_here, block_count + 1, 128), F32).at[:, block_target, :].add(returned)
    )
    return result + incoming[:, :block_count, :].reshape(traits_here, animals)


def body(
    sol_u, res_u, dir_u, rec_weight, inv_diag_u, sol_a, res_a, dir_a, inv_diag_a,
    genotypes, allele_freq, geno_weight, snp_ridge, genetic_inv, sire, dam,
):
    shape = ny, nz, nc = tuple(lax.axis_size(a) for a in HERD)
    nx = lax.axis_size("x")
    herd, near = ny * nz * nc, ny * nc
    x_index = lax.axis_index("x")
    here, animals = dir_u.shape
    traits, _, columns = dir_a.shape
    genotyped, snps = genotypes.shape
    blocks = animals // 128
    half = here * blocks
    lists, values = 2 * CAP, here * CAP
    spare = traits // near * 128
    scale = 2.0 / math.sqrt(snps * nx)
    sds = lambda *s: jax.ShapeDtypeStruct(s, F32)
    vmem = lambda *s: pltpu.VMEM(s, F32)
    d_a, r_a, s_a, i_a = (a[:, 0, :] for a in (dir_a, res_a, sol_a, inv_diag_a))
    freq = allele_freq[None, :]
    sire_row, dam_row = sire[None, :], dam[None, :]
    mine = jnp.arange(128) // genotyped == x_index
    weight_here = jnp.where(mine[None, :], geno_weight[:, None], 0.0)

    out_z, rank, table = call(
        functools.partial(lists_kernel, shape=shape),
        (sds(nz, near, lists + spare), jax.ShapeDtypeStruct((1, animals), jnp.int32), sds(half, 128)),
        scratch=[vmem(3 * CAP // 2, 2 * herd)],
    )(dir_u, d_a, sire_row, dam_row)
    in_z = lax.all_to_all(out_z, "z", 0, 0, tiled=True)
    from_others = [
        lax.ppermute(table, "x", [(i, (i + k) % nx) for i in range(nx)]) for k in range(1, nx)
    ]
    out_near = call(
        functools.partial(forward_kernel, columns=columns, lists=lists),
        sds(ny, traits, nc * lists + nz * columns),
    )(in_z)
    out_near, place = lax.optimization_barrier((out_near, x_index))
    all_tables = []
    for j in range(nx):
        chosen = table
        for k in range(1, nx):
            chosen = jnp.where(place == (j + k) % nx, from_others[k - 1], chosen)
        all_tables.append(chosen)
    all_tables = jnp.stack(all_tables)
    in_y = lax.all_to_all(out_near, "y", 0, 0, tiled=True)

    on_chip = pl.BlockSpec(memory_space=pltpu.VMEM)
    scalars = pl.BlockSpec(memory_space=pltpu.SMEM)
    mixed_table, c_term, add = call(
        functools.partial(offspring_kernel, shape=shape),
        (sds(half, 128), sds(here, animals), sds(near, nz, values)),
        scratch=[vmem(here * CAP, 2 * herd)],
        in_specs=[scalars] + [on_chip] * 4,
    )(genetic_inv, all_tables, sire_row, dam_row, rank)
    in_y, mixed_table, c_term, add = lax.optimization_barrier((in_y, mixed_table, c_term, add))
    in_near = lax.all_gather(in_y, "c", axis=0)

    to_x, asked, turned, over = call(
        functools.partial(predict_kernel, shape=shape, columns=columns, lists=lists, scale=scale),
        (sds(nx, 2 * here, 128), sds(near, nz, lists), sds(lists, herd), sds(8, 128)),
        scratch=[vmem(traits, nz * nc * columns), vmem(traits, 128)],
        in_specs=[scalars] + [on_chip] * 4,
    )(lax.axis_index("c").reshape(1), in_near, genotypes, freq, weight_here)
    from_x = lax.all_to_all(to_x, "x", 0, 0, tiled=True)

    back_near, resid = call(
        functools.partial(reply_kernel, shape=shape, columns=columns, scale=scale),
        (sds(near, traits, 2 * values + nz * columns), sds(traits, 128)),
        scratch=[vmem(values, herd), vmem(traits, nz * nc * columns)],
    )(mixed_table, add, all_tables, from_x, turned, genotypes, freq)
    got_near = lax.all_to_all(back_near, ("y", "c"), 0, 0, tiled=True)
    back_z = call(
        functools.partial(backward_kernel, columns=columns, values=2 * values),
        sds(nz, near, 2 * values + spare),
    )(got_near)
    back_z, asked = lax.optimization_barrier((back_z, asked))
    got_z = lax.all_to_all(back_z, "z", 0, 0, tiled=True)
    ordered = call(order_kernel, sds(lists, herd), scratch=[vmem(nz, near, lists)])(asked)
    too_long = over[0, 0] > 0.5
    got_z, ordered, too_long = lax.optimization_barrier((got_z, ordered, too_long))

    own_resid = lax.dynamic_slice_in_dim(resid, x_index * here, here, 0)
    image_u, image_a, sums = call(
        functools.partial(image_kernel, shape=shape),
        (sds(here, animals), sds(traits, columns), sds(1, 128)),
        scratch=[vmem(here * blocks, 256), vmem(half, 128), vmem(values, herd), vmem(blocks // 2, 256),
            vmem(here * blocks, 256),
        ],
    )(
        got_z, c_term, rank, sire_row, dam_row, ordered, mixed_table, own_resid,
        dir_u, rec_weight, res_u, inv_diag_u, snp_ridge[:, None], d_a, r_a, i_a,
    )

    u, a = sds(here, animals), sds(traits, columns)

    def reduced(sums):
        close = lax.all_to_all(
            jnp.broadcast_to(sums[None], (near * nx, 1, 128)), ("y", "c", "x"), 0, 0, tiled=True
        )
        close = jnp.sum(close, axis=0, keepdims=True)
        return lax.all_to_all(jnp.broadcast_to(close, (nz, 1, 128)), "z", 0, 0, tiled=True)

    def finish(image, far):
        return tuple(
            call(update_kernel, (u, u, u, a, a, a))(
                far, sol_u, res_u, dir_u, inv_diag_u, image, s_a, r_a, d_a, i_a, image_a
            )
        )

    def by_blocks(_):
        dir_all = all_tables.reshape(traits, animals)
        mixed = jnp.dot(genetic_inv, dir_all, precision=lax.Precision.HIGHEST)
        image = rec_weight * dir_u + pedigree_by_blocks(mixed, sire, dam, herd, lax.axis_index(HERD))
        image = image.at[:, :genotyped].add(own_resid[:, :genotyped])
        cells = [
            jnp.sum(inv_diag_u * res_u * res_u) + jnp.sum(i_a * r_a * r_a),
            jnp.sum(dir_u * image) + jnp.sum(d_a * image_a),
            jnp.sum(inv_diag_u * res_u * image) + jnp.sum(i_a * r_a * image_a),
            jnp.sum(inv_diag_u * image * image) + jnp.sum(i_a * image_a * image_a),
        ]
        return finish(image, reduced(jnp.pad(jnp.stack(cells), (0, 124))[None, :]))

    far, too_long = lax.optimization_barrier((reduced(sums), too_long))
    outs = finish(image_u, far)
    outs = lax.cond(too_long, by_blocks, lambda done: done, outs)
    return outs[:3] + tuple(o[:, None, :] for o in outs[3:])


def solution(mesh):
    herd, nx = mesh.devices.shape
    ny, nc = 4, 2
    grid = Mesh(mesh.devices.reshape(ny, herd // (ny * nc), nc, nx), HERD + ("x",))
    u = P("x", HERD)
    a = P(None, "x", HERD)
    return jax.shard_map(
        body,
        mesh=grid,
        in_specs=(
            u, u, u, u, u, a, a, a, a,
            P(HERD, "x"), P("x"), P("x"), P(), P("x", None), P(HERD), P(HERD),
        ),
        out_specs=(u, u, u, a, a, a),
        check_vma=False,
    )
```
